32 devices in a mesh: tok: 8 (over y, x, core), mlp: 4 (over z).
Axes of the slice: x: 2, y: 2, z: 4, core: 2. Of those that a mesh axis runs over, the one named last changes fastest.
Arguments:
- tokens: bfloat16 [8192, 2048], P('tok'), may hold values from -6 to 6
- segment_ids: int32 [8192], P('tok'), may hold values from 0 to 1, as said below
- owner_table: int32 [8], replicated, may hold values from 0 to 7, each once
- cotangent: bfloat16 [8192, 2048], P('tok'), may hold values from -6 to 6
- w_in_rec: float32 [2, 2048, 2816], P(None, 'tok', 'mlp'), may hold values from -0.125 to 0.125
- m_in_rec: float32 [2, 2048, 2816], P(None, 'tok', 'mlp'), may hold values from -32 to 32
- v_in_rec: float32 [2, 2048, 2816], P(None, 'tok', 'mlp'), may hold values from 2.048 to 8.192
- q_in_rec: float32 [2, 32, 44, 2, 64, 64], P(None, 'tok', 'mlp'), may hold values from -1 to 1, as said below
- w_out_rec: float32 [2816, 2048], P('mlp', 'tok'), may hold values from -0.375 to 0.375
- m_out_rec: float32 [2816, 2048], P('mlp', 'tok'), may hold values from -32 to 32
- v_out_rec: float32 [2816, 2048], P('mlp', 'tok'), may hold values from 2.048 to 8.192
- q_out_rec: float32 [44, 32, 2, 64, 64], P('mlp', 'tok'), may hold values from -1 to 1, as said below
- w_in_mlp: float32 [2, 2048, 6144], P(None, 'tok', 'mlp'), may hold values from -0.125 to 0.125
- m_in_mlp: float32 [2, 2048, 6144], P(None, 'tok', 'mlp'), may hold values from -32 to 32
- v_in_mlp: float32 [2, 2048, 6144], P(None, 'tok', 'mlp'), may hold values from 2.048 to 8.192
- q_in_mlp: float32 [2, 32, 96, 2, 64, 64], P(None, 'tok', 'mlp'), may hold values from -1 to 1, as said below
- w_out_mlp: float32 [6144, 2048], P('mlp', 'tok'), may hold values from -0.109375 to 0.109375
- m_out_mlp: float32 [6144, 2048], P('mlp', 'tok'), may hold values from -32 to 32
- v_out_mlp: float32 [6144, 2048], P('mlp', 'tok'), may hold values from 2.048 to 8.192
- q_out_mlp: float32 [96, 32, 2, 64, 64], P('mlp', 'tok'), may hold values from -1 to 1, as said below
- w_gates: float32 [2, 16, 30976], P(None, 'mlp', 'tok'), may hold values from -0.4375 to 0.4375
- m_gates: float32 [2, 16, 30976], P(None, 'mlp', 'tok'), may hold values from -32 to 32
- v_gates: float32 [2, 16, 30976], P(None, 'mlp', 'tok'), may hold values from 2.048 to 8.192
- w_rnn: float32 [8, 2816], P(None, ('mlp', 'tok')), may hold values from -13 to 3
- m_rnn: float32 [8, 2816], P(None, ('mlp', 'tok')), may hold values from -768 to 768
- v_rnn: float32 [8, 2816], P(None, ('mlp', 'tok')), may hold values from 2048 to 8192
- w_gains: float32 [2, 2048], P(None, 'tok'), may hold values from 0.5 to 1.5
- m_gains: float32 [2, 2048], P(None, 'tok'), may hold values from -768 to 768
- v_gains: float32 [2, 2048], P(None, 'tok'), may hold values from 573.44 to 2293.76
Outputs:
- block_out: bfloat16 [8192, 2048], P('tok')
- grad_tokens: float32 [8192, 2048], P('tok')
- new_m_in_rec: float32 [2, 2048, 2816], P(None, 'tok', 'mlp')
- new_v_in_rec: float32 [2, 2048, 2816], P(None, 'tok', 'mlp')
- new_w_in_rec: float32 [2, 2048, 2816], P(None, 'tok', 'mlp')
- new_m_out_rec: float32 [2816, 2048], P('mlp', 'tok')
- new_v_out_rec: float32 [2816, 2048], P('mlp', 'tok')
- new_w_out_rec: float32 [2816, 2048], P('mlp', 'tok')
- new_m_in_mlp: float32 [2, 2048, 6144], P(None, 'tok', 'mlp')
- new_v_in_mlp: float32 [2, 2048, 6144], P(None, 'tok', 'mlp')
- new_w_in_mlp: float32 [2, 2048, 6144], P(None, 'tok', 'mlp')
- new_m_out_mlp: float32 [6144, 2048], P('mlp', 'tok')
- new_v_out_mlp: float32 [6144, 2048], P('mlp', 'tok')
- new_w_out_mlp: float32 [6144, 2048], P('mlp', 'tok')
- new_m_gates: float32 [2, 16, 30976], P(None, 'mlp', 'tok')
- new_v_gates: float32 [2, 16, 30976], P(None, 'mlp', 'tok')
- new_w_gates: float32 [2, 16, 30976], P(None, 'mlp', 'tok')
- new_m_rnn: float32 [8, 2816], P(None, ('mlp', 'tok'))
- new_v_rnn: float32 [8, 2816], P(None, ('mlp', 'tok'))
- new_m_gains: float32 [2, 2048], P(None, 'tok')
- new_v_gains: float32 [2, 2048], P(None, 'tok')
The draws below stay inside these ranges and needn't reach their ends.
Inputs may be any that keep to these rules, and one draw needn't show every extreme that they name: `owner_table`: a permutation of the indices of tok. `segment_ids`: never falls, starts at 0 and rises by one at each new document; no document starts at a multiple of 1024 other than token 0. `q_in_rec`: every 64 x 64 matrix q[..., 0, :, :] and q[..., 1, :, :] is orthogonal. `q_out_rec`: every 64 x 64 matrix q[..., 0, :, :] and q[..., 1, :, :] is orthogonal. `q_in_mlp`: every 64 x 64 matrix q[..., 0, :, :] and q[..., 1, :, :] is orthogonal. `q_out_mlp`: every 64 x 64 matrix q[..., 0, :, :] and q[..., 1, :, :] is orthogonal.
All inputs are finite; a program needn't handle non-finite values.
Results may differ from the reference program's by a relative error of at most 0.01.
The reference program's roundings to bfloat16 on the way count: a program that leaves them out, or rounds other values in their place, can miss the bound.
Values may be sent and summed in bfloat16 or wider, within the bound.
No kernel may reach another device: no remote copies, remote signals or barrier semaphores. Data moves between devices by JAX's collectives and lax.ppermute only.
A program may use at most 384 MiB of HBM per device.

```python
import math
import jax
import jax.numpy as jnp
from jax import lax

D = 2048
R = 2816
FF = 6144
NB = 16
BW = 176
CONV = 4
TILE = 64
STEP = 7
TOK_DEV = 1024
TOKENS = 8192
LENGTH = 8192
SEGS = 2
N_TOK = 8
N_MLP = 4


def orthogonal_tiles(key, shape):
    width = shape[-1]
    jitter = jnp.clip(jax.random.normal(key, shape, jnp.float32), -6.0, 6.0) * (0.4 / width ** 0.5)
    matrix = (jnp.eye(width, dtype=jnp.float32) + jitter) / 1.9
    for repeat in range(20):
        gram_matrix = jnp.einsum('...ki,...kj->...ij', matrix, matrix, precision=lax.Precision.HIGHEST)
        matrix = 1.5 * matrix - 0.5 * jnp.einsum('...ik,...kj->...ij', matrix, gram_matrix, precision=lax.Precision.HIGHEST)
    return matrix


def draw_segment_ids(key, part):
    devices_tok = TOKENS // TOK_DEV
    inner = TOK_DEV - 1
    order = jax.random.permutation(jax.random.fold_in(key, 31), devices_tok * inner)[:SEGS - 1]
    cuts = order // inner * TOK_DEV + order % inner + 1
    position = jnp.arange(TOKENS, dtype=jnp.int32)
    return jnp.sum((cuts[None, :] <= position[:, None]).astype(jnp.int32), axis=1).astype(jnp.int32)


def draw_q_in_rec(key, part):
    return orthogonal_tiles(jax.random.fold_in(key, 11), (2, D // TILE, R // TILE, 2, TILE, TILE))


def draw_q_out_rec(key, part):
    return orthogonal_tiles(jax.random.fold_in(key, 12), (R // TILE, D // TILE, 2, TILE, TILE))


def draw_q_in_mlp(key, part):
    return orthogonal_tiles(jax.random.fold_in(key, 13), (2, D // TILE, FF // TILE, 2, TILE, TILE))


def draw_q_out_mlp(key, part):
    return orthogonal_tiles(jax.random.fold_in(key, 14), (FF // TILE, D // TILE, 2, TILE, TILE))


def draw_w_rnn(key, part):
    keys = jax.random.split(jax.random.fold_in(key, 21), 4)
    taps = jnp.clip(jax.random.normal(keys[0], (CONV, R), jnp.float32), -6.0, 6.0) * 0.5
    conv_bias = jnp.clip(jax.random.normal(keys[1], (1, R), jnp.float32), -6.0, 6.0) * 0.3
    lowest = jnp.log(0.05 / LENGTH)
    highest_log = jnp.log(10.0 / LENGTH)
    rates = jnp.exp(jax.random.uniform(keys[2], (1, R), jnp.float32, lowest, highest_log))
    decay_param = jnp.log(jnp.expm1(rates))
    gate_bias = jnp.clip(jax.random.normal(keys[3], (2, R), jnp.float32), -6.0, 6.0) * 0.5
    return jnp.concatenate([taps, conv_bias, decay_param, gate_bias], axis=0)


def block_levels(own_key, extent, pieces, smallest, top_value):
    level, own = 1.0, jax.random.fold_in(own_key, 6)
    for axis_at, blocks in pieces:
        draws = jnp.exp(jax.random.uniform(jax.random.fold_in(own, axis_at), (blocks,), jnp.float32, smallest / len(pieces), top_value / len(pieces)))
        level = level * jnp.repeat(draws, extent[axis_at] // blocks).reshape([-1 if axis == axis_at else 1 for axis in range(len(extent))])
    return level


def gaussian(own_key, dims, scale, limit, cuts=(), kind=jnp.bfloat16):
    level = block_levels(own_key, dims, cuts, -0.22, 0.18) if cuts else 1.0
    values = jax.random.normal(own_key, dims, jnp.float32) * scale * level
    return jnp.minimum(jnp.maximum(values, -limit), limit).astype(kind)


def setup_inputs(seed: int = 0) -> dict:
    splits = jax.random.split(jax.random.key(seed), 30)
    return {
        "tokens": gaussian(splits[0], (TOKENS, D), 1.0, 6.0, ((0, 8),)),
        "segment_ids": draw_segment_ids(jax.random.fold_in(splits[29], 71), 0),
        "owner_table": jax.random.permutation(splits[2], N_TOK).astype(jnp.int32),
        "cotangent": gaussian(splits[3], (TOKENS, D), 1.0, 6.0, ((0, 8),)),
        "w_in_rec": gaussian(splits[4], (2, D, R), D ** -0.5, 0.125, ((1, 8), (2, 4)), jnp.float32),
        "m_in_rec": gaussian(splits[5], (2, D, R), (0.055 * TOKENS ** 0.5), 32.0, ((1, 8), (2, 4)), jnp.float32),
        "v_in_rec": jnp.clip(jnp.exp(math.log(8.192) - 1.3862944 * jax.random.uniform(splits[6], (2, D, R), jnp.float32) ** block_levels(splits[6], (2, D, R), ((1, 8), (2, 4)), -0.2, 0.2)), 2.048, 8.192),
        "q_in_rec": draw_q_in_rec(jax.random.fold_in(splits[29], 71), 0),
        "w_out_rec": gaussian(splits[8], (R, D), (R // 10) ** -0.5, 0.375, ((0, 4), (1, 8)), jnp.float32),
        "m_out_rec": gaussian(splits[9], (R, D), (0.055 * TOKENS ** 0.5), 32.0, ((0, 4), (1, 8)), jnp.float32),
        "v_out_rec": jnp.clip(jnp.exp(math.log(8.192) - 1.3862944 * jax.random.uniform(splits[10], (R, D), jnp.float32) ** block_levels(splits[10], (R, D), ((0, 4), (1, 8)), -0.2, 0.2)), 2.048, 8.192),
        "q_out_rec": draw_q_out_rec(jax.random.fold_in(splits[29], 71), 0),
        "w_in_mlp": gaussian(splits[12], (2, D, FF), D ** -0.5, 0.125, ((1, 8), (2, 4)), jnp.float32),
        "m_in_mlp": gaussian(splits[13], (2, D, FF), (0.055 * TOKENS ** 0.5), 32.0, ((1, 8), (2, 4)), jnp.float32),
        "v_in_mlp": jnp.clip(jnp.exp(math.log(8.192) - 1.3862944 * jax.random.uniform(splits[14], (2, D, FF), jnp.float32) ** block_levels(splits[14], (2, D, FF), ((1, 8), (2, 4)), -0.2, 0.2)), 2.048, 8.192),
        "q_in_mlp": draw_q_in_mlp(jax.random.fold_in(splits[29], 71), 0),
        "w_out_mlp": gaussian(splits[16], (FF, D), (FF // 2) ** -0.5, 0.109375, ((0, 4), (1, 8)), jnp.float32),
        "m_out_mlp": gaussian(splits[17], (FF, D), (0.055 * TOKENS ** 0.5), 32.0, ((0, 4), (1, 8)), jnp.float32),
        "v_out_mlp": jnp.clip(jnp.exp(math.log(8.192) - 1.3862944 * jax.random.uniform(splits[18], (FF, D), jnp.float32) ** block_levels(splits[18], (FF, D), ((0, 4), (1, 8)), -0.2, 0.2)), 2.048, 8.192),
        "q_out_mlp": draw_q_out_mlp(jax.random.fold_in(splits[29], 71), 0),
        "w_gates": gaussian(splits[20], (2, NB, BW * BW), BW ** -0.5, 0.4375, ((1, 4), (2, 8)), jnp.float32),
        "m_gates": gaussian(splits[21], (2, NB, BW * BW), (0.055 * TOKENS ** 0.5), 32.0, ((1, 4), (2, 8)), jnp.float32),
        "v_gates": jnp.clip(jnp.exp(math.log(8.192) - 1.3862944 * jax.random.uniform(splits[22], (2, NB, BW * BW), jnp.float32) ** block_levels(splits[22], (2, NB, BW * BW), ((1, 4), (2, 8)), -0.2, 0.2)), 2.048, 8.192),
        "w_rnn": draw_w_rnn(jax.random.fold_in(splits[29], 71), 0),
        "m_rnn": gaussian(splits[24], (CONV + 4, R), (1.5 * TOKENS ** 0.5), 768.0, ((1, 32),), jnp.float32),
        "v_rnn": jnp.clip(jnp.exp(math.log(8192.0) - 1.3862944 * jax.random.uniform(splits[25], (CONV + 4, R), jnp.float32) ** block_levels(splits[25], (CONV + 4, R), ((1, 32),), -0.2, 0.2)), 2048.0, 8192.0),
        "w_gains": jnp.clip(1.0 + 0.1 * jax.random.normal(splits[26], (2, D), jnp.float32), 0.5, 1.5),
        "m_gains": gaussian(splits[27], (2, D), (1.5 * TOKENS ** 0.5), 768.0, ((1, 8),), jnp.float32),
        "v_gains": jnp.clip(jnp.exp(math.log(2293.76) - 1.3862944 * jax.random.uniform(splits[28], (2, D), jnp.float32) ** block_levels(splits[28], (2, D), ((1, 8),), -0.2, 0.2)), 573.44, 2293.76),
    }


@jax.custom_vjp
def low(v):
    return lax.optimization_barrier(v.astype(jnp.bfloat16)).astype(jnp.float32)

@jax.custom_vjp
def low_back(v):
    return v

def low_keep(v):
    return (low(v), None)

def low_pass(kept, grad):
    return (grad,)

def back_keep(v):
    return (v, None)

def back_low(kept, grad):
    return (low(grad),)
low.defvjp(low_keep, low_pass)
low_back.defvjp(back_keep, back_low)
norm_eps = 1e-06
learn_rate = 0.02
beta_first = 0.9
beta_second = 0.999
adam_eps = 1e-08
decay_rate = 0.1
highest = lax.Precision.HIGHEST

def matmul_high(left, right):
    return jnp.dot(left, right, precision=highest, preferred_element_type=jnp.float32)

def gelu_tanh(value):
    return 0.5 * value * (1.0 + jnp.tanh(0.7978845608028654 * (value + 0.044715 * value * value * value)))

def rms_norm(value, gain):
    return value * lax.rsqrt(lax.optimization_barrier(jnp.mean(value * value, axis=-1, keepdims=True)) + norm_eps) * gain

def link_pairs(earlier, later):
    return (earlier[0] * later[0], later[0] * earlier[1] + later[1])

def reorder(array, dim, order, groups):
    shape = array.shape
    parts = order.shape[0]
    reshaped = array.reshape(shape[:dim] + (groups, parts, shape[dim] // (groups * parts)) + shape[dim + 1:])
    return jnp.take(reshaped, order, axis=dim + 1).reshape(shape)

def to_tiles(array):
    leading = array.shape[:-2]
    row_count = array.shape[-2]
    col_count = array.shape[-1]
    reshaped = array.reshape(leading + (row_count // TILE, TILE, col_count // TILE, TILE))
    return jnp.swapaxes(reshaped, -3, -2)

def from_tiles(array):
    leading = array.shape[:-4]
    joined = jnp.swapaxes(array, -3, -2)
    return joined.reshape(leading + (array.shape[-4] * TILE, array.shape[-3] * TILE))

def soap_update(master, first, second, gradient, bases):
    left_basis = bases[..., 0, :, :]
    right_basis = bases[..., 1, :, :]
    rotated = jnp.einsum('...ki,...kl,...lj->...ij', left_basis, to_tiles(gradient), right_basis, precision=highest)
    new_first = beta_first * to_tiles(first) + (1.0 - beta_first) * rotated
    new_second = beta_second * to_tiles(second) + (1.0 - beta_second) * rotated * rotated
    normalized = new_first / (1.0 - beta_first ** STEP) / (jnp.sqrt(new_second / (1.0 - beta_second ** STEP)) + adam_eps)
    turned = jnp.einsum('...ik,...kl,...jl->...ij', left_basis, normalized, right_basis, precision=highest)
    new_master = master - learn_rate * (from_tiles(turned) + decay_rate * master)
    return (from_tiles(new_first), from_tiles(new_second), new_master)

def adam_update(master, first, second, gradient, decay):
    new_first = beta_first * first + (1.0 - beta_first) * gradient
    new_second = beta_second * second + (1.0 - beta_second) * gradient * gradient
    normalized = new_first / (1.0 - beta_first ** STEP) / (jnp.sqrt(new_second / (1.0 - beta_second ** STEP)) + adam_eps)
    return (new_first, new_second, master - learn_rate * (normalized + decay * master))

def moment_update(first, second, gradient):
    new_first = beta_first * first + (1.0 - beta_first) * gradient
    new_second = beta_second * second + (1.0 - beta_second) * gradient * gradient
    return (new_first, new_second)

def forward(inputs, p_in_rec, p_out_rec, p_in_mlp, p_out_mlp, p_gates, p_rnn, p_gains, live, reset):
    in_rec = low(p_in_rec)
    out_rec = low(p_out_rec)
    in_mlp = low(p_in_mlp)
    out_mlp = low(p_out_mlp)
    gate_mats = low(p_gates).reshape(2, NB, BW, BW)
    rnn_vec = low(p_rnn)
    gains = low(p_gains)
    xn1 = low(rms_norm(inputs, gains[0]))
    y_pre = low_back(matmul_high(xn1, in_rec[0]))
    u_val = low_back(low(matmul_high(xn1, in_rec[1])))
    lag = CONV - 1
    u_pad = jnp.concatenate([jnp.zeros((lag, R), jnp.float32), u_val])
    live_pad = jnp.concatenate([jnp.zeros((lag,), jnp.float32), live])
    conv_val = rnn_vec[CONV] + rnn_vec[0] * u_val
    valid = jnp.ones((TOKENS,), jnp.float32)
    for offset in range(1, CONV):
        valid = valid * live_pad[lag - offset + 1:lag - offset + 1 + TOKENS]
        conv_val = conv_val + rnn_vec[offset] * valid[:, None] * u_pad[lag - offset:lag - offset + TOKENS]
    conv_low = low(conv_val)
    blocked = conv_low.reshape(TOKENS, NB, BW)
    pre_decay = low_back(jnp.einsum('tnb,nbc->tnc', blocked, gate_mats[0], precision=highest).reshape(TOKENS, R) + rnn_vec[CONV + 2])
    pre_input = low_back(jnp.einsum('tnb,nbc->tnc', blocked, gate_mats[1], precision=highest).reshape(TOKENS, R) + rnn_vec[CONV + 3])
    rate_gate = jax.nn.sigmoid(pre_decay)
    input_gate = jax.nn.sigmoid(pre_input)
    log_decay = -8.0 * jax.nn.softplus(rnn_vec[CONV + 1]) * rate_gate
    scale = reset[:, None] + live[:, None] * jnp.sqrt(-jnp.expm1(2.0 * log_decay))
    decay_eff = jnp.exp(log_decay) * live[:, None]
    drive = input_gate * conv_low * scale
    _, state = lax.associative_scan(link_pairs, (decay_eff, drive), axis=0)
    mixed = low(state * gelu_tanh(y_pre))
    second = inputs + low_back(matmul_high(mixed, out_rec))
    xn2 = low(rms_norm(second, gains[1]))
    z_gate = low_back(matmul_high(xn2, in_mlp[0]))
    z_up = low_back(matmul_high(xn2, in_mlp[1]))
    hidden = low(gelu_tanh(z_gate) * z_up)
    return second + matmul_high(hidden, out_mlp)

def reference(tokens, segment_ids, owner_table, cotangent, w_in_rec, m_in_rec, v_in_rec, q_in_rec, w_out_rec, m_out_rec, v_out_rec, q_out_rec, w_in_mlp, m_in_mlp, v_in_mlp, q_in_mlp, w_out_mlp, m_out_mlp, v_out_mlp, q_out_mlp, w_gates, m_gates, v_gates, w_rnn, m_rnn, v_rnn, w_gains, m_gains, v_gains):
    position = jnp.arange(TOKENS, dtype=jnp.int32)
    previous = jnp.concatenate([segment_ids[:1], segment_ids[:-1]])
    starts = (position % LENGTH == 0) | (segment_ids != previous)
    reset = jnp.where(starts, 1.0, 0.0).astype(jnp.float32)
    live = 1.0 - reset
    params = (reorder(w_in_rec, 1, owner_table, 1), reorder(w_out_rec, 1, owner_table, 1), reorder(w_in_mlp, 1, owner_table, 1), reorder(w_out_mlp, 1, owner_table, 1), reorder(w_gates, 2, owner_table, 1), reorder(w_rnn, 1, owner_table, N_MLP), reorder(w_gains, 1, owner_table, 1))

    def run(inputs, p_in_rec, p_out_rec, p_in_mlp, p_out_mlp, p_gates, p_rnn, p_gains):
        return forward(inputs, p_in_rec, p_out_rec, p_in_mlp, p_out_mlp, p_gates, p_rnn, p_gains, live, reset)
    result, pullback = jax.vjp(run, tokens.astype(jnp.float32), *params)
    grads = pullback(cotangent.astype(jnp.float32))
    inverse = jnp.argsort(owner_table).astype(jnp.int32)
    g_in_rec = reorder(grads[1], 1, inverse, 1)
    g_out_rec = reorder(grads[2], 1, inverse, 1)
    g_in_mlp = reorder(grads[3], 1, inverse, 1)
    g_out_mlp = reorder(grads[4], 1, inverse, 1)
    g_gates = reorder(grads[5], 2, inverse, 1)
    g_rnn = reorder(grads[6], 1, inverse, N_MLP)
    g_gains = reorder(grads[7], 1, inverse, 1)
    in_rec_new = soap_update(w_in_rec, m_in_rec, v_in_rec, g_in_rec, q_in_rec)
    out_rec_new = soap_update(w_out_rec, m_out_rec, v_out_rec, g_out_rec, q_out_rec)
    in_mlp_new = soap_update(w_in_mlp, m_in_mlp, v_in_mlp, g_in_mlp, q_in_mlp)
    out_mlp_new = soap_update(w_out_mlp, m_out_mlp, v_out_mlp, g_out_mlp, q_out_mlp)
    gates_new = adam_update(w_gates, m_gates, v_gates, g_gates, decay_rate)
    rnn_new = moment_update(m_rnn, v_rnn, g_rnn)
    gains_new = moment_update(m_gains, v_gains, g_gains)
    return (result.astype(jnp.bfloat16), grads[0], in_rec_new[0], in_rec_new[1], in_rec_new[2], out_rec_new[0], out_rec_new[1], out_rec_new[2], in_mlp_new[0], in_mlp_new[1], in_mlp_new[2], out_mlp_new[0], out_mlp_new[1], out_mlp_new[2], gates_new[0], gates_new[1], gates_new[2], rnn_new[0], rnn_new[1], gains_new[0], gains_new[1])
```

```python
import functools

import jax
import jax.numpy as jnp
from jax import lax
from jax.experimental import pallas as pl
from jax.experimental.pallas import tpu as pltpu
from jax.sharding import PartitionSpec as P

BW = 176
CONV = 4
TILE = 64
STEP = 7
HALO = 16
LANES = 128

norm_eps = 1e-06
learn_rate = 0.02
beta_first = 0.9
beta_second = 0.999
adam_eps = 1e-08
decay_rate = 0.1

f32 = jnp.float32
bf16 = jnp.bfloat16


def params(limit=56):
    return pltpu.CompilerParams(
        dimension_semantics=("arbitrary",), vmem_limit_bytes=limit * 1024 * 1024
    )


def whole(shape):
    return pl.BlockSpec(shape, lambda *_: (0,) * len(shape), pipeline_mode=pl.Buffered(1))


def nn(left, right):
    return lax.dot_general(left, right, (((1,), (0,)), ((), ())), preferred_element_type=f32)


def nt(left, right):
    return lax.dot_general(left, right, (((1,), (1,)), ((), ())), preferred_element_type=f32)


def tn(left, right):
    return lax.dot_general(left, right, (((0,), (0,)), ((), ())), preferred_element_type=f32)


def gelu_both(value):
    square = value * value
    bent = jnp.tanh(0.7978845608028654 * (value + 0.044715 * value * square))
    half = 0.5 * (1.0 + bent)
    slope = half + (0.5 * 0.7978845608028654) * value * (1.0 - bent * bent) * (
        1.0 + (3.0 * 0.044715) * square
    )
    return value * half, slope


def gelu_tanh(value):
    return (
        0.5
        * value
        * (1.0 + jnp.tanh(0.7978845608028654 * (value + 0.044715 * value * value * value)))
    )


def one_less_exp(value):
    series = 1.0 + value * (1.0 / 9.0)
    for order in range(8, 1, -1):
        series = 1.0 + value * series * (1.0 / order)
    return jnp.where(value > -0.5, -value * series, 1.0 - jnp.exp(value))


def gate_terms(pre_decay, pre_input, slope, live):
    rate = 1.0 / (1.0 + jnp.exp(-pre_decay))
    gate = 1.0 / (1.0 + jnp.exp(-pre_input))
    log_decay = slope * rate
    raw = jnp.exp(log_decay)
    root = jnp.sqrt(one_less_exp(2.0 * log_decay))
    mult = (1.0 - live) + live * root
    return rate, gate, raw, root, mult


def put_tiles(buffer, value):
    width = value.shape[1]
    for tile in range(pl.cdiv(width, LANES)):
        size = min(LANES, width - tile * LANES)
        buffer[tile, :, :size] = value[:, tile * LANES : tile * LANES + size]


def scan_tiles(first, second, carry_state, carry_prod, out_state, out_prod, width, backward):
    rows = first.shape[1]
    span = rows // 8
    for tile in range(pl.cdiv(width, LANES)):
        size = min(LANES, width - tile * LANES)
        cols = slice(tile * LANES, tile * LANES + size)

        def body(step, held, tile=tile):
            state, prod = held
            row = (span - 1 - step) if backward else step
            at = pl.ds(row, 8, stride=span)
            decay = first[tile, at, :]
            drive = second[tile, at, :]
            if backward:
                total = drive + state
                second[tile, at, :] = total
                first[tile, at, :] = prod
                return decay * total, decay * prod
            state = decay * state + drive
            prod = decay * prod
            second[tile, at, :] = state
            first[tile, at, :] = prod
            return state, prod

        state, prod = lax.fori_loop(
            0,
            span,
            body,
            (jnp.zeros((8, LANES), f32), jnp.ones((8, LANES), f32)),
            unroll=8,
        )
        state_in = carry_state[0:1, tile * LANES : (tile + 1) * LANES]
        prod_in = carry_prod[0:1, tile * LANES : (tile + 1) * LANES]
        for chunk in range(7, -1, -1) if backward else range(8):
            at = slice(chunk * span, (chunk + 1) * span)
            local = first[tile, at, :]
            out_state[at, cols] = (second[tile, at, :] + local * state_in)[:, :size]
            out_prod[at, cols] = (local * prod_in)[:, :size]
            state_in = state[chunk : chunk + 1] + prod[chunk : chunk + 1] * state_in
            prod_in = prod[chunk : chunk + 1] * prod_in
        carry_state[0:1, tile * LANES : (tile + 1) * LANES] = state_in
        carry_prod[0:1, tile * LANES : (tile + 1) * LANES] = prod_in


def rms_low(value, gain):
    return (
        value * lax.rsqrt(jnp.mean(value * value, axis=-1, keepdims=True) + norm_eps) * gain
    ).astype(bf16)


def front_kernel(
    tok, halo, gain, w_in, w_a, w_i, vec, mask,
    xn_o, y_o, u_o, uh_o, xc_o, pa_o, pi_o, a_o, h_o, p_o, end_o,
    ubuf, abuf, bbuf, car_s, car_p,
):
    step = pl.program_id(0)
    rows = tok.shape[0]
    width = y_o.shape[1]

    @pl.when(step == 0)
    def _():
        low = nn(rms_low(halo[...].astype(f32), gain[...]), w_in[1]).astype(bf16)
        uh_o[...] = low
        ubuf[0:HALO, :] = low.astype(f32)
        car_s[...] = jnp.zeros_like(car_s)
        car_p[...] = jnp.ones_like(car_p)

    xn = rms_low(tok[...].astype(f32), gain[...])
    xn_o[...] = xn
    y_o[...] = nn(xn, w_in[0])
    u_low = nn(xn, w_in[1]).astype(bf16)
    u_o[...] = u_low
    u_now = u_low.astype(f32)
    ubuf[HALO : HALO + rows, :] = u_now
    conv = vec[CONV : CONV + 1] + vec[0:1] * u_now
    for back in range(1, CONV):
        conv = conv + vec[back : back + 1] * mask[:, back : back + 1] * ubuf[
            HALO - back : HALO - back + rows, :
        ]
    ubuf[0:HALO, :] = u_now[rows - HALO :, :]
    conv_low = conv.astype(bf16)
    xc_o[...] = conv_low
    pre_decay = nn(conv_low, w_a[...]) + vec[CONV + 2 : CONV + 3]
    pre_input = nn(conv_low, w_i[...]) + vec[CONV + 3 : CONV + 4]
    pa_o[...] = pre_decay
    pi_o[...] = pre_input
    live = mask[:, 0:1]
    _, gate, raw, _, mult = gate_terms(pre_decay, pre_input, vec[CONV + 1 : CONV + 2], live)
    decay = raw * live
    a_o[...] = decay
    put_tiles(abuf, decay)
    put_tiles(bbuf, gate * conv_low.astype(f32) * mult)
    scan_tiles(abuf, bbuf, car_s, car_p, h_o, p_o, width, False)
    end_o[0:1, :] = car_s[0:1, :width]
    end_o[1:2, :] = car_p[0:1, :width]


def front(tok, halo, gain, w_in, w_a, w_i, vec, mask, rows):
    count, model = tok.shape
    width = w_in.shape[2]
    tiles = pl.cdiv(width, LANES)
    row = lambda size: pl.BlockSpec((rows, size), lambda i: (i, 0))
    like = lambda size, kind: jax.ShapeDtypeStruct((count, size), kind)
    return pl.pallas_call(
        front_kernel,
        grid=(count // rows,),
        in_specs=[
            row(model), whole(halo.shape), whole(gain.shape), whole(w_in.shape), whole(w_a.shape),
            whole(w_i.shape), whole(vec.shape), row(mask.shape[1]),
        ],
        out_specs=[
            row(model), row(width), row(width), whole((HALO, width)), row(width), row(width),
            row(width), row(width), row(width), row(width), whole((8, width)),
        ],
        out_shape=[
            like(model, bf16), like(width, f32), like(width, bf16),
            jax.ShapeDtypeStruct((HALO, width), bf16), like(width, bf16), like(width, f32),
            like(width, f32), like(width, f32), like(width, f32), like(width, f32),
            jax.ShapeDtypeStruct((8, width), f32),
        ],
        scratch_shapes=[
            pltpu.VMEM((HALO + rows, width), f32),
            pltpu.VMEM((tiles, rows, LANES), f32),
            pltpu.VMEM((tiles, rows, LANES), f32),
            pltpu.VMEM((8, tiles * LANES), f32),
            pltpu.VMEM((8, tiles * LANES), f32),
        ],
        compiler_params=params(),
        name="front",
    )(tok, halo, gain, w_in, w_a, w_i, vec, mask)


def state_kernel(rank, ends, h_l, p_l, y, w_o, h_o, hp_o, o_o, part_o, hin, hbuf):
    step = pl.program_id(0)
    rows = h_l.shape[0]

    @pl.when(step == 0)
    def _():
        def fold(at, held):
            return jnp.where(at < rank[0], ends[at, 0:1, :] + ends[at, 1:2, :] * held, held)

        start = lax.fori_loop(0, ends.shape[0], fold, jnp.zeros((1, h_l.shape[1]), f32))
        hin[0:1, :] = start
        hbuf[7:8, :] = start

    state = h_l[...] + p_l[...] * hin[0:1, :]
    h_o[...] = state
    hbuf[8 : 8 + rows, :] = state
    hp_o[...] = hbuf[7 : 7 + rows, :]
    hbuf[7:8, :] = state[rows - 1 :, :]
    mixed = (state * gelu_tanh(y[...])).astype(bf16)
    o_o[...] = mixed
    part_o[...] = nt(mixed, w_o[...]).astype(bf16)


def finish_state(rank, ends, h_l, p_l, y, w_o, rows):
    count, width = h_l.shape
    model = w_o.shape[0]
    row = lambda size: pl.BlockSpec((rows, size), lambda i: (i, 0))
    like = lambda size, kind: jax.ShapeDtypeStruct((count, size), kind)
    return pl.pallas_call(
        state_kernel,
        grid=(count // rows,),
        in_specs=[
            pl.BlockSpec(memory_space=pltpu.SMEM), whole(ends.shape), row(width), row(width),
            row(width), whole(w_o.shape),
        ],
        out_specs=[row(width), row(width), row(width), row(model)],
        out_shape=[like(width, f32), like(width, f32), like(width, bf16), like(model, bf16)],
        scratch_shapes=[pltpu.VMEM((8, width), f32), pltpu.VMEM((8 + rows, width), f32)],
        compiler_params=params(),
        name="finish_state",
    )(rank, ends, h_l, p_l, y, w_o)


def mlp_kernel(xn, dhid, w_g, w_u, hm_o, dg_o, du_o, part_o):
    hidden = dhid.shape[1]
    piece = hidden // 3
    total = None
    for at in range(0, hidden, piece):
        cols = slice(at, at + piece)
        z_gate = nn(xn[...], w_g[:, cols])
        z_up = nn(xn[...], w_u[:, cols])
        d_hid = dhid[:, cols]
        act, slope = gelu_both(z_gate)
        hm_o[:, cols] = (act * z_up).astype(bf16)
        d_gate = (d_hid * z_up * slope).astype(bf16)
        d_up = (d_hid * act).astype(bf16)
        dg_o[:, cols] = d_gate
        du_o[:, cols] = d_up
        more = nt(d_gate, w_g[:, cols]) + nt(d_up, w_u[:, cols])
        total = more if total is None else total + more
    part_o[...] = total.astype(bf16)


def mlp(xn, dhid, w_g, w_u, rows):
    count, model = xn.shape
    hidden = dhid.shape[1]
    row = lambda size: pl.BlockSpec((rows, size), lambda i: (i, 0))
    like = lambda size: jax.ShapeDtypeStruct((count, size), bf16)
    return pl.pallas_call(
        mlp_kernel,
        grid=(count // rows,),
        in_specs=[row(model), row(hidden), whole(w_g.shape), whole(w_u.shape)],
        out_specs=[row(hidden), row(hidden), row(hidden), row(model)],
        out_shape=[like(hidden), like(hidden), like(hidden), like(model)],
        compiler_params=params(),
        name="mlp",
    )(xn, dhid, w_g, w_u)


def back_kernel(
    d_rec, w_o, y, h, a, dy_o, g_o, p_o, end_o, abuf, bbuf, car_s, car_p
):
    step = pl.program_id(0)
    width = y.shape[1]

    @pl.when(step == 0)
    def _():
        car_s[...] = jnp.zeros_like(car_s)
        car_p[...] = jnp.ones_like(car_p)

    d_mixed = nn(d_rec[...], w_o[...])
    act, slope = gelu_both(y[...])
    dy_o[...] = (d_mixed * h[...] * slope).astype(bf16)
    put_tiles(abuf, a[...])
    put_tiles(bbuf, d_mixed * act)
    scan_tiles(abuf, bbuf, car_s, car_p, g_o, p_o, width, True)
    end_o[0:1, :] = car_s[0:1, :width]
    end_o[1:2, :] = car_p[0:1, :width]


def back_scan(d_rec, w_o, y, h, a, rows):
    count, model = d_rec.shape
    width = y.shape[1]
    tiles = pl.cdiv(width, LANES)
    steps = count // rows
    row = lambda size: pl.BlockSpec((rows, size), lambda i: (steps - 1 - i, 0))
    like = lambda size, kind: jax.ShapeDtypeStruct((count, size), kind)
    return pl.pallas_call(
        back_kernel,
        grid=(steps,),
        in_specs=[row(model), whole(w_o.shape), row(width), row(width), row(width)],
        out_specs=[row(width), row(width), row(width), whole((8, width))],
        out_shape=[
            like(width, bf16), like(width, f32), like(width, f32),
            jax.ShapeDtypeStruct((8, width), f32),
        ],
        scratch_shapes=[
            pltpu.VMEM((tiles, rows, LANES), f32),
            pltpu.VMEM((tiles, rows, LANES), f32),
            pltpu.VMEM((8, tiles * LANES), f32),
            pltpu.VMEM((8, tiles * LANES), f32),
        ],
        compiler_params=params(),
        name="back_scan",
    )(d_rec, w_o, y, h, a)


def gates_kernel(
    rank, ends, g_l, p_l, pa, pi, xc, hp, u, u_prev, u_halo, mask, w_a, w_i, vec,
    dpa_o, dpi_o, du_o, tail_o, head_o, sum_o,
    qin, dbuf, ubuf,
):
    step = pl.program_id(0)
    steps = pl.num_programs(0)
    rows, width = g_l.shape

    @pl.when(step == 0)
    def _():
        count = ends.shape[0]

        def fold(back, held):
            at = count - 1 - back
            return jnp.where(at > rank[0], ends[at, 0:1, :] + ends[at, 1:2, :] * held, held)

        qin[0:1, :] = lax.fori_loop(0, count, fold, jnp.zeros((1, width), f32))
        sum_o[...] = jnp.zeros_like(sum_o)
        dbuf[rows : rows + 8, :] = jnp.zeros((8, width), f32)

    grad = g_l[...] + p_l[...] * qin[0:1, :]
    live = mask[:, 0:1]
    slope = vec[CONV + 1 : CONV + 2]
    rate, gate, raw, root, mult = gate_terms(pa[...], pi[...], slope, live)
    conv = xc[...].astype(f32)
    d_mult = grad * gate * conv
    d_log = live * (grad * hp[...] * raw - d_mult * (raw * raw) / root)
    d_log_rate = d_log * rate
    d_conv = grad * gate * mult
    d_pa = (d_log_rate * slope * (1.0 - rate)).astype(bf16)
    d_pi = (grad * mult * conv * gate * (1.0 - gate)).astype(bf16)
    dpa_o[...] = d_pa
    dpi_o[...] = d_pi
    d_conv = d_conv + nt(d_pa, w_a[...]) + nt(d_pi, w_i[...])
    total = lambda value: jnp.sum(value, axis=0, keepdims=True)
    u_now = u[...].astype(f32)
    before = jnp.where(step == steps - 1, u_halo[...], u_prev[...]).astype(f32)
    ubuf[0:HALO, :] = before
    ubuf[HALO : HALO + rows, :] = u_now
    dbuf[0:rows, :] = d_conv
    sum_o[0:1, :] += total(d_conv * u_now)
    d_u = vec[0:1] * d_conv
    for back in range(1, CONV):
        sum_o[back : back + 1, :] += total(
            d_conv * mask[:, back : back + 1] * ubuf[HALO - back : HALO - back + rows, :]
        )
        d_u = d_u + vec[back : back + 1] * mask[:, CONV - 1 + back : CONV + back] * dbuf[
            back : back + rows, :
        ]
    sum_o[CONV : CONV + 1, :] += total(d_conv)
    sum_o[CONV + 1 : CONV + 2, :] += total(d_log_rate)
    sum_o[CONV + 2 : CONV + 3, :] += total(d_pa.astype(f32))
    sum_o[CONV + 3 : CONV + 4, :] += total(d_pi.astype(f32))
    du_o[...] = d_u.astype(bf16)

    @pl.when(step == 0)
    def _():
        tail_o[...] = d_u[rows - HALO :, :]

    head = d_conv[0:8, :]
    dbuf[rows : rows + 8, :] = head
    head_o[...] = head


def gates_back(rank, ends, g_l, p_l, pa, pi, xc, hp, u, u_halo, mask, w_a, w_i, vec, rows):
    count, width = g_l.shape
    steps = count // rows
    at = lambda i: steps - 1 - i
    row = lambda size: pl.BlockSpec((rows, size), lambda i: (at(i), 0))
    like = lambda size, kind: jax.ShapeDtypeStruct((count, size), kind)
    per = rows // HALO
    return pl.pallas_call(
        gates_kernel,
        grid=(steps,),
        in_specs=[
            pl.BlockSpec(memory_space=pltpu.SMEM), whole(ends.shape), row(width), row(width),
            row(width), row(width), row(width), row(width), row(width),
            pl.BlockSpec((HALO, width), lambda i: (jnp.maximum(at(i) * per - 1, 0), 0)),
            whole(u_halo.shape), row(mask.shape[1]), whole(w_a.shape), whole(w_i.shape),
            whole(vec.shape),
        ],
        out_specs=[
            row(width), row(width), row(width), whole((HALO, width)), whole((8, width)),
            whole((8, width)),
        ],
        out_shape=[
            like(width, bf16), like(width, bf16), like(width, bf16),
            jax.ShapeDtypeStruct((HALO, width), f32), jax.ShapeDtypeStruct((8, width), f32),
            jax.ShapeDtypeStruct((8, width), f32),
        ],
        scratch_shapes=[
            pltpu.VMEM((8, width), f32),
            pltpu.VMEM((rows + 8, width), f32),
            pltpu.VMEM((HALO + rows, width), f32),
        ],
        compiler_params=params(),
        name="gates_back",
    )(rank, ends, g_l, p_l, pa, pi, xc, hp, u, u, u_halo, mask, w_a, w_i, vec)


def pair_kernel(left, right, weights, out):
    out[...] = (nt(left[...], weights[0]) + nt(right[...], weights[1])).astype(bf16)


def pair_back(left, right, weights, rows):
    count, width = left.shape
    model = weights.shape[1]
    row = lambda size: pl.BlockSpec((rows, size), lambda i: (i, 0))
    return pl.pallas_call(
        pair_kernel,
        grid=(count // rows,),
        in_specs=[row(width), row(width), whole(weights.shape)],
        out_specs=row(model),
        out_shape=jax.ShapeDtypeStruct((count, model), bf16),
        compiler_params=params(),
        name="pair_back",
    )(left, right, weights)


def moments_step(first, second, grad):
    new_first = beta_first * first + (1.0 - beta_first) * grad
    new_second = beta_second * second + (1.0 - beta_second) * grad * grad
    normal = (
        new_first
        * (1.0 / (1.0 - beta_first**STEP))
        / (jnp.sqrt(new_second * (1.0 / (1.0 - beta_second**STEP))) + adam_eps)
    )
    return new_first, new_second, normal


def soap_body(turned, w, m, v, q, nm, nv, nw):
    tile_rows = w.shape[0] // TILE
    tile_cols = w.shape[1] // TILE
    side = lax.broadcasted_iota(jnp.int32, (TILE, 2 * TILE), 1) < TILE
    square = (lax.broadcasted_iota(jnp.int32, (2 * TILE, 2 * TILE), 0) < TILE) == (
        lax.broadcasted_iota(jnp.int32, (2 * TILE, 2 * TILE), 1) < TILE
    )
    for i in range(tile_rows):
        for j in range(0, tile_cols, 2):
            pair = j + 1 < tile_cols
            rows = slice(i * TILE, (i + 1) * TILE)
            cols = slice(j * TILE, (j + (2 if pair else 1)) * TILE)
            lefts = [q[i, j, 0].astype(bf16)]
            right = q[i, j, 1].astype(bf16)
            if pair:
                lefts.append(q[i, j + 1, 0].astype(bf16))
                both = jnp.concatenate([q[i, j, 1], q[i, j + 1, 1]], axis=0)
                right = jnp.where(
                    square, jnp.concatenate([both, both], axis=1), 0.0
                ).astype(bf16)
            choose = lambda parts: jnp.where(side, parts[0], parts[1]) if pair else parts[0]
            inner = choose([turned(rows, cols, left) for left in lefts]).astype(bf16)
            grad = nn(inner, right)
            new_first, new_second, normal = moments_step(m[rows, cols], v[rows, cols], grad)
            nm[rows, cols] = new_first
            nv[rows, cols] = new_second
            low = normal.astype(bf16)
            outer = choose([nn(left, low) for left in lefts]).astype(bf16)
            master = w[rows, cols]
            nw[rows, cols] = master - learn_rate * (nt(outer, right) + decay_rate * master)


def soap_in_kernel(w, m, v, g, q, nm, nv, nw):
    soap_body(lambda rows, cols, left: tn(left, g[rows, cols]), w, m, v, q, nm, nv, nw)


def soap_out_kernel(w, m, v, g, q, nm, nv, nw):
    def turned(rows, cols, left):
        return lax.dot_general(
            left, g[cols, rows], (((0,), (1,)), ((), ())), preferred_element_type=f32
        )

    soap_body(turned, w, m, v, q, nm, nv, nw)


def soap_in(w, m, v, g, q):
    shape = w.shape
    flat = lambda array: array.reshape((-1, shape[-1]))
    w, m, v, g = flat(w), flat(m), flat(v), flat(g)
    height, width = w.shape
    q = q.reshape((height // TILE, width // TILE, 2, TILE, TILE))
    row = pl.BlockSpec((TILE, width), lambda i: (i, 0))
    out = jax.ShapeDtypeStruct(w.shape, f32)
    results = pl.pallas_call(
        soap_in_kernel,
        grid=(height // TILE,),
        in_specs=[row] * 4
        + [pl.BlockSpec((1, width // TILE, 2, TILE, TILE), lambda i: (i, 0, 0, 0, 0))],
        out_specs=[row] * 3,
        out_shape=[out] * 3,
        compiler_params=params(),
        name="soap_in",
    )(w, m, v, g, q)
    return [array.reshape(shape) for array in results]


def soap_out(w, m, v, g, q):
    height, width = w.shape
    rows = height
    for parts in (4, 3, 2):
        if height % (parts * 2 * TILE) == 0:
            rows = height // parts
            break
    row = pl.BlockSpec((rows, width), lambda i: (i, 0))
    out = jax.ShapeDtypeStruct(w.shape, f32)
    return pl.pallas_call(
        soap_out_kernel,
        grid=(height // rows,),
        in_specs=[row] * 3
        + [
            pl.BlockSpec((width, rows), lambda i: (0, i)),
            pl.BlockSpec((rows // TILE, width // TILE, 2, TILE, TILE), lambda i: (i, 0, 0, 0, 0)),
        ],
        out_specs=[row] * 3,
        out_shape=[out] * 3,
        compiler_params=params(),
        name="soap_out",
    )(w, m, v, g, q)


def reorder(array, dim, order):
    shape = array.shape
    parts = order.shape[0]
    reshaped = array.reshape(shape[:dim] + (parts, shape[dim] // parts) + shape[dim + 1 :])
    return jnp.take(reshaped, order, axis=dim, mode="clip").reshape(shape)


def gather_slabs(array):
    return lax.all_gather(array, "mlp", axis=0, tiled=True)


def scatter_slabs(array):
    return lax.psum_scatter(array, "mlp", scatter_dimension=0, tiled=True)


def line_scatter(array):
    count = lax.axis_size("mlp")
    slab = lax.axis_index("mlp")
    share = array.shape[0] // count
    piece = lambda at: lax.dynamic_slice_in_dim(
        array, jnp.clip(at, 0, count - 1) * share, share, 0
    ).astype(f32)
    up = down = 0.0
    for step in range(1, count):
        send_up = (piece(slab + count - step) + up).astype(bf16)
        send_down = (piece(slab - count + step) + down).astype(bf16)
        up = lax.ppermute(send_up, "mlp", [(i, i + 1) for i in range(step)]).astype(f32)
        down = lax.ppermute(
            send_down, "mlp", [(i, i - 1) for i in range(count - step, count)]
        ).astype(f32)
    return piece(slab) + up + down


def line_gather(array):
    count = lax.axis_size("mlp")
    slab = lax.axis_index("mlp")
    share = array.shape[0]
    ups, downs = [array], [array]
    for step in range(1, count):
        ups.append(lax.ppermute(ups[-1], "mlp", [(i, i + 1) for i in range(step - 1, count - 1)]))
        downs.append(lax.ppermute(downs[-1], "mlp", [(i, i - 1) for i in range(1, count - step + 1)]))
    out = jnp.zeros((count * share,) + array.shape[1:], array.dtype)
    out = lax.dynamic_update_slice_in_dim(out, array, slab * share, 0)
    for step in range(1, count):
        part = jnp.where(slab >= step, ups[step], downs[count - step])
        out = lax.dynamic_update_slice_in_dim(out, part, (slab - step) % count * share, 0)
    return out


def hop(array, pairs):
    count = lax.axis_size("tok")
    return lax.ppermute(array, "tok", [(i, i ^ pairs[i % 2]) for i in range(count)])


CORE, NEAR, FAR = (1, 1), (2, 4), (4, 2)


def stored_order(parts, rank):
    indices = jnp.arange(parts, dtype=jnp.int32)
    if parts != 8:
        return indices, indices
    near, far = indices // 2 % 2, indices % 2
    spots = rank ^ (
        indices // 4 + jnp.where(rank % 2 == 0, near * 2 + far * 4, near * 4 + far * 2)
    )
    return spots, invert(spots)


def invert(order):
    indices = jnp.arange(order.shape[0], dtype=jnp.int32)
    return jnp.sum(jnp.where(order[None, :] == indices[:, None], indices[None, :], 0), axis=1)


def gather_tok(array, dim):
    if lax.axis_size("tok") != 8:
        return lax.all_gather(array, "tok", axis=dim, tiled=True)
    two = jnp.concatenate([array, hop(array, FAR)], axis=dim)
    other = hop(two, NEAR)
    four = jnp.concatenate([two, other], axis=dim)
    rest = jnp.split(hop(four, CORE), 4, axis=dim)
    return jnp.concatenate([four, rest[0], rest[2], rest[1], rest[3]], axis=dim)


def scatter_tok(keep, send):
    if lax.axis_size("tok") != 8:
        whole_sum = jnp.concatenate([keep.astype(send.dtype), send], axis=0)
        return lax.psum_scatter(whole_sum, "tok", scatter_dimension=0, tiled=True)
    rows = keep.shape[0] // 4
    low = send.dtype
    got = hop(send, CORE).reshape((2, 2, rows) + keep.shape[1:])
    keep = keep.reshape(got.shape)
    added = lambda at: keep[at].astype(f32) + got[:, at].astype(f32)
    near = hop(added(1).astype(low), NEAR)
    stay = added(0)
    summed = lambda at: stay[at] + near[at].astype(f32)
    far = hop(summed(1).astype(low), FAR)
    return summed(0) + far.astype(f32)


def grad_owned(left, right):
    half = left.shape[1] // 2
    return scatter_tok(
        tn(left[:, :half], right), tn(left[:, half:], right).astype(bf16)
    )


def permute_kernel(order, array, out):
    out[...] = array[...]


def permute_columns(array, order):
    parts = order.shape[0]
    rows, width = array.shape
    size = width // parts
    if size % LANES:
        return reorder(array, 1, order)
    return pl.pallas_call(
        permute_kernel,
        grid_spec=pltpu.PrefetchScalarGridSpec(
            num_scalar_prefetch=1,
            grid=(parts,),
            in_specs=[pl.BlockSpec((rows, size), lambda i, order: (0, order[i]))],
            out_specs=pl.BlockSpec((rows, size), lambda i, order: (0, i)),
        ),
        out_shape=jax.ShapeDtypeStruct(array.shape, array.dtype),
        compiler_params=params(),
        name="permute_columns",
    )(order, array)


def norm_back(value, upstream, gain):
    scale = lax.rsqrt(jnp.mean(value * value, axis=-1, keepdims=True) + norm_eps)
    weighted = upstream * gain
    inner = jnp.mean(value * weighted, axis=-1, keepdims=True)
    d_value = scale * weighted - value * (scale * scale * scale) * inner
    return d_value, jnp.sum(upstream * value * scale, axis=0)


def block_diagonal(blocks):
    count, width, _ = blocks.shape
    return jnp.concatenate(
        [
            jnp.pad(blocks[n], ((0, 0), (n * width, (count - 1 - n) * width)))
            for n in range(count)
        ],
        axis=0,
    )


def diagonal_blocks(array, count):
    width = array.shape[0] // count
    return jnp.stack(
        [array[n * width : (n + 1) * width, n * width : (n + 1) * width] for n in range(count)]
    )


def on_device(
    tokens, segment_ids, owner_table, cotangent,
    w_in_rec, m_in_rec, v_in_rec, q_in_rec,
    w_out_rec, m_out_rec, v_out_rec, q_out_rec,
    w_in_mlp, m_in_mlp, v_in_mlp, q_in_mlp,
    w_out_mlp, m_out_mlp, v_out_mlp, q_out_mlp,
    w_gates, m_gates, v_gates, w_rnn, m_rnn, v_rnn, w_gains, m_gains, v_gains,
):
    parts = lax.axis_size("tok")
    rank = lax.axis_index("tok")
    slabs = lax.axis_size("mlp")
    slab = lax.axis_index("mlp")
    count, model = tokens.shape
    length = count * parts
    share = count // slabs
    rows = min(256, count)
    half = parts // 2
    spots, places = stored_order(parts, rank)
    into_local = jnp.take(invert(owner_table), spots, mode="clip")
    from_local = jnp.take(places, owner_table, mode="clip")
    rank_ref = rank.reshape(1).astype(jnp.int32)

    in_rec = gather_tok(w_in_rec.astype(bf16), 1)
    out_rec_own, in_rec = lax.optimization_barrier((w_out_rec.T.astype(bf16), in_rec))
    out_rec = gather_tok(out_rec_own, 0)
    mlp_own = jnp.concatenate([w_in_mlp[0], w_in_mlp[1], w_out_mlp.T], axis=1).astype(bf16)
    mlp_own, out_rec = lax.optimization_barrier((mlp_own, out_rec))
    mlp_all = gather_tok(mlp_own, 0)
    hid = w_in_mlp.shape[2]

    blocks = w_gates.shape[1]
    gate_part = w_gates.shape[2]
    lead = 2 * blocks
    rnn_part = w_rnn.shape[1]
    small = jnp.concatenate(
        [w_gates.reshape(lead, gate_part), w_rnn, w_gains.reshape(lead, -1)], axis=1
    ).astype(bf16)
    small_all = lax.all_gather(small, "tok", axis=0, tiled=False)
    gains_all = small_all[:, :, gate_part + rnn_part :].reshape(parts, 2, model // parts)
    gains_f = (
        jnp.take(gains_all, spots, axis=0, mode="clip")
        .transpose(1, 0, 2)
        .reshape(2, model)
        .astype(f32)
    )
    ordered = jnp.take(small_all[:, :, : gate_part + rnn_part], owner_table, axis=0, mode="clip")
    gate_mats = ordered[:, :, :gate_part].transpose(1, 0, 2).reshape(2, blocks, BW, BW)
    w_a = block_diagonal(gate_mats[0])
    w_i = block_diagonal(gate_mats[1])
    rnn_f = ordered[:, :, gate_part:].transpose(1, 0, 2).reshape(lead, -1).astype(f32)
    lam = rnn_f[CONV + 1]
    vec = rnn_f.at[CONV + 1].set(-8.0 * jax.nn.softplus(lam))

    tok_s = permute_columns(tokens, into_local)
    cot_s = permute_columns(cotangent, into_local)
    forward_pairs = [(i, i + 1) for i in range(parts - 1)]
    rim = lax.ppermute(tokens[count - HALO :], "tok", forward_pairs)
    halo = reorder(rim, 1, into_local)
    rim_ids = lax.ppermute(segment_ids[count - HALO :], "tok", forward_pairs)
    position = rank * count - HALO + jnp.arange(count + HALO, dtype=jnp.int32)
    ids_ext = jnp.concatenate([rim_ids, segment_ids])
    starts = (position % length == 0) | (ids_ext != jnp.concatenate([ids_ext[:1], ids_ext[:-1]]))
    live_ext = jnp.where(starts, 0.0, 1.0).astype(f32)
    live = live_ext[HALO:]
    valid = [live]
    for back in range(1, CONV):
        before = valid[-1] if back > 1 else jnp.ones((count,), f32)
        valid.append(before * live_ext[HALO - back + 1 : HALO - back + 1 + count])
    ahead = [jnp.concatenate([valid[k][k:], jnp.zeros((k,), f32)]) for k in range(1, CONV)]
    mask = jnp.stack(valid + ahead + [live], axis=1)

    xn_one, y_pre, u_low, u_halo, conv_low, pre_decay, pre_input, decay, h_loc, p_loc, ends = front(
        tok_s, halo, gains_f[0:1], in_rec, w_a, w_i, vec, mask, rows
    )
    ends_all = lax.all_gather(ends[0:2], "tok", axis=0, tiled=False)
    state, state_prev, mixed, branch = finish_state(
        rank_ref, ends_all, h_loc, p_loc, y_pre, out_rec, rows
    )
    own = lambda array: lax.dynamic_slice_in_dim(array, slab * share, share, 0)
    second = own(tok_s).astype(f32) + scatter_slabs(branch).astype(f32)
    second_low = rms_low(second, gains_f[1])
    w_g, w_u, w_d = mlp_all[:, :hid], mlp_all[:, hid : 2 * hid], mlp_all[:, 2 * hid :]
    d_hidden = nn(cot_s, w_d)
    xn_two = gather_slabs(second_low)
    hidden, d_gate, d_up, d_branch = mlp(xn_two, d_hidden, w_g, w_u, rows)
    d_xn_two = scatter_slabs(d_branch).astype(f32)
    g_out_mlp = grad_owned(cot_s, hidden)
    g_in_mlp = jnp.stack([grad_owned(xn_two, d_gate), grad_owned(xn_two, d_up)])
    result_own = second + line_scatter(nt(hidden, w_d).astype(bf16))
    result = line_gather(permute_columns(result_own.astype(bf16), from_local))

    d_value, g_gain_two = norm_back(second, d_xn_two, gains_f[1])
    d_second = own(cot_s).astype(f32) + d_value
    d_rec = gather_slabs(d_second.astype(bf16))
    d_ypre, g_loc, q_loc, ends_back = back_scan(d_rec, out_rec, y_pre, state, decay, rows)
    ends_back_all = lax.all_gather(ends_back[0:2], "tok", axis=0, tiled=False)
    d_pa, d_pi, d_u, d_u_tail, d_conv_head, sums = gates_back(
        rank_ref, ends_back_all, g_loc, q_loc, pre_decay, pre_input, conv_low, state_prev,
        u_low, u_halo, mask, w_a, w_i, vec, rows,
    )
    spill = []
    for ahead_by in range(CONV - 1, 0, -1):
        row_sum = 0.0
        for back in range(ahead_by, CONV):
            at = back - ahead_by
            row_sum = row_sum + rnn_f[back] * mask[at, back] * d_conv_head[at]
        spill.append(row_sum)
    from_next = lax.ppermute(jnp.stack(spill), "tok", [(i + 1, i) for i in range(parts - 1)])
    d_u_tail = d_u_tail + jnp.pad(from_next, ((HALO - CONV + 1, 0), (0, 0)))
    d_u = lax.dynamic_update_slice_in_dim(d_u, d_u_tail.astype(bf16), count - HALO, 0)
    d_xn_one = scatter_slabs(pair_back(d_ypre, d_u, in_rec, rows)).astype(f32)
    g_out_rec = grad_owned(d_rec, mixed)
    g_in_rec = jnp.stack([grad_owned(xn_one, d_ypre), grad_owned(xn_one, d_u)])
    d_value_one, g_gain_one = norm_back(own(tok_s).astype(f32), d_xn_one, gains_f[0])
    d_input_own = (d_second + d_value_one).astype(bf16)
    d_input = gather_slabs(permute_columns(d_input_own, from_local)).astype(f32)

    g_gates = jnp.stack(
        [
            diagonal_blocks(tn(conv_low, d_pa), blocks),
            diagonal_blocks(tn(conv_low, d_pi), blocks),
        ]
    )
    g_rnn = sums.at[CONV + 1].multiply(-8.0 * jax.nn.sigmoid(lam))
    g_small = jnp.concatenate(
        [g_gates.reshape(lead, parts, gate_part), g_rnn.reshape(lead, parts, rnn_part)], axis=2
    ).transpose(1, 0, 2)
    g_small = jnp.take(g_small, into_local, axis=0, mode="clip")
    sum_small = scatter_tok(g_small[:half], g_small[half:])[0]
    sum_gates = sum_small[:, :gate_part].reshape(w_gates.shape)
    sum_rnn = sum_small[:, gate_part:]
    g_gains = jnp.stack([g_gain_one, g_gain_two]).reshape(2, parts, -1).transpose(1, 0, 2)
    sum_gains = lax.psum(scatter_tok(g_gains[:half], g_gains[half:])[0], "mlp")

    low = lambda array: array.astype(bf16)
    out_mlp_new = soap_out(w_out_mlp, m_out_mlp, v_out_mlp, low(g_out_mlp), q_out_mlp)
    in_mlp_new = soap_in(w_in_mlp, m_in_mlp, v_in_mlp, low(g_in_mlp), q_in_mlp)
    out_rec_new = soap_out(w_out_rec, m_out_rec, v_out_rec, low(g_out_rec), q_out_rec)
    in_rec_new = soap_in(w_in_rec, m_in_rec, v_in_rec, low(g_in_rec), q_in_rec)
    gates_m, gates_v, gates_n = moments_step(m_gates, v_gates, sum_gates)
    gates_w = w_gates - learn_rate * (gates_n + decay_rate * w_gates)
    rnn_m, rnn_v, _ = moments_step(m_rnn, v_rnn, sum_rnn)
    gains_m, gains_v, _ = moments_step(m_gains, v_gains, sum_gains)
    return (
        result, d_input,
        in_rec_new[0], in_rec_new[1], in_rec_new[2],
        out_rec_new[0], out_rec_new[1], out_rec_new[2],
        in_mlp_new[0], in_mlp_new[1], in_mlp_new[2],
        out_mlp_new[0], out_mlp_new[1], out_mlp_new[2],
        gates_m, gates_v, gates_w, rnn_m, rnn_v, gains_m, gains_v,
    )


def solution(mesh):
    in_specs = (
        P("tok", None),
        P("tok"),
        P(),
        P("tok", None),
        P(None, "tok", "mlp"),
        P(None, "tok", "mlp"),
        P(None, "tok", "mlp"),
        P(None, "tok", "mlp", None, None, None),
        P("mlp", "tok"),
        P("mlp", "tok"),
        P("mlp", "tok"),
        P("mlp", "tok", None, None, None),
        P(None, "tok", "mlp"),
        P(None, "tok", "mlp"),
        P(None, "tok", "mlp"),
        P(None, "tok", "mlp", None, None, None),
        P("mlp", "tok"),
        P("mlp", "tok"),
        P("mlp", "tok"),
        P("mlp", "tok", None, None, None),
        P(None, "mlp", "tok"),
        P(None, "mlp", "tok"),
        P(None, "mlp", "tok"),
        P(None, ("mlp", "tok")),
        P(None, ("mlp", "tok")),
        P(None, ("mlp", "tok")),
        P(None, "tok"),
        P(None, "tok"),
        P(None, "tok"),
    )
    out_specs = (
        P("tok", None),
        P("tok", None),
        P(None, "tok", "mlp"),
        P(None, "tok", "mlp"),
        P(None, "tok", "mlp"),
        P("mlp", "tok"),
        P("mlp", "tok"),
        P("mlp", "tok"),
        P(None, "tok", "mlp"),
        P(None, "tok", "mlp"),
        P(None, "tok", "mlp"),
        P("mlp", "tok"),
        P("mlp", "tok"),
        P("mlp", "tok"),
        P(None, "mlp", "tok"),
        P(None, "mlp", "tok"),
        P(None, "mlp", "tok"),
        P(None, ("mlp", "tok")),
        P(None, ("mlp", "tok")),
        P(None, "tok"),
        P(None, "tok"),
    )
    return jax.shard_map(
        on_device, mesh=mesh, in_specs=in_specs, out_specs=out_specs, check_vma=False
    )
```

```python
import functools

import jax
import jax.numpy as jnp
from jax import lax
from jax.experimental import pallas as pl
from jax.experimental.pallas import tpu as pltpu
from jax.sharding import PartitionSpec as P

BW = 176
CONV = 4
TILE = 64
STEP = 7
HALO = 16
LANES = 128

norm_eps = 1e-06
learn_rate = 0.02
beta_first = 0.9
beta_second = 0.999
adam_eps = 1e-08
decay_rate = 0.1

f32 = jnp.float32
bf16 = jnp.bfloat16


def params(limit=56):
    return pltpu.CompilerParams(
        dimension_semantics=("arbitrary",), vmem_limit_bytes=limit * 1024 * 1024
    )


def whole(shape):
    return pl.BlockSpec(shape, lambda *_: (0,) * len(shape), pipeline_mode=pl.Buffered(1))


def nn(left, right):
    return lax.dot_general(left, right, (((1,), (0,)), ((), ())), preferred_element_type=f32)


def nt(left, right):
    return lax.dot_general(left, right, (((1,), (1,)), ((), ())), preferred_element_type=f32)


def tn(left, right):
    return lax.dot_general(left, right, (((0,), (0,)), ((), ())), preferred_element_type=f32)


def gelu_both(value):
    square = value * value
    bent = jnp.tanh(0.7978845608028654 * (value + 0.044715 * value * square))
    half = 0.5 * (1.0 + bent)
    slope = half + (0.5 * 0.7978845608028654) * value * (1.0 - bent * bent) * (
        1.0 + (3.0 * 0.044715) * square
    )
    return value * half, slope


def gelu_tanh(value):
    return (
        0.5
        * value
        * (1.0 + jnp.tanh(0.7978845608028654 * (value + 0.044715 * value * value * value)))
    )


def one_less_square(log_value, value):
    twice = 2.0 * log_value
    series = 1.0 + twice * (1.0 / 6.0)
    for order in range(5, 1, -1):
        series = 1.0 + twice * series * (1.0 / order)
    return jnp.where(twice > -0.0625, -twice * series, 1.0 - value * value)


def gate_terms(pre_decay, pre_input, slope, live):
    rate = 0.5 + 0.5 * jnp.tanh(0.5 * pre_decay)
    gate = 0.5 + 0.5 * jnp.tanh(0.5 * pre_input)
    log_decay = slope * rate
    raw = jnp.exp(log_decay)
    root = jnp.sqrt(one_less_square(log_decay, raw))
    mult = (1.0 - live) + live * root
    return rate, gate, raw, root, mult


def put_tiles(buffer, value):
    width = value.shape[1]
    for tile in range(pl.cdiv(width, LANES)):
        size = min(LANES, width - tile * LANES)
        buffer[tile, :, :size] = value[:, tile * LANES : tile * LANES + size]


def scan_tiles(first, second, carry_state, carry_prod, out_state, out_prod, width, backward):
    tiles, rows, _ = first.shape
    span = rows // 8

    def body(step, held):
        row = (span - 1 - step) if backward else step
        at = pl.ds(row, 8, stride=span)
        states, prods = [], []
        for tile in range(tiles):
            state, prod = held[0][tile], held[1][tile]
            decay = first[tile, at, :]
            drive = second[tile, at, :]
            if backward:
                total = drive + state
                second[tile, at, :] = total
                first[tile, at, :] = prod
                states.append(decay * total)
                prods.append(decay * prod)
            else:
                states.append(decay * state + drive)
                prods.append(decay * prod)
                second[tile, at, :] = states[-1]
                first[tile, at, :] = prods[-1]
        return tuple(states), tuple(prods)

    states, prods = lax.fori_loop(
        0,
        span,
        body,
        (
            (jnp.zeros((8, LANES), f32),) * tiles,
            (jnp.ones((8, LANES), f32),) * tiles,
        ),
        unroll=4,
    )
    for tile in range(tiles):
        size = min(LANES, width - tile * LANES)
        cols = slice(tile * LANES, tile * LANES + size)
        wide = slice(tile * LANES, (tile + 1) * LANES)
        state, prod = states[tile], prods[tile]
        state_in = carry_state[0:1, wide]
        prod_in = carry_prod[0:1, wide]
        for chunk in range(7, -1, -1) if backward else range(8):
            at = slice(chunk * span, (chunk + 1) * span)
            local = first[tile, at, :]
            out_state[at, cols] = (second[tile, at, :] + local * state_in)[:, :size]
            out_prod[at, cols] = (local * prod_in)[:, :size]
            state_in = state[chunk : chunk + 1] + prod[chunk : chunk + 1] * state_in
            prod_in = prod[chunk : chunk + 1] * prod_in
        carry_state[0:1, wide] = state_in
        carry_prod[0:1, wide] = prod_in


def piece_spot(array, piece):
    return (0, 2, 1, 3)[piece] if array == 1 else piece


def load_pieces(arrays, which, held, sem, along):
    copies = []
    for number, array in enumerate(arrays):
        size = array.shape[1 + along]
        base = sum(before.shape[0] for before in arrays[:number])
        if base * size >= held.shape[along]:
            break
        for piece in range(array.shape[0]):
            at = pl.ds((base + piece_spot(number, piece)) * size, size)
            for slot, kind in enumerate(which):
                place = held.at[slot, at, :] if along == 1 else held.at[slot, :, at]
                copies.append(pltpu.make_async_copy(array.at[piece, kind], place, sem))
    for copy in copies:
        copy.start()
    for copy in copies:
        copy.wait()


def any_spec():
    return pl.BlockSpec(memory_space=pl.ANY)


def rms_low(value, gain):
    return (
        value * lax.rsqrt(jnp.mean(value * value, axis=-1, keepdims=True) + norm_eps) * gain
    ).astype(bf16)


def front_kernel(
    tok, halo, gain, w_own, w_far, w_a, w_i, vec, mask,
    xn_o, y_o, u_o, uh_o, xc_o, pa_o, pi_o, a_o, h_o, p_o, end_o,
    ubuf, abuf, bbuf, car_s, car_p, w_in, sem,
):
    step = pl.program_id(0)
    rows = tok.shape[0]
    width = y_o.shape[1]

    @pl.when(step == 0)
    def _():
        load_pieces((w_own, w_far), (0, 1), w_in, sem, 2)
        low = nt(rms_low(halo[...].astype(f32), gain[...]), w_in[1]).astype(bf16)
        uh_o[...] = low
        ubuf[0:HALO, :] = low.astype(f32)
        car_s[...] = jnp.zeros_like(car_s)
        car_p[...] = jnp.ones_like(car_p)

    xn = rms_low(tok[...].astype(f32), gain[...])
    xn_o[...] = xn
    y_o[...] = nt(xn, w_in[0])
    u_low = nt(xn, w_in[1]).astype(bf16)
    u_o[...] = u_low
    u_now = u_low.astype(f32)
    ubuf[HALO : HALO + rows, :] = u_now
    conv = vec[CONV : CONV + 1] + vec[0:1] * u_now
    for back in range(1, CONV):
        conv = conv + vec[back : back + 1] * mask[:, back : back + 1] * ubuf[
            HALO - back : HALO - back + rows, :
        ]
    ubuf[0:HALO, :] = u_now[rows - HALO :, :]
    conv_low = conv.astype(bf16)
    xc_o[...] = conv_low
    pre_decay = nn(conv_low, w_a[...]) + vec[CONV + 2 : CONV + 3]
    pre_input = nn(conv_low, w_i[...]) + vec[CONV + 3 : CONV + 4]
    pa_o[...] = pre_decay
    pi_o[...] = pre_input
    live = mask[:, 0:1]
    _, gate, raw, _, mult = gate_terms(pre_decay, pre_input, vec[CONV + 1 : CONV + 2], live)
    decay = raw * live
    a_o[...] = decay
    put_tiles(abuf, decay)
    put_tiles(bbuf, gate * conv_low.astype(f32) * mult)
    scan_tiles(abuf, bbuf, car_s, car_p, h_o, p_o, width, False)
    end_o[0:1, :] = car_s[0:1, :width]
    end_o[1:2, :] = car_p[0:1, :width]


def front(tok, halo, gain, weights, w_a, w_i, vec, mask, rows):
    count, model = tok.shape
    width = weights[0].shape[2]
    tiles = pl.cdiv(width, LANES)
    row = lambda size: pl.BlockSpec((rows, size), lambda i: (i, 0))
    like = lambda size, kind: jax.ShapeDtypeStruct((count, size), kind)
    return pl.pallas_call(
        front_kernel,
        grid=(count // rows,),
        in_specs=[
            row(model), whole(halo.shape), whole(gain.shape), any_spec(), any_spec(),
            whole(w_a.shape), whole(w_i.shape), whole(vec.shape), row(mask.shape[1]),
        ],
        out_specs=[
            row(model), row(width), row(width), whole((HALO, width)), row(width), row(width),
            row(width), row(width), row(width), row(width), whole((8, width)),
        ],
        out_shape=[
            like(model, bf16), like(width, f32), like(width, bf16),
            jax.ShapeDtypeStruct((HALO, width), bf16), like(width, bf16), like(width, f32),
            like(width, f32), like(width, f32), like(width, f32), like(width, f32),
            jax.ShapeDtypeStruct((8, width), f32),
        ],
        scratch_shapes=[
            pltpu.VMEM((HALO + rows, width), f32),
            pltpu.VMEM((tiles, rows, LANES), f32),
            pltpu.VMEM((tiles, rows, LANES), f32),
            pltpu.VMEM((8, tiles * LANES), f32),
            pltpu.VMEM((8, tiles * LANES), f32),
            pltpu.VMEM((2, width, model), bf16),
            pltpu.SemaphoreType.DMA,
        ],
        compiler_params=params(),
        name="front",
    )(tok, halo, gain, *weights, w_a, w_i, vec, mask)


def state_kernel(
    rank, ends, h_l, p_l, y, w_own, w_far, h_o, hp_o, o_o, part_o, hin, hbuf, w_o, sem
):
    step = pl.program_id(0)
    rows = h_l.shape[0]

    @pl.when(step == 0)
    def _():
        load_pieces((w_own, w_far), (2,), w_o, sem, 2)

        def fold(at, held):
            return jnp.where(at < rank[0], ends[at, 0:1, :] + ends[at, 1:2, :] * held, held)

        start = lax.fori_loop(0, ends.shape[0], fold, jnp.zeros((1, h_l.shape[1]), f32))
        hin[0:1, :] = start
        hbuf[7:8, :] = start

    state = h_l[...] + p_l[...] * hin[0:1, :]
    h_o[...] = state
    hbuf[8 : 8 + rows, :] = state
    hp_o[...] = hbuf[7 : 7 + rows, :]
    hbuf[7:8, :] = state[rows - 1 :, :]
    mixed = (state * gelu_tanh(y[...])).astype(bf16)
    o_o[...] = mixed
    part_o[...] = nn(mixed, w_o[0]).astype(bf16)


def finish_state(rank, ends, h_l, p_l, y, weights, model, rows):
    count, width = h_l.shape
    row = lambda size: pl.BlockSpec((rows, size), lambda i: (i, 0))
    like = lambda size, kind: jax.ShapeDtypeStruct((count, size), kind)
    return pl.pallas_call(
        state_kernel,
        grid=(count // rows,),
        in_specs=[
            pl.BlockSpec(memory_space=pltpu.SMEM), whole(ends.shape), row(width), row(width),
            row(width), any_spec(), any_spec(),
        ],
        out_specs=[row(width), row(width), row(width), row(model)],
        out_shape=[like(width, f32), like(width, f32), like(width, bf16), like(model, bf16)],
        scratch_shapes=[
            pltpu.VMEM((8, width), f32),
            pltpu.VMEM((8 + rows, width), f32),
            pltpu.VMEM((1, width, model), bf16),
            pltpu.SemaphoreType.DMA,
        ],
        compiler_params=params(),
        name="finish_state",
    )(rank, ends, h_l, p_l, y, *weights)


def mlp_kernel(xn, dhid, w_own, w_far, hm_o, dg_o, du_o, part_o, held, sem):
    @pl.when(pl.program_id(0) == 0)
    def _():
        load_pieces((w_own, w_far), (0, 1), held, sem, 1)

    w_g, w_u = held.at[0], held.at[1]
    hidden = dhid.shape[1]
    piece = hidden // 3
    for at in range(0, hidden, piece):
        cols = slice(at, at + piece)
        z_gate = nn(xn[...], w_g[:, cols])
        z_up = nn(xn[...], w_u[:, cols])
        d_hid = dhid[:, cols]
        act, slope = gelu_both(z_gate)
        hm_o[:, cols] = (act * z_up).astype(bf16)
        dg_o[:, cols] = (d_hid * z_up * slope).astype(bf16)
        du_o[:, cols] = (d_hid * act).astype(bf16)
    model = xn.shape[1]
    piece = model // 4
    for at in range(0, model, piece):
        cols = slice(at, at + piece)
        part_o[:, cols] = (nt(dg_o[...], w_g[cols, :]) + nt(du_o[...], w_u[cols, :])).astype(bf16)


def mlp(xn, dhid, weights, rows):
    count, model = xn.shape
    hidden = dhid.shape[1]
    row = lambda size: pl.BlockSpec((rows, size), lambda i: (i, 0))
    like = lambda size: jax.ShapeDtypeStruct((count, size), bf16)
    return pl.pallas_call(
        mlp_kernel,
        grid=(count // rows,),
        in_specs=[row(model), row(hidden), any_spec(), any_spec()],
        out_specs=[row(hidden), row(hidden), row(hidden), row(model)],
        out_shape=[like(hidden), like(hidden), like(hidden), like(model)],
        scratch_shapes=[pltpu.VMEM((2, model, hidden), bf16), pltpu.SemaphoreType.DMA],
        compiler_params=params(),
        name="mlp",
    )(xn, dhid, *weights)


def back_kernel(
    d_rec, w_own, w_far, y, h, a, dy_o, g_o, p_o, end_o, abuf, bbuf, car_s, car_p, w_o, sem
):
    step = pl.program_id(0)
    width = y.shape[1]

    @pl.when(step == 0)
    def _():
        load_pieces((w_own, w_far), (2,), w_o, sem, 2)
        car_s[...] = jnp.zeros_like(car_s)
        car_p[...] = jnp.ones_like(car_p)

    d_mixed = nt(d_rec[...], w_o[0])
    act, slope = gelu_both(y[...])
    dy_o[...] = (d_mixed * h[...] * slope).astype(bf16)
    put_tiles(abuf, a[...])
    put_tiles(bbuf, d_mixed * act)
    scan_tiles(abuf, bbuf, car_s, car_p, g_o, p_o, width, True)
    end_o[0:1, :] = car_s[0:1, :width]
    end_o[1:2, :] = car_p[0:1, :width]


def back_scan(d_rec, weights, y, h, a, rows):
    count, model = d_rec.shape
    width = y.shape[1]
    tiles = pl.cdiv(width, LANES)
    steps = count // rows
    row = lambda size: pl.BlockSpec((rows, size), lambda i: (steps - 1 - i, 0))
    like = lambda size, kind: jax.ShapeDtypeStruct((count, size), kind)
    return pl.pallas_call(
        back_kernel,
        grid=(steps,),
        in_specs=[row(model), any_spec(), any_spec(), row(width), row(width), row(width)],
        out_specs=[row(width), row(width), row(width), whole((8, width))],
        out_shape=[
            like(width, bf16), like(width, f32), like(width, f32),
            jax.ShapeDtypeStruct((8, width), f32),
        ],
        scratch_shapes=[
            pltpu.VMEM((tiles, rows, LANES), f32),
            pltpu.VMEM((tiles, rows, LANES), f32),
            pltpu.VMEM((8, tiles * LANES), f32),
            pltpu.VMEM((8, tiles * LANES), f32),
            pltpu.VMEM((1, width, model), bf16),
            pltpu.SemaphoreType.DMA,
        ],
        compiler_params=params(),
        name="back_scan",
    )(d_rec, *weights, y, h, a)


def gates_kernel(
    rank, ends, g_l, p_l, pa, pi, xc, hp, u, u_prev, u_halo, mask, w_a, w_i, vec,
    dpa_o, dpi_o, du_o, tail_o, spill_o, sum_o,
    qin, dbuf, ubuf,
):
    step = pl.program_id(0)
    steps = pl.num_programs(0)
    rows, width = g_l.shape

    @pl.when(step == 0)
    def _():
        count = ends.shape[0]

        def fold(back, held):
            at = count - 1 - back
            return jnp.where(at > rank[0], ends[at, 0:1, :] + ends[at, 1:2, :] * held, held)

        qin[0:1, :] = lax.fori_loop(0, count, fold, jnp.zeros((1, width), f32))
        sum_o[...] = jnp.zeros_like(sum_o)
        dbuf[rows : rows + 8, :] = jnp.zeros((8, width), f32)

    grad = g_l[...] + p_l[...] * qin[0:1, :]
    live = mask[:, 0:1]
    slope = vec[CONV + 1 : CONV + 2]
    rate, gate, raw, root, mult = gate_terms(pa[...], pi[...], slope, live)
    conv = xc[...].astype(f32)
    d_mult = grad * gate * conv
    d_log = live * (grad * hp[...] * raw - d_mult * (raw * raw) / root)
    d_log_rate = d_log * rate
    d_conv = grad * gate * mult
    d_pa = (d_log_rate * slope * (1.0 - rate)).astype(bf16)
    d_pi = (grad * mult * conv * gate * (1.0 - gate)).astype(bf16)
    dpa_o[...] = d_pa
    dpi_o[...] = d_pi
    d_conv = d_conv + nt(d_pa, w_a[...]) + nt(d_pi, w_i[...])
    total = lambda value: jnp.sum(value, axis=0, keepdims=True)
    u_now = u[...].astype(f32)
    before = jnp.where(step == steps - 1, u_halo[...], u_prev[...]).astype(f32)
    ubuf[0:HALO, :] = before
    ubuf[HALO : HALO + rows, :] = u_now
    dbuf[0:rows, :] = d_conv
    sum_o[0:1, :] += total(d_conv * u_now)
    d_u = vec[0:1] * d_conv
    for back in range(1, CONV):
        sum_o[back : back + 1, :] += total(
            d_conv * mask[:, back : back + 1] * ubuf[HALO - back : HALO - back + rows, :]
        )
        d_u = d_u + vec[back : back + 1] * mask[:, CONV - 1 + back : CONV + back] * dbuf[
            back : back + rows, :
        ]
    sum_o[CONV : CONV + 1, :] += total(d_conv)
    sum_o[CONV + 1 : CONV + 2, :] += total(d_log_rate)
    sum_o[CONV + 2 : CONV + 3, :] += total(d_pa.astype(f32))
    sum_o[CONV + 3 : CONV + 4, :] += total(d_pi.astype(f32))
    du_o[...] = d_u.astype(bf16)

    @pl.when(step == 0)
    def _():
        tail_o[...] = d_u[rows - HALO :, :]

    head = d_conv[0:8, :]
    dbuf[rows : rows + 8, :] = head

    @pl.when(step == steps - 1)
    def _():
        spill_o[...] = jnp.zeros_like(spill_o)
        for ahead in range(CONV - 1, 0, -1):
            row = 0.0
            for back in range(ahead, CONV):
                at = back - ahead
                row = row + vec[back : back + 1] * mask[at : at + 1, back : back + 1] * d_conv[
                    at : at + 1, :
                ]
            spill_o[HALO - ahead : HALO - ahead + 1, :] = row


def gates_back(rank, ends, g_l, p_l, pa, pi, xc, hp, u, u_halo, mask, w_a, w_i, vec, rows):
    count, width = g_l.shape
    steps = count // rows
    at = lambda i: steps - 1 - i
    row = lambda size: pl.BlockSpec((rows, size), lambda i: (at(i), 0))
    like = lambda size, kind: jax.ShapeDtypeStruct((count, size), kind)
    per = rows // HALO
    return pl.pallas_call(
        gates_kernel,
        grid=(steps,),
        in_specs=[
            pl.BlockSpec(memory_space=pltpu.SMEM), whole(ends.shape), row(width), row(width),
            row(width), row(width), row(width), row(width), row(width),
            pl.BlockSpec((HALO, width), lambda i: (jnp.maximum(at(i) * per - 1, 0), 0)),
            whole(u_halo.shape), row(mask.shape[1]), whole(w_a.shape), whole(w_i.shape),
            whole(vec.shape),
        ],
        out_specs=[
            row(width), row(width), row(width), whole((HALO, width)), whole((HALO, width)),
            whole((8, width)),
        ],
        out_shape=[
            like(width, bf16), like(width, bf16), like(width, bf16),
            jax.ShapeDtypeStruct((HALO, width), f32), jax.ShapeDtypeStruct((HALO, width), f32),
            jax.ShapeDtypeStruct((8, width), f32),
        ],
        scratch_shapes=[
            pltpu.VMEM((8, width), f32),
            pltpu.VMEM((rows + 8, width), f32),
            pltpu.VMEM((HALO + rows, width), f32),
        ],
        compiler_params=params(),
        name="gates_back",
    )(rank, ends, g_l, p_l, pa, pi, xc, hp, u, u, u_halo, mask, w_a, w_i, vec)


def pair_kernel(left, right, tail, more, w_own, w_far, out, right_o, held, sem):
    step = pl.program_id(0)
    rows = left.shape[0]

    @pl.when(step == 0)
    def _():
        load_pieces((w_own, w_far), (0, 1), held, sem, 2)

    right_o[...] = right[...]

    @pl.when(step == pl.num_programs(0) - 1)
    def _():
        right_o[rows - HALO :, :] = (tail[...] + more[...]).astype(bf16)

    out[...] = (nn(left[...], held[0]) + nn(right_o[...], held[1])).astype(bf16)


def pair_back(left, right, tail, more, weights, model, rows):
    count, width = left.shape
    row = lambda size: pl.BlockSpec((rows, size), lambda i: (i, 0))
    return pl.pallas_call(
        pair_kernel,
        grid=(count // rows,),
        in_specs=[
            row(width), row(width), whole(tail.shape), whole(more.shape), any_spec(), any_spec(),
        ],
        out_specs=[row(model), row(width)],
        out_shape=[
            jax.ShapeDtypeStruct((count, model), bf16),
            jax.ShapeDtypeStruct((count, width), bf16),
        ],
        scratch_shapes=[pltpu.VMEM((2, width, model), bf16), pltpu.SemaphoreType.DMA],
        compiler_params=params(),
        name="pair_back",
    )(left, right, tail, more, *weights)


def mask_kernel(ids, out):
    rows = out.shape[0]
    now = ids[HALO : HALO + rows, :]
    same = lambda by: (now == ids[HALO + by : HALO + by + rows, :]).astype(f32)
    out[...] = jnp.zeros_like(out)
    out[:, 0:1] = same(-1)
    for back in range(1, CONV):
        out[:, back : back + 1] = same(-back)
        out[:, CONV - 1 + back : CONV + back] = same(back)


def masks(ids, count):
    return pl.pallas_call(
        mask_kernel,
        out_shape=jax.ShapeDtypeStruct((count, 8), f32),
        compiler_params=pltpu.CompilerParams(vmem_limit_bytes=16 * 1024 * 1024),
        name="masks",
    )(ids)


def moments_step(first, second, grad):
    new_first = beta_first * first + (1.0 - beta_first) * grad
    new_second = beta_second * second + (1.0 - beta_second) * grad * grad
    normal = (
        new_first
        * (1.0 / (1.0 - beta_first**STEP))
        / (jnp.sqrt(new_second * (1.0 / (1.0 - beta_second**STEP))) + adam_eps)
    )
    return new_first, new_second, normal


def soap_tiles(turned, tile_rows, tile_cols, w, m, v, bases, nm, nv, nw):
    side = lax.broadcasted_iota(jnp.int32, (TILE, 2 * TILE), 1) < TILE
    square = (lax.broadcasted_iota(jnp.int32, (2 * TILE, 2 * TILE), 0) < TILE) == (
        lax.broadcasted_iota(jnp.int32, (2 * TILE, 2 * TILE), 1) < TILE
    )
    for i in range(tile_rows):
        for j in range(0, tile_cols, 2):
            rows = slice(i * TILE, (i + 1) * TILE)
            cols = slice(j * TILE, (j + 2) * TILE)
            left_a, right_a = bases(i, j)
            left_b, right_b = bases(i, j + 1)
            lefts = [left_a.astype(bf16), left_b.astype(bf16)]
            both = jnp.concatenate([right_a, right_b], axis=0)
            right = jnp.where(square, jnp.concatenate([both, both], axis=1), 0.0).astype(bf16)
            choose = lambda parts: jnp.where(side, parts[0], parts[1])
            inner = choose([turned(rows, cols, left) for left in lefts]).astype(bf16)
            grad = nn(inner, right)
            new_first, new_second, normal = moments_step(m[rows, cols], v[rows, cols], grad)
            nm[rows, cols] = new_first
            nv[rows, cols] = new_second
            low = normal.astype(bf16)
            outer = choose([nn(left, low) for left in lefts]).astype(bf16)
            master = w[rows, cols]
            nw[rows, cols] = master - learn_rate * (nt(outer, right) + decay_rate * master)


def soap_kernel(turned, swapped, w, m, v, g, q, nm, nv, nw):
    def plain(rows, cols, left):
        return tn(left, g[0, rows, cols])

    def across(rows, cols, left):
        return lax.dot_general(
            left, g[0, cols, rows], (((0,), (1,)), ((), ())), preferred_element_type=f32
        )

    if swapped:
        bases = lambda i, j: (q[0, j, i, 1], q[0, j, i, 0])
    else:
        bases = lambda i, j: (q[0, i, j, 0], q[0, i, j, 1])
    soap_tiles(
        across if turned else plain, w.shape[1] // TILE, w.shape[2] // TILE,
        w.at[0], m.at[0], v.at[0], bases, nm.at[0], nv.at[0], nw.at[0],
    )


def soap(w, m, v, g, q, rows, turned=False, swapped=False):
    group, height, width = w.shape
    if width < 2 * TILE:
        q = jnp.concatenate([q, q], axis=1 if swapped else 2)
        padded = [jnp.concatenate([array, array], axis=2) for array in (w, m, v)]
        g = jnp.concatenate([g, g], axis=1 if turned else 2)
        results = soap(*padded, g, q, rows, turned, swapped)
        return [array[:, :, :width] for array in results]
    row = pl.BlockSpec((1, rows, width), lambda n, i: (n, i, 0))
    out = jax.ShapeDtypeStruct(w.shape, f32)
    if swapped:
        q_block = (1, width // TILE, rows // TILE, 2, TILE, TILE)
        q_at = lambda n, i: (n, 0, i, 0, 0, 0)
    else:
        q_block = (1, rows // TILE, width // TILE, 2, TILE, TILE)
        q_at = lambda n, i: (n, i, 0, 0, 0, 0)
    return pl.pallas_call(
        functools.partial(soap_kernel, turned, swapped),
        grid=(group, height // rows),
        in_specs=[row] * 3
        + [
            pl.BlockSpec((1, width, rows), lambda n, i: (n, 0, i)) if turned else row,
            pl.BlockSpec(q_block, q_at),
        ],
        out_specs=[row] * 3,
        out_shape=[out] * 3,
        compiler_params=pltpu.CompilerParams(
            dimension_semantics=("arbitrary", "arbitrary"), vmem_limit_bytes=56 * 1024 * 1024
        ),
        name="soap",
    )(w, m, v, g, q)


def reorder(array, dim, order):
    shape = array.shape
    parts = order.shape[0]
    reshaped = array.reshape(shape[:dim] + (parts, shape[dim] // parts) + shape[dim + 1 :])
    return jnp.take(reshaped, order, axis=dim, mode="clip").reshape(shape)


def gather_slabs(array):
    return lax.all_gather(array, "mlp", axis=0, tiled=True)


def scatter_slabs(array):
    return lax.psum_scatter(array, "mlp", scatter_dimension=0, tiled=True)


def hop(array, pairs):
    count = lax.axis_size("tok")
    return lax.ppermute(array, "tok", [(i, i ^ pairs[i % 2]) for i in range(count)])


CORE, NEAR, FAR = (1, 1), (2, 4), (4, 2)


def stored_order(parts, rank):
    indices = jnp.arange(parts, dtype=jnp.int32)
    if parts != 8:
        return indices, indices
    near, far = indices // 2 % 2, indices % 2
    spots = rank ^ (
        indices // 4 + jnp.where(rank % 2 == 0, near * 2 + far * 4, near * 4 + far * 2)
    )
    return spots, invert(spots)


def invert(order):
    indices = jnp.arange(order.shape[0], dtype=jnp.int32)
    return jnp.sum(jnp.where(order[None, :] == indices[:, None], indices[None, :], 0), axis=1)


def gather_start(own):
    two = jnp.concatenate([own, hop(own, FAR)], axis=0)
    return jnp.concatenate([two, hop(two, NEAR)], axis=0)


class Sums:
    def __init__(self, keep, send, dim):
        self.keep, self.send, self.dim = keep, send, dim
        self.whole = lax.axis_size("tok") != 8

    def cut(self, array, blocks, at):
        size = array.shape[self.dim] // blocks
        return lax.slice_in_dim(array, at * size, (at + 1) * size, axis=self.dim).astype(f32)

    def mixed(self, at, there):
        return self.cut(self.keep, 4, at) + self.cut(self.got, 4, there)

    def first(self, *before):
        if self.whole:
            return self.send
        self.got = hop(self.send, CORE)
        self.near_send = after(
            jnp.concatenate([self.mixed(2, 1), self.mixed(3, 3)], axis=self.dim).astype(
                self.send.dtype
            ),
            *before,
        )
        return self.near_send

    def second(self, *before):
        if self.whole:
            return self.send
        self.near = hop(self.near_send, NEAR)
        self.far_send = after(
            (self.mixed(1, 2) + self.cut(self.near, 2, 1)).astype(self.send.dtype), *before
        )
        return self.far_send

    def third(self):
        if self.whole:
            both = jnp.concatenate([self.keep.astype(self.send.dtype), self.send], axis=self.dim)
            return lax.psum_scatter(both, "tok", scatter_dimension=self.dim, tiled=True)
        far = hop(self.far_send, FAR)
        return self.mixed(0, 0) + self.cut(self.near, 2, 0) + far.astype(f32)


def sums_of(array):
    half = array.shape[0] // 2
    sums = Sums(array[:half], array[half:], 0)
    sums.first()
    sums.second()
    return sums.third()


def halves(array):
    half = array.shape[1] // 2
    return array[:, :half], array[:, half:]


def grad_rows(left, right):
    keep, send = halves(left)
    return Sums(tn(keep, right), tn(send, right).astype(bf16), 0)


def grad_columns(left, right):
    keep, send = halves(right)
    return Sums(tn(left, keep), tn(left, send).astype(bf16), 1)


def permute_kernel(order, array, out):
    parts = order.shape[0]
    size = array.shape[1] // parts
    for part in range(parts):
        at = pl.multiple_of(order[part] * size, LANES)
        out[:, part * size : (part + 1) * size] = array[:, pl.ds(at, size)]


def permute_columns(array, order):
    parts = order.shape[0]
    count, width = array.shape
    if width // parts % LANES:
        return reorder(array, 1, order)
    rows = min(256, count)
    row = pl.BlockSpec((rows, width), lambda i: (i, 0))
    return pl.pallas_call(
        permute_kernel,
        grid=(count // rows,),
        in_specs=[pl.BlockSpec(memory_space=pltpu.SMEM), row],
        out_specs=row,
        out_shape=jax.ShapeDtypeStruct(array.shape, array.dtype),
        compiler_params=params(),
        name="permute_columns",
    )(order, array)


def settle_kernel(move, order, value, upstream, gain, base, total_o, low_o, sum_o, hold):
    @pl.when(pl.program_id(0) == 0)
    def _():
        sum_o[...] = jnp.zeros_like(sum_o)

    held = value[...].astype(f32)
    grad = upstream[...].astype(f32)
    scale = lax.rsqrt(jnp.mean(held * held, axis=-1, keepdims=True) + norm_eps)
    weighted = grad * gain[...]
    inner = jnp.mean(held * weighted, axis=-1, keepdims=True)
    total = base[...].astype(f32) + (scale * weighted - held * (scale * scale * scale * inner))
    sum_o[0:1, :] += jnp.sum(grad * held * scale, axis=0, keepdims=True)
    total_o[...] = total
    low = total.astype(bf16)
    if not move:
        low_o[...] = low
        return
    hold[...] = low
    parts = order.shape[0]
    size = low.shape[1] // parts
    for part in range(parts):
        at = pl.multiple_of(order[part] * size, LANES)
        low_o[:, part * size : (part + 1) * size] = hold[:, pl.ds(at, size)]


def settle(value, upstream, gain, base, order, move):
    count, model = value.shape
    inside = move and (model // order.shape[0]) % LANES == 0
    rows = min(128, count)
    row = pl.BlockSpec((rows, model), lambda i: (i, 0))
    total, low, sums = pl.pallas_call(
        functools.partial(settle_kernel, inside),
        grid=(count // rows,),
        in_specs=[pl.BlockSpec(memory_space=pltpu.SMEM), row, row, whole(gain.shape), row],
        out_specs=[row, row, whole((8, model))],
        out_shape=[
            jax.ShapeDtypeStruct((count, model), f32),
            jax.ShapeDtypeStruct((count, model), bf16),
            jax.ShapeDtypeStruct((8, model), f32),
        ],
        scratch_shapes=[pltpu.VMEM((rows, model), bf16)],
        compiler_params=params(),
        name="settle",
    )(order, value, upstream, gain, base)
    if move and not inside:
        low = reorder(low, 1, order)
    return total, low, sums[0]


def after(array, *others):
    return lax.optimization_barrier((array,) + others)[0]


def block_diagonal(blocks):
    count, width, _ = blocks.shape
    return jnp.concatenate(
        [
            jnp.pad(blocks[n], ((0, 0), (n * width, (count - 1 - n) * width)))
            for n in range(count)
        ],
        axis=0,
    )


def diagonal_blocks(array, count):
    width = array.shape[0] // count
    return jnp.stack(
        [array[n * width : (n + 1) * width, n * width : (n + 1) * width] for n in range(count)]
    )


def on_device(
    tokens, segment_ids, owner_table, cotangent,
    w_in_rec, m_in_rec, v_in_rec, q_in_rec,
    w_out_rec, m_out_rec, v_out_rec, q_out_rec,
    w_in_mlp, m_in_mlp, v_in_mlp, q_in_mlp,
    w_out_mlp, m_out_mlp, v_out_mlp, q_out_mlp,
    w_gates, m_gates, v_gates, w_rnn, m_rnn, v_rnn, w_gains, m_gains, v_gains,
):
    parts = lax.axis_size("tok")
    rank = lax.axis_index("tok")
    slabs = lax.axis_size("mlp")
    slab = lax.axis_index("mlp")
    count, model = tokens.shape
    length = count * parts
    share = count // slabs
    rows = min(256, count)
    spots, places = stored_order(parts, rank)
    into_local = jnp.take(invert(owner_table), spots, mode="clip")
    from_local = jnp.take(places, owner_table, mode="clip")
    rank_ref = rank.reshape(1).astype(jnp.int32)

    blocks = w_gates.shape[1]
    gate_part = w_gates.shape[2]
    lead = 2 * blocks
    rnn_part = w_rnn.shape[1]
    small = jnp.concatenate(
        [w_gates.reshape(lead, gate_part), w_rnn, w_gains.reshape(lead, -1)], axis=1
    ).astype(bf16)
    if parts == 8:
        small_four = gather_start(small[None])
        small_rest = hop(small_four, CORE)
        small_all = jnp.concatenate(
            [small_four] + [small_rest[p : p + 1] for p in (0, 2, 1, 3)], axis=0
        )
    else:
        small_all = lax.all_gather(small, "tok", axis=0, tiled=False)
    turn = lambda array: jnp.swapaxes(array, 1, 2)
    rec_own = jnp.concatenate([turn(w_in_rec), w_out_rec[None]], axis=0).astype(bf16)[None]
    join = lambda *arrays: jnp.concatenate(arrays, axis=0)
    if parts == 8:
        rec_far = hop(rec_own, FAR)
        rec_two = join(rec_own, rec_far)
        rec_near = hop(rec_two, NEAR)
    gains_all = small_all[:, :, gate_part + rnn_part :].reshape(parts, 2, model // parts)
    gains_f = (
        gains_all
        .transpose(1, 0, 2)
        .reshape(2, model)
        .astype(f32)
    )
    ordered = jnp.take(small_all[:, :, : gate_part + rnn_part], from_local, axis=0, mode="clip")
    gate_mats = ordered[:, :, :gate_part].transpose(1, 0, 2).reshape(2, blocks, BW, BW)
    w_a = block_diagonal(gate_mats[0])
    w_i = block_diagonal(gate_mats[1])
    rnn_f = ordered[:, :, gate_part:].transpose(1, 0, 2).reshape(lead, -1).astype(f32)
    lam = rnn_f[CONV + 1]
    vec = rnn_f.at[CONV + 1].set(-8.0 * jax.nn.softplus(lam))

    tok_s = permute_columns(tokens, into_local)
    cot_s = permute_columns(cotangent, into_local)
    forward_pairs = [(i, i + 1) for i in range(parts - 1)]
    rim = lax.ppermute(tokens[count - HALO :], "tok", forward_pairs)
    halo = permute_columns(rim, into_local)
    rim_ids = lax.ppermute(segment_ids[count - HALO :], "tok", forward_pairs)
    ids = jnp.concatenate(
        [
            jnp.where(rank == 0, -1, rim_ids).astype(f32),
            segment_ids.astype(f32),
            jnp.full((HALO,), -1.0, f32),
        ]
    )
    mask = masks(ids[:, None], count)
    if parts == 8:
        rec_near = after(rec_near, tok_s, halo, mask, w_a, w_i, vec)
        rec_four = join(rec_two, rec_near)
        rec_w = (rec_four, hop(rec_four, CORE))
    else:
        rec_all = lax.all_gather(rec_own[0], "tok", axis=2, tiled=True)[None]
        rec_w = (rec_all, rec_all)

    xn_one, y_pre, u_low, u_halo, conv_low, pre_decay, pre_input, decay, h_loc, p_loc, ends = front(
        tok_s, halo, gains_f[0:1], rec_w, w_a, w_i, vec, mask, rows
    )
    ends_all = lax.all_gather(ends[0:2], "tok", axis=0, tiled=False)
    state, state_prev, mixed, branch = finish_state(
        rank_ref, ends_all, h_loc, p_loc, y_pre, rec_w, model, rows
    )
    own = lambda array: lax.dynamic_slice_in_dim(array, slab * share, share, 0)
    own_tok = own(tok_s)
    second = own_tok.astype(f32) + scatter_slabs(branch).astype(f32)
    second_low = rms_low(second, gains_f[1])
    up_own = after(w_in_mlp.astype(bf16)[None], branch)
    down_own = after(w_out_mlp.astype(bf16)[None], branch)
    if parts == 8:
        down_four = gather_start(down_own)
        down_rest = hop(down_four, CORE)
        down = jnp.concatenate(
            [down_four[p] for p in range(4)] + [down_rest[p] for p in (0, 2, 1, 3)], axis=1
        )
        up_two = join(up_own, hop(after(up_own, down_four), FAR))
        up_near = after(hop(up_two, NEAR), second_low)
        up_four = join(up_two, up_near)
        up_w = (up_four, hop(up_four, CORE))
    else:
        down = lax.all_gather(down_own[0], "tok", axis=1, tiled=True)
        up_all = lax.all_gather(up_own[0], "tok", axis=1, tiled=True)[None]
        up_w = (up_all, up_all)
    cot_s = permute_columns(after(cotangent, branch), into_local)
    d_hidden = nt(cot_s, down)
    xn_two = gather_slabs(second_low)
    hidden, d_gate, d_up, d_branch = mlp(xn_two, d_hidden, up_w, min(512, count))
    d_xn_two = scatter_slabs(d_branch)
    low = lambda array: array.astype(bf16)
    sum_gate = grad_rows(xn_two, d_gate)
    sum_up = grad_rows(xn_two, d_up)
    sum_down = grad_rows(cot_s, hidden)
    branch_two = nn(hidden, down).astype(bf16)
    d_xn_two = after(
        d_xn_two, sum_gate.first(), sum_up.first(), sum_down.first(), branch_two
    )
    sum_gate.second()
    sum_up.second()
    sum_down.second()
    g_in_mlp = jnp.stack([low(sum_gate.third()), low(sum_up.third())])
    g_out_mlp = low(sum_down.third())

    lead_one = lambda *arrays: [array[None] for array in arrays]
    split = lambda height: max(
        n for n in range(2 * TILE, height + 1, 2 * TILE) if height % n == 0 and n <= 512
    )
    in_mlp_new = soap(w_in_mlp, m_in_mlp, v_in_mlp, g_in_mlp, q_in_mlp, TILE)

    d_second, d_second_low, g_gain_two = settle(
        second, d_xn_two, gains_f[1:2], own(cot_s), from_local, False
    )
    d_rec = gather_slabs(d_second_low)
    branch_two = after(branch_two, in_mlp_new[0])
    d_rec = after(d_rec, in_mlp_new[0])
    result_own = second + scatter_slabs(branch_two).astype(f32)
    result_low = permute_columns(result_own.astype(bf16), from_local)
    d_ypre, g_loc, q_loc, ends_back = back_scan(d_rec, rec_w, y_pre, state, decay, rows)
    ends_back_all = lax.all_gather(ends_back[0:2], "tok", axis=0, tiled=False)
    d_pa, d_pi, d_u, d_u_tail, spill, sums = gates_back(
        rank_ref, ends_back_all, g_loc, q_loc, pre_decay, pre_input, conv_low, state_prev,
        u_low, u_halo, mask, w_a, w_i, vec, rows,
    )
    from_next = lax.ppermute(spill, "tok", [(i + 1, i) for i in range(parts - 1)])
    d_pair, d_u = pair_back(d_ypre, d_u, d_u_tail, from_next, rec_w, model, rows)
    d_xn_one = scatter_slabs(d_pair)
    out_mlp_new = soap(
        *lead_one(w_out_mlp, m_out_mlp, v_out_mlp, after(g_out_mlp, d_pair), q_out_mlp),
        split(w_out_mlp.shape[0]), turned=True,
    )
    d_rec, mixed, xn_one, d_ypre, d_u, d_pa, d_pi, conv_low = lax.optimization_barrier(
        (d_rec, mixed, xn_one, d_ypre, d_u, d_pa, d_pi, conv_low, d_pair)
    )[:8]
    sum_out = grad_columns(mixed, d_rec)
    sum_y = grad_columns(d_ypre, xn_one)
    sum_u = grad_columns(d_u, xn_one)
    d_xn_one = after(
        d_xn_one, sum_out.first(), sum_y.first(), sum_u.first(), out_mlp_new[0]
    )
    _, d_input_low, g_gain_one = settle(
        own_tok, d_xn_one, gains_f[0:1], d_second, from_local, True
    )
    d_input = gather_slabs(d_input_low)
    sum_out.second()
    sum_y.second()
    sum_u.second()
    g_out_rec = low(sum_out.third())
    g_in_rec = jnp.stack([low(sum_y.third()), low(sum_u.third())])
    result = gather_slabs(after(result_low, d_input_low))

    g_gates = jnp.stack(
        [
            diagonal_blocks(tn(conv_low, d_pa), blocks),
            diagonal_blocks(tn(conv_low, d_pi), blocks),
        ]
    )
    g_rnn = sums.at[CONV + 1].multiply(-8.0 * jax.nn.sigmoid(lam))
    g_small = jnp.concatenate(
        [g_gates.reshape(lead, parts, gate_part), g_rnn.reshape(lead, parts, rnn_part)], axis=2
    ).transpose(1, 0, 2)
    g_small = jnp.take(g_small, into_local, axis=0, mode="clip")
    sum_small = sums_of(g_small)[0]
    sum_gates = sum_small[:, :gate_part].reshape(w_gates.shape)
    sum_rnn = sum_small[:, gate_part:]
    g_gains = jnp.stack([g_gain_one, g_gain_two]).reshape(2, parts, -1).transpose(1, 0, 2)
    sum_gains = lax.psum(sums_of(g_gains)[0], "mlp")

    out_rec_new = soap(
        *lead_one(w_out_rec, m_out_rec, v_out_rec, g_out_rec, q_out_rec), w_out_rec.shape[0]
    )
    in_rec_new = soap(
        turn(w_in_rec), turn(m_in_rec), turn(v_in_rec), g_in_rec, q_in_rec, w_in_rec.shape[2],
        swapped=True,
    )
    out_mlp_new = [array[0] for array in out_mlp_new]
    out_rec_new = [array[0] for array in out_rec_new]
    in_rec_new = [turn(array) for array in in_rec_new]
    gates_m, gates_v, gates_n = moments_step(m_gates, v_gates, sum_gates)
    gates_w = w_gates - learn_rate * (gates_n + decay_rate * w_gates)
    rnn_m, rnn_v, _ = moments_step(m_rnn, v_rnn, sum_rnn)
    gains_m, gains_v, _ = moments_step(m_gains, v_gains, sum_gains)
    d_input = after(
        d_input, in_rec_new[0], out_rec_new[0], gates_w, rnn_m
    ).astype(f32)
    return (
        result, d_input,
        in_rec_new[0], in_rec_new[1], in_rec_new[2],
        out_rec_new[0], out_rec_new[1], out_rec_new[2],
        in_mlp_new[0], in_mlp_new[1], in_mlp_new[2],
        out_mlp_new[0], out_mlp_new[1], out_mlp_new[2],
        gates_m, gates_v, gates_w, rnn_m, rnn_v, gains_m, gains_v,
    )


def solution(mesh):
    in_specs = (
        P("tok", None),
        P("tok"),
        P(),
        P("tok", None),
        P(None, "tok", "mlp"),
        P(None, "tok", "mlp"),
        P(None, "tok", "mlp"),
        P(None, "tok", "mlp", None, None, None),
        P("mlp", "tok"),
        P("mlp", "tok"),
        P("mlp", "tok"),
        P("mlp", "tok", None, None, None),
        P(None, "tok", "mlp"),
        P(None, "tok", "mlp"),
        P(None, "tok", "mlp"),
        P(None, "tok", "mlp", None, None, None),
        P("mlp", "tok"),
        P("mlp", "tok"),
        P("mlp", "tok"),
        P("mlp", "tok", None, None, None),
        P(None, "mlp", "tok"),
        P(None, "mlp", "tok"),
        P(None, "mlp", "tok"),
        P(None, ("mlp", "tok")),
        P(None, ("mlp", "tok")),
        P(None, ("mlp", "tok")),
        P(None, "tok"),
        P(None, "tok"),
        P(None, "tok"),
    )
    out_specs = (
        P("tok", None),
        P("tok", None),
        P(None, "tok", "mlp"),
        P(None, "tok", "mlp"),
        P(None, "tok", "mlp"),
        P("mlp", "tok"),
        P("mlp", "tok"),
        P("mlp", "tok"),
        P(None, "tok", "mlp"),
        P(None, "tok", "mlp"),
        P(None, "tok", "mlp"),
        P("mlp", "tok"),
        P("mlp", "tok"),
        P("mlp", "tok"),
        P(None, "mlp", "tok"),
        P(None, "mlp", "tok"),
        P(None, "mlp", "tok"),
        P(None, ("mlp", "tok")),
        P(None, ("mlp", "tok")),
        P(None, "tok"),
        P(None, "tok"),
    )
    return jax.shard_map(
        on_device, mesh=mesh, in_specs=in_specs, out_specs=out_specs, check_vma=False
    )
```

```python
import functools

import jax
import jax.numpy as jnp
from jax import lax
from jax.experimental import pallas as pl
from jax.experimental.pallas import tpu as pltpu
from jax.sharding import PartitionSpec as P

BW = 176
CONV = 4
TILE = 64
STEP = 7
HALO = 16
LANES = 128

norm_eps = 1e-06
learn_rate = 0.02
beta_first = 0.9
beta_second = 0.999
adam_eps = 1e-08
decay_rate = 0.1

f32 = jnp.float32
bf16 = jnp.bfloat16


def params(limit=56):
    return pltpu.CompilerParams(
        dimension_semantics=("arbitrary",), vmem_limit_bytes=limit * 1024 * 1024
    )


def cost(micros):
    return pl.CostEstimate(
        flops=int(micros * 1.1e9), bytes_accessed=int(micros * 3.3e6), transcendentals=0
    )


def whole(shape):
    return pl.BlockSpec(shape, lambda *_: (0,) * len(shape), pipeline_mode=pl.Buffered(1))


def nn(left, right):
    return lax.dot_general(left, right, (((1,), (0,)), ((), ())), preferred_element_type=f32)


def nt(left, right):
    return lax.dot_general(left, right, (((1,), (1,)), ((), ())), preferred_element_type=f32)


def tn(left, right):
    return lax.dot_general(left, right, (((0,), (0,)), ((), ())), preferred_element_type=f32)


def gelu_both(value):
    square = value * value
    bent = jnp.tanh(0.7978845608028654 * (value + 0.044715 * value * square))
    half = 0.5 * (1.0 + bent)
    slope = half + (0.5 * 0.7978845608028654) * value * (1.0 - bent * bent) * (
        1.0 + (3.0 * 0.044715) * square
    )
    return value * half, slope


def gelu_tanh(value):
    return (
        0.5
        * value
        * (1.0 + jnp.tanh(0.7978845608028654 * (value + 0.044715 * value * value * value)))
    )


def one_less_square(log_value, value):
    twice = 2.0 * log_value
    series = 1.0 + twice * (1.0 / 6.0)
    for order in range(5, 1, -1):
        series = 1.0 + twice * series * (1.0 / order)
    return jnp.where(twice > -0.0625, -twice * series, 1.0 - value * value)


def gate_terms(pre_decay, pre_input, slope, live):
    rate = 0.5 + 0.5 * jnp.tanh(0.5 * pre_decay)
    gate = 0.5 + 0.5 * jnp.tanh(0.5 * pre_input)
    log_decay = slope * rate
    raw = jnp.exp(log_decay)
    root = jnp.sqrt(one_less_square(log_decay, raw))
    mult = (1.0 - live) + live * root
    return rate, gate, raw, root, mult


def put_tiles(buffer, value):
    width = value.shape[1]
    for tile in range(pl.cdiv(width, LANES)):
        size = min(LANES, width - tile * LANES)
        buffer[tile, :, :size] = value[:, tile * LANES : tile * LANES + size]


def scan_tiles(first, second, carry_state, carry_prod, out_state, out_prod, width, backward):
    tiles, rows, _ = first.shape
    span = rows // 8

    def body(step, held):
        row = (span - 1 - step) if backward else step
        at = pl.ds(row, 8, stride=span)
        states, prods = [], []
        for tile in range(tiles):
            state, prod = held[0][tile], held[1][tile]
            decay = first[tile, at, :]
            drive = second[tile, at, :]
            if backward:
                total = drive + state
                second[tile, at, :] = total
                first[tile, at, :] = prod
                states.append(decay * total)
                prods.append(decay * prod)
            else:
                states.append(decay * state + drive)
                prods.append(decay * prod)
                second[tile, at, :] = states[-1]
                first[tile, at, :] = prods[-1]
        return tuple(states), tuple(prods)

    states, prods = lax.fori_loop(
        0,
        span,
        body,
        (
            (jnp.zeros((8, LANES), f32),) * tiles,
            (jnp.ones((8, LANES), f32),) * tiles,
        ),
        unroll=4,
    )
    for tile in range(tiles):
        size = min(LANES, width - tile * LANES)
        cols = slice(tile * LANES, tile * LANES + size)
        wide = slice(tile * LANES, (tile + 1) * LANES)
        state, prod = states[tile], prods[tile]
        state_in = carry_state[0:1, wide]
        prod_in = carry_prod[0:1, wide]
        for chunk in range(7, -1, -1) if backward else range(8):
            at = slice(chunk * span, (chunk + 1) * span)
            local = first[tile, at, :]
            out_state[at, cols] = (second[tile, at, :] + local * state_in)[:, :size]
            out_prod[at, cols] = (local * prod_in)[:, :size]
            state_in = state[chunk : chunk + 1] + prod[chunk : chunk + 1] * state_in
            prod_in = prod[chunk : chunk + 1] * prod_in
        carry_state[0:1, wide] = state_in
        carry_prod[0:1, wide] = prod_in


SPOTS = ((0, 1), (2, 3), (4, 6), (5, 7))


def load_pieces(arrays, which, held, sem, along):
    copies = []
    for array, spots in zip(arrays, SPOTS):
        size = array.shape[1 + along]
        if size == held.shape[along]:
            spots = (0,)
        for piece, spot in enumerate(spots):
            at = pl.ds(spot * size, size)
            for slot, kind in enumerate(which):
                place = held.at[slot, at, :] if along == 1 else held.at[slot, :, at]
                copies.append(pltpu.make_async_copy(array.at[piece, kind], place, sem))
        if size == held.shape[along]:
            break
    for copy in copies:
        copy.start()
    for copy in copies:
        copy.wait()


def any_specs():
    return [pl.BlockSpec(memory_space=pl.ANY)] * len(SPOTS)


def rms_low(value, gain):
    return (
        value * lax.rsqrt(jnp.mean(value * value, axis=-1, keepdims=True) + norm_eps) * gain
    ).astype(bf16)


def front_kernel(
    tok, halo, gain, w_0, w_1, w_2, w_3, w_a, w_i, vec, mask,
    xn_o, y_o, u_o, uh_o, xc_o, pa_o, pi_o, a_o, h_o, p_o, end_o,
    ubuf, abuf, bbuf, car_s, car_p, w_in, sem,
):
    step = pl.program_id(0)
    rows = tok.shape[0]
    width = y_o.shape[1]

    @pl.when(step == 0)
    def _():
        load_pieces((w_0, w_1, w_2, w_3), (0, 1), w_in, sem, 2)
        low = nt(rms_low(halo[...].astype(f32), gain[...]), w_in[1]).astype(bf16)
        uh_o[...] = low
        ubuf[0:HALO, :] = low.astype(f32)
        car_s[...] = jnp.zeros_like(car_s)
        car_p[...] = jnp.ones_like(car_p)

    xn = rms_low(tok[...].astype(f32), gain[...])
    xn_o[...] = xn
    y_o[...] = nt(xn, w_in[0])
    u_low = nt(xn, w_in[1]).astype(bf16)
    u_o[...] = u_low
    u_now = u_low.astype(f32)
    ubuf[HALO : HALO + rows, :] = u_now
    conv = vec[CONV : CONV + 1] + vec[0:1] * u_now
    for back in range(1, CONV):
        conv = conv + vec[back : back + 1] * mask[:, back : back + 1] * ubuf[
            HALO - back : HALO - back + rows, :
        ]
    ubuf[0:HALO, :] = u_now[rows - HALO :, :]
    conv_low = conv.astype(bf16)
    xc_o[...] = conv_low
    pre_decay = nn(conv_low, w_a[...]) + vec[CONV + 2 : CONV + 3]
    pre_input = nn(conv_low, w_i[...]) + vec[CONV + 3 : CONV + 4]
    pa_o[...] = pre_decay
    pi_o[...] = pre_input
    live = mask[:, 0:1]
    _, gate, raw, _, mult = gate_terms(pre_decay, pre_input, vec[CONV + 1 : CONV + 2], live)
    decay = raw * live
    a_o[...] = decay
    put_tiles(abuf, decay)
    put_tiles(bbuf, gate * conv_low.astype(f32) * mult)
    scan_tiles(abuf, bbuf, car_s, car_p, h_o, p_o, width, False)
    end_o[0:1, :] = car_s[0:1, :width]
    end_o[1:2, :] = car_p[0:1, :width]


def front(tok, halo, gain, weights, w_a, w_i, vec, mask, rows):
    count, model = tok.shape
    width = weights[0].shape[2]
    tiles = pl.cdiv(width, LANES)
    row = lambda size: pl.BlockSpec((rows, size), lambda i: (i, 0))
    like = lambda size, kind: jax.ShapeDtypeStruct((count, size), kind)
    return pl.pallas_call(
        front_kernel,
        grid=(count // rows,),
        in_specs=[
            row(model), whole(halo.shape), whole(gain.shape), *any_specs(),
            whole(w_a.shape), whole(w_i.shape), whole(vec.shape), row(mask.shape[1]),
        ],
        out_specs=[
            row(model), row(width), row(width), whole((HALO, width)), row(width), row(width),
            row(width), row(width), row(width), row(width), whole((8, width)),
        ],
        out_shape=[
            like(model, bf16), like(width, f32), like(width, bf16),
            jax.ShapeDtypeStruct((HALO, width), bf16), like(width, bf16), like(width, f32),
            like(width, f32), like(width, f32), like(width, f32), like(width, f32),
            jax.ShapeDtypeStruct((8, width), f32),
        ],
        scratch_shapes=[
            pltpu.VMEM((HALO + rows, width), f32),
            pltpu.VMEM((tiles, rows, LANES), f32),
            pltpu.VMEM((tiles, rows, LANES), f32),
            pltpu.VMEM((8, tiles * LANES), f32),
            pltpu.VMEM((8, tiles * LANES), f32),
            pltpu.VMEM((2, width, model), bf16),
            pltpu.SemaphoreType.DMA,
        ],
        compiler_params=params(),
        cost_estimate=cost(34),
        name="front",
    )(tok, halo, gain, *weights, w_a, w_i, vec, mask)


def state_kernel(
    rank, ends, h_l, p_l, y, h_o, hp_o, o_o, hin, hbuf
):
    step = pl.program_id(0)
    rows = h_l.shape[0]

    @pl.when(step == 0)
    def _():
        def fold(at, held):
            return jnp.where(at < rank[0], ends[at, 0:1, :] + ends[at, 1:2, :] * held, held)

        start = lax.fori_loop(0, ends.shape[0], fold, jnp.zeros((1, h_l.shape[1]), f32))
        hin[0:1, :] = start
        hbuf[7:8, :] = start

    state = h_l[...] + p_l[...] * hin[0:1, :]
    h_o[...] = state
    hbuf[8 : 8 + rows, :] = state
    hp_o[...] = hbuf[7 : 7 + rows, :]
    hbuf[7:8, :] = state[rows - 1 :, :]
    o_o[...] = (state * gelu_tanh(y[...])).astype(bf16)


def finish_state(rank, ends, h_l, p_l, y, rows):
    count, width = h_l.shape
    row = lambda size: pl.BlockSpec((rows, size), lambda i: (i, 0))
    like = lambda size, kind: jax.ShapeDtypeStruct((count, size), kind)
    return pl.pallas_call(
        state_kernel,
        grid=(count // rows,),
        in_specs=[
            pl.BlockSpec(memory_space=pltpu.SMEM), whole(ends.shape), row(width), row(width),
            row(width),
        ],
        out_specs=[row(width), row(width), row(width)],
        out_shape=[like(width, f32), like(width, f32), like(width, bf16)],
        scratch_shapes=[
            pltpu.VMEM((8, width), f32),
            pltpu.VMEM((8 + rows, width), f32),
        ],
        compiler_params=params(),
        cost_estimate=cost(8),
        name="finish_state",
    )(rank, ends, h_l, p_l, y)


def lift_kernel(slab, mixed, tok, gain, w_0, w_1, w_2, w_3, xn_o, own_o, w_o, sem):
    step = pl.program_id(0)

    @pl.when(step == 0)
    def _():
        load_pieces((w_0, w_1, w_2, w_3), range(w_o.shape[0]), w_o, sem, 2)

    total = nn(mixed[0], w_o[0])
    for kind in range(1, w_o.shape[0]):
        total = total + nn(mixed[kind], w_o[kind])
    second = tok[...].astype(f32) + total
    xn_o[...] = rms_low(second, gain[...])

    @pl.when(step == slab[0])
    def _():
        own_o[...] = second


def lift(slab, mixed, tok, gain, weights):
    count, model = tok.shape
    slabs, _, width = mixed.shape
    rows = count // slabs
    row = lambda size: pl.BlockSpec((rows, size), lambda i: (i, 0))
    return pl.pallas_call(
        lift_kernel,
        grid=(slabs,),
        in_specs=[
            pl.BlockSpec(memory_space=pltpu.SMEM),
            pl.BlockSpec((slabs, rows, width), lambda i: (0, i, 0)),
            row(model), whole(gain.shape), *any_specs(),
        ],
        out_specs=[row(model), whole((rows, model))],
        out_shape=[
            jax.ShapeDtypeStruct((count, model), bf16),
            jax.ShapeDtypeStruct((rows, model), f32),
        ],
        scratch_shapes=[pltpu.VMEM((slabs, width, model), bf16), pltpu.SemaphoreType.DMA],
        compiler_params=params(),
        cost_estimate=cost(22),
        name="lift",
    )(slab, mixed, tok, gain, *weights)


def mlp_kernel(xn, dhid, w_0, w_1, w_2, w_3, hm_o, dg_o, du_o, part_o, held, sem):
    @pl.when(pl.program_id(0) == 0)
    def _():
        load_pieces((w_0, w_1, w_2, w_3), (0, 1), held, sem, 1)

    w_g, w_u = held.at[0], held.at[1]
    hidden = dhid.shape[1]
    piece = hidden // 3
    for at in range(0, hidden, piece):
        cols = slice(at, at + piece)
        z_gate = nn(xn[...], w_g[:, cols])
        z_up = nn(xn[...], w_u[:, cols])
        d_hid = dhid[:, cols]
        act, slope = gelu_both(z_gate)
        hm_o[:, cols] = (act * z_up).astype(bf16)
        dg_o[:, cols] = (d_hid * z_up * slope).astype(bf16)
        du_o[:, cols] = (d_hid * act).astype(bf16)
    model = xn.shape[1]
    piece = model // 4
    for at in range(0, model, piece):
        cols = slice(at, at + piece)
        part_o[:, cols] = (nt(dg_o[...], w_g[cols, :]) + nt(du_o[...], w_u[cols, :])).astype(bf16)


def mlp(xn, dhid, weights, rows):
    count, model = xn.shape
    hidden = dhid.shape[1]
    row = lambda size: pl.BlockSpec((rows, size), lambda i: (i, 0))
    like = lambda size: jax.ShapeDtypeStruct((count, size), bf16)
    return pl.pallas_call(
        mlp_kernel,
        grid=(count // rows,),
        in_specs=[row(model), row(hidden), *any_specs()],
        out_specs=[row(hidden), row(hidden), row(hidden), row(model)],
        out_shape=[like(hidden), like(hidden), like(hidden), like(model)],
        scratch_shapes=[pltpu.VMEM((2, model, hidden), bf16), pltpu.SemaphoreType.DMA],
        compiler_params=params(),
        cost_estimate=cost(36),
        name="mlp",
    )(xn, dhid, *weights)


def back_kernel(
    slab, d_rec, w_0, w_1, w_2, w_3, y, h, a, dy_o, g_o, p_o, end_o, abuf, bbuf, car_s, car_p, w_o, sem
):
    step = pl.program_id(0)
    width = y.shape[1]

    @pl.when(step == 0)
    def _():
        load_pieces((w_0, w_1, w_2, w_3), (slab[0],), w_o, sem, 2)
        car_s[...] = jnp.zeros_like(car_s)
        car_p[...] = jnp.ones_like(car_p)

    d_mixed = nt(d_rec[...], w_o[0])
    act, slope = gelu_both(y[...])
    dy_o[...] = (d_mixed * h[...] * slope).astype(bf16)
    put_tiles(abuf, a[...])
    put_tiles(bbuf, d_mixed * act)
    scan_tiles(abuf, bbuf, car_s, car_p, g_o, p_o, width, True)
    end_o[0:1, :] = car_s[0:1, :width]
    end_o[1:2, :] = car_p[0:1, :width]


def back_scan(slab, d_rec, weights, y, h, a, rows):
    count, model = d_rec.shape
    width = y.shape[1]
    tiles = pl.cdiv(width, LANES)
    steps = count // rows
    row = lambda size: pl.BlockSpec((rows, size), lambda i: (steps - 1 - i, 0))
    like = lambda size, kind: jax.ShapeDtypeStruct((count, size), kind)
    return pl.pallas_call(
        back_kernel,
        grid=(steps,),
        in_specs=[
            pl.BlockSpec(memory_space=pltpu.SMEM), row(model), *any_specs(), row(width), row(width),
            row(width),
        ],
        out_specs=[row(width), row(width), row(width), whole((8, width))],
        out_shape=[
            like(width, bf16), like(width, f32), like(width, f32),
            jax.ShapeDtypeStruct((8, width), f32),
        ],
        scratch_shapes=[
            pltpu.VMEM((tiles, rows, LANES), f32),
            pltpu.VMEM((tiles, rows, LANES), f32),
            pltpu.VMEM((8, tiles * LANES), f32),
            pltpu.VMEM((8, tiles * LANES), f32),
            pltpu.VMEM((1, width, model), bf16),
            pltpu.SemaphoreType.DMA,
        ],
        compiler_params=params(),
        cost_estimate=cost(20),
        name="back_scan",
    )(slab, d_rec, *weights, y, h, a)


def gates_kernel(
    rank, ends, g_l, p_l, pa, pi, xc, hp, u, u_prev, u_halo, mask, w_a, w_i, vec,
    dpa_o, dpi_o, du_o, tail_o, spill_o, sum_o,
    qin, dbuf, ubuf,
):
    step = pl.program_id(0)
    steps = pl.num_programs(0)
    rows, width = g_l.shape

    @pl.when(step == 0)
    def _():
        count = ends.shape[0]

        def fold(back, held):
            at = count - 1 - back
            return jnp.where(at > rank[0], ends[at, 0:1, :] + ends[at, 1:2, :] * held, held)

        qin[0:1, :] = lax.fori_loop(0, count, fold, jnp.zeros((1, width), f32))
        sum_o[...] = jnp.zeros_like(sum_o)
        dbuf[rows : rows + 8, :] = jnp.zeros((8, width), f32)

    grad = g_l[...] + p_l[...] * qin[0:1, :]
    live = mask[:, 0:1]
    slope = vec[CONV + 1 : CONV + 2]
    rate, gate, raw, root, mult = gate_terms(pa[...], pi[...], slope, live)
    conv = xc[...].astype(f32)
    d_mult = grad * gate * conv
    d_log = live * (grad * hp[...] * raw - d_mult * (raw * raw) / root)
    d_log_rate = d_log * rate
    d_conv = grad * gate * mult
    d_pa = (d_log_rate * slope * (1.0 - rate)).astype(bf16)
    d_pi = (grad * mult * conv * gate * (1.0 - gate)).astype(bf16)
    dpa_o[...] = d_pa
    dpi_o[...] = d_pi
    d_conv = d_conv + nt(d_pa, w_a[...]) + nt(d_pi, w_i[...])
    total = lambda value: jnp.sum(value, axis=0, keepdims=True)
    u_now = u[...].astype(f32)
    before = jnp.where(step == steps - 1, u_halo[...], u_prev[...]).astype(f32)
    ubuf[0:HALO, :] = before
    ubuf[HALO : HALO + rows, :] = u_now
    dbuf[0:rows, :] = d_conv
    sum_o[0:1, :] += total(d_conv * u_now)
    d_u = vec[0:1] * d_conv
    for back in range(1, CONV):
        sum_o[back : back + 1, :] += total(
            d_conv * mask[:, back : back + 1] * ubuf[HALO - back : HALO - back + rows, :]
        )
        d_u = d_u + vec[back : back + 1] * mask[:, CONV - 1 + back : CONV + back] * dbuf[
            back : back + rows, :
        ]
    sum_o[CONV : CONV + 1, :] += total(d_conv)
    sum_o[CONV + 1 : CONV + 2, :] += total(d_log_rate)
    sum_o[CONV + 2 : CONV + 3, :] += total(d_pa.astype(f32))
    sum_o[CONV + 3 : CONV + 4, :] += total(d_pi.astype(f32))
    du_o[...] = d_u.astype(bf16)

    @pl.when(step == 0)
    def _():
        tail_o[...] = d_u[rows - HALO :, :]

    head = d_conv[0:8, :]
    dbuf[rows : rows + 8, :] = head

    @pl.when(step == steps - 1)
    def _():
        spill_o[...] = jnp.zeros_like(spill_o)
        for ahead in range(CONV - 1, 0, -1):
            row = 0.0
            for back in range(ahead, CONV):
                at = back - ahead
                row = row + vec[back : back + 1] * mask[at : at + 1, back : back + 1] * d_conv[
                    at : at + 1, :
                ]
            spill_o[HALO - ahead : HALO - ahead + 1, :] = row


def gates_back(rank, ends, g_l, p_l, pa, pi, xc, hp, u, u_halo, mask, w_a, w_i, vec, rows):
    count, width = g_l.shape
    steps = count // rows
    at = lambda i: steps - 1 - i
    row = lambda size: pl.BlockSpec((rows, size), lambda i: (at(i), 0))
    like = lambda size, kind: jax.ShapeDtypeStruct((count, size), kind)
    per = rows // HALO
    return pl.pallas_call(
        gates_kernel,
        grid=(steps,),
        in_specs=[
            pl.BlockSpec(memory_space=pltpu.SMEM), whole(ends.shape), row(width), row(width),
            row(width), row(width), row(width), row(width), row(width),
            pl.BlockSpec((HALO, width), lambda i: (jnp.maximum(at(i) * per - 1, 0), 0)),
            whole(u_halo.shape), row(mask.shape[1]), whole(w_a.shape), whole(w_i.shape),
            whole(vec.shape),
        ],
        out_specs=[
            row(width), row(width), row(width), whole((HALO, width)), whole((HALO, width)),
            whole((8, width)),
        ],
        out_shape=[
            like(width, bf16), like(width, bf16), like(width, bf16),
            jax.ShapeDtypeStruct((HALO, width), f32), jax.ShapeDtypeStruct((HALO, width), f32),
            jax.ShapeDtypeStruct((8, width), f32),
        ],
        scratch_shapes=[
            pltpu.VMEM((8, width), f32),
            pltpu.VMEM((rows + 8, width), f32),
            pltpu.VMEM((HALO + rows, width), f32),
        ],
        compiler_params=params(),
        cost_estimate=cost(19),
        name="gates_back",
    )(rank, ends, g_l, p_l, pa, pi, xc, hp, u, u, u_halo, mask, w_a, w_i, vec)


def pair_kernel(left, right, tail, more, w_0, w_1, w_2, w_3, out, right_o, held, sem):
    step = pl.program_id(0)
    rows = left.shape[0]

    @pl.when(step == 0)
    def _():
        load_pieces((w_0, w_1, w_2, w_3), (0, 1), held, sem, 2)

    right_o[...] = right[...]

    @pl.when(step == pl.num_programs(0) - 1)
    def _():
        right_o[rows - HALO :, :] = (tail[...] + more[...]).astype(bf16)

    out[...] = (nn(left[...], held[0]) + nn(right_o[...], held[1])).astype(bf16)


def pair_back(left, right, tail, more, weights, model, rows):
    count, width = left.shape
    row = lambda size: pl.BlockSpec((rows, size), lambda i: (i, 0))
    return pl.pallas_call(
        pair_kernel,
        grid=(count // rows,),
        in_specs=[
            row(width), row(width), whole(tail.shape), whole(more.shape), *any_specs(),
        ],
        out_specs=[row(model), row(width)],
        out_shape=[
            jax.ShapeDtypeStruct((count, model), bf16),
            jax.ShapeDtypeStruct((count, width), bf16),
        ],
        scratch_shapes=[pltpu.VMEM((2, width, model), bf16), pltpu.SemaphoreType.DMA],
        compiler_params=params(),
        cost_estimate=cost(12),
        name="pair_back",
    )(left, right, tail, more, *weights)


def mask_kernel(ids, out):
    rows = out.shape[0]
    now = ids[HALO : HALO + rows, :]
    same = lambda by: (now == ids[HALO + by : HALO + by + rows, :]).astype(f32)
    out[...] = jnp.zeros_like(out)
    out[:, 0:1] = same(-1)
    for back in range(1, CONV):
        out[:, back : back + 1] = same(-back)
        out[:, CONV - 1 + back : CONV + back] = same(back)


def masks(ids, count):
    return pl.pallas_call(
        mask_kernel,
        out_shape=jax.ShapeDtypeStruct((count, 8), f32),
        compiler_params=pltpu.CompilerParams(vmem_limit_bytes=16 * 1024 * 1024),
        cost_estimate=cost(2),
        name="masks",
    )(ids)


def moments_step(first, second, grad):
    new_first = beta_first * first + (1.0 - beta_first) * grad
    new_second = beta_second * second + (1.0 - beta_second) * grad * grad
    normal = (
        new_first
        * (1.0 / (1.0 - beta_first**STEP))
        / (jnp.sqrt(new_second * (1.0 / (1.0 - beta_second**STEP))) + adam_eps)
    )
    return new_first, new_second, normal


def soap_tiles(turned, tile_rows, tile_cols, w, m, v, bases, nm, nv, nw):
    side = lax.broadcasted_iota(jnp.int32, (TILE, 2 * TILE), 1) < TILE
    square = (lax.broadcasted_iota(jnp.int32, (2 * TILE, 2 * TILE), 0) < TILE) == (
        lax.broadcasted_iota(jnp.int32, (2 * TILE, 2 * TILE), 1) < TILE
    )
    for i in range(tile_rows):
        for j in range(0, tile_cols, 2):
            rows = slice(i * TILE, (i + 1) * TILE)
            cols = slice(j * TILE, (j + 2) * TILE)
            left_a, right_a = bases(i, j)
            left_b, right_b = bases(i, j + 1)
            lefts = [left_a.astype(bf16), left_b.astype(bf16)]
            both = jnp.concatenate([right_a, right_b], axis=0)
            right = jnp.where(square, jnp.concatenate([both, both], axis=1), 0.0).astype(bf16)
            choose = lambda parts: jnp.where(side, parts[0], parts[1])
            inner = choose([turned(rows, cols, left) for left in lefts]).astype(bf16)
            grad = nn(inner, right)
            new_first, new_second, normal = moments_step(m[rows, cols], v[rows, cols], grad)
            nm[rows, cols] = new_first
            nv[rows, cols] = new_second
            low = normal.astype(bf16)
            outer = choose([nn(left, low) for left in lefts]).astype(bf16)
            master = w[rows, cols]
            nw[rows, cols] = master - learn_rate * (nt(outer, right) + decay_rate * master)


def soap_kernel(turned, swapped, w, m, v, g, q, nm, nv, nw):
    def plain(rows, cols, left):
        return tn(left, g[0, rows, cols])

    def across(rows, cols, left):
        return lax.dot_general(
            left, g[0, cols, rows], (((0,), (1,)), ((), ())), preferred_element_type=f32
        )

    if swapped:
        bases = lambda i, j: (q[0, j, i, 1], q[0, j, i, 0])
    else:
        bases = lambda i, j: (q[0, i, j, 0], q[0, i, j, 1])
    soap_tiles(
        across if turned else plain, w.shape[1] // TILE, w.shape[2] // TILE,
        w.at[0], m.at[0], v.at[0], bases, nm.at[0], nv.at[0], nw.at[0],
    )


def soap(w, m, v, g, q, rows, turned=False, swapped=False):
    group, height, width = w.shape
    if width < 2 * TILE:
        q = jnp.concatenate([q, q], axis=1 if swapped else 2)
        padded = [jnp.concatenate([array, array], axis=2) for array in (w, m, v)]
        g = jnp.concatenate([g, g], axis=1 if turned else 2)
        results = soap(*padded, g, q, rows, turned, swapped)
        return [array[:, :, :width] for array in results]
    row = pl.BlockSpec((1, rows, width), lambda n, i: (n, i, 0))
    out = jax.ShapeDtypeStruct(w.shape, f32)
    if swapped:
        q_block = (1, width // TILE, rows // TILE, 2, TILE, TILE)
        q_at = lambda n, i: (n, 0, i, 0, 0, 0)
    else:
        q_block = (1, rows // TILE, width // TILE, 2, TILE, TILE)
        q_at = lambda n, i: (n, i, 0, 0, 0, 0)
    return pl.pallas_call(
        functools.partial(soap_kernel, turned, swapped),
        grid=(group, height // rows),
        in_specs=[row] * 3
        + [
            pl.BlockSpec((1, width, rows), lambda n, i: (n, 0, i)) if turned else row,
            pl.BlockSpec(q_block, q_at),
        ],
        out_specs=[row] * 3,
        out_shape=[out] * 3,
        compiler_params=pltpu.CompilerParams(
            dimension_semantics=("arbitrary", "arbitrary"), vmem_limit_bytes=56 * 1024 * 1024
        ),
        cost_estimate=cost(group * height * width / 24000),
        name="soap",
    )(w, m, v, g, q)


def reorder(array, dim, order):
    shape = array.shape
    parts = order.shape[0]
    reshaped = array.reshape(shape[:dim] + (parts, shape[dim] // parts) + shape[dim + 1 :])
    return jnp.take(reshaped, order, axis=dim, mode="clip").reshape(shape)


def gather_slabs(array):
    return lax.all_gather(array, "mlp", axis=0, tiled=True)


def scatter_slabs(array):
    return lax.psum_scatter(array, "mlp", scatter_dimension=0, tiled=True)


def hop(array, pairs):
    count = lax.axis_size("tok")
    return lax.ppermute(array, "tok", [(i, i ^ pairs[i % 2]) for i in range(count)])


CORE, NEAR, FAR = (1, 1), (2, 4), (4, 2)


def stored_order(parts, rank):
    indices = jnp.arange(parts, dtype=jnp.int32)
    if parts != 8:
        return indices, indices
    near, far = indices // 2 % 2, indices % 2
    spots = rank ^ (
        indices // 4 + jnp.where(rank % 2 == 0, near * 2 + far * 4, near * 4 + far * 2)
    )
    return spots, invert(spots)


def invert(order):
    indices = jnp.arange(order.shape[0], dtype=jnp.int32)
    return jnp.sum(jnp.where(order[None, :] == indices[:, None], indices[None, :], 0), axis=1)


def gather_start(own):
    two = jnp.concatenate([own, hop(own, FAR)], axis=0)
    return jnp.concatenate([two, hop(two, NEAR)], axis=0)


class Sums:
    def __init__(self, keep, send, dim):
        self.keep, self.send, self.dim = keep, send, dim
        self.whole = lax.axis_size("tok") != 8

    def cut(self, array, blocks, at):
        size = array.shape[self.dim] // blocks
        return lax.slice_in_dim(array, at * size, (at + 1) * size, axis=self.dim).astype(f32)

    def mixed(self, at, there):
        return self.cut(self.keep, 4, at) + self.cut(self.got, 4, there)

    def first(self, *before):
        if self.whole:
            return self.send
        self.got = hop(self.send, CORE)
        self.near_send = after(
            jnp.concatenate([self.mixed(2, 1), self.mixed(3, 3)], axis=self.dim).astype(
                self.send.dtype
            ),
            *before,
        )
        return self.near_send

    def second(self, *before):
        if self.whole:
            return self.send
        self.near = hop(self.near_send, NEAR)
        self.far_send = after(
            (self.mixed(1, 2) + self.cut(self.near, 2, 1)).astype(self.send.dtype), *before
        )
        return self.far_send

    def third(self):
        if self.whole:
            both = jnp.concatenate([self.keep.astype(self.send.dtype), self.send], axis=self.dim)
            return lax.psum_scatter(both, "tok", scatter_dimension=self.dim, tiled=True)
        far = hop(self.far_send, FAR)
        return self.mixed(0, 0) + self.cut(self.near, 2, 0) + far.astype(f32)


def sums_of(array):
    half = array.shape[0] // 2
    sums = Sums(array[:half], array[half:], 0)
    sums.first()
    sums.second()
    return sums.third()


def halves(array):
    half = array.shape[1] // 2
    return array[:, :half], array[:, half:]


def grad_rows(left, right):
    keep, send = halves(left)
    return Sums(tn(keep, right), tn(send, right).astype(bf16), 0)


def grad_columns(left, right):
    keep, send = halves(right)
    return Sums(tn(left, keep), tn(left, send).astype(bf16), 1)


def permute_kernel(order, array, out):
    parts = order.shape[0]
    size = array.shape[1] // parts
    for part in range(parts):
        at = pl.multiple_of(order[part] * size, LANES)
        out[:, part * size : (part + 1) * size] = array[:, pl.ds(at, size)]


def permute_columns(array, order):
    parts = order.shape[0]
    count, width = array.shape
    if width // parts % LANES:
        return reorder(array, 1, order)
    rows = min(256, count)
    row = pl.BlockSpec((rows, width), lambda i: (i, 0))
    return pl.pallas_call(
        permute_kernel,
        grid=(count // rows,),
        in_specs=[pl.BlockSpec(memory_space=pltpu.SMEM), row],
        out_specs=row,
        out_shape=jax.ShapeDtypeStruct(array.shape, array.dtype),
        compiler_params=params(),
        cost_estimate=cost(count * width / 420000),
        name="permute_columns",
    )(order, array)


def settle_kernel(move, order, value, upstream, gain, base, total_o, low_o, sum_o, hold):
    @pl.when(pl.program_id(0) == 0)
    def _():
        sum_o[...] = jnp.zeros_like(sum_o)

    held = value[...].astype(f32)
    grad = upstream[...].astype(f32)
    scale = lax.rsqrt(jnp.mean(held * held, axis=-1, keepdims=True) + norm_eps)
    weighted = grad * gain[...]
    inner = jnp.mean(held * weighted, axis=-1, keepdims=True)
    total = base[...].astype(f32) + (scale * weighted - held * (scale * scale * scale * inner))
    sum_o[0:1, :] += jnp.sum(grad * held * scale, axis=0, keepdims=True)
    total_o[...] = total
    low = total.astype(bf16)
    if not move:
        low_o[...] = low
        return
    hold[...] = low
    parts = order.shape[0]
    size = low.shape[1] // parts
    for part in range(parts):
        at = pl.multiple_of(order[part] * size, LANES)
        low_o[:, part * size : (part + 1) * size] = hold[:, pl.ds(at, size)]


def settle(value, upstream, gain, base, order, move):
    count, model = value.shape
    inside = move and (model // order.shape[0]) % LANES == 0
    rows = min(128, count)
    row = pl.BlockSpec((rows, model), lambda i: (i, 0))
    total, low, sums = pl.pallas_call(
        functools.partial(settle_kernel, inside),
        grid=(count // rows,),
        in_specs=[pl.BlockSpec(memory_space=pltpu.SMEM), row, row, whole(gain.shape), row],
        out_specs=[row, row, whole((8, model))],
        out_shape=[
            jax.ShapeDtypeStruct((count, model), f32),
            jax.ShapeDtypeStruct((count, model), bf16),
            jax.ShapeDtypeStruct((8, model), f32),
        ],
        scratch_shapes=[pltpu.VMEM((rows, model), bf16)],
        compiler_params=params(),
        cost_estimate=cost(4),
        name="settle",
    )(order, value, upstream, gain, base)
    if move and not inside:
        low = reorder(low, 1, order)
    return total, low, sums[0]


def after(array, *others):
    return lax.optimization_barrier((array,) + others)[0]


def block_diagonal(blocks):
    count, width, _ = blocks.shape
    return jnp.concatenate(
        [
            jnp.pad(blocks[n], ((0, 0), (n * width, (count - 1 - n) * width)))
            for n in range(count)
        ],
        axis=0,
    )


def diagonal_blocks(array, count):
    width = array.shape[0] // count
    return jnp.stack(
        [array[n * width : (n + 1) * width, n * width : (n + 1) * width] for n in range(count)]
    )


def on_device(
    tokens, segment_ids, owner_table, cotangent,
    w_in_rec, m_in_rec, v_in_rec, q_in_rec,
    w_out_rec, m_out_rec, v_out_rec, q_out_rec,
    w_in_mlp, m_in_mlp, v_in_mlp, q_in_mlp,
    w_out_mlp, m_out_mlp, v_out_mlp, q_out_mlp,
    w_gates, m_gates, v_gates, w_rnn, m_rnn, v_rnn, w_gains, m_gains, v_gains,
):
    parts = lax.axis_size("tok")
    rank = lax.axis_index("tok")
    slabs = lax.axis_size("mlp")
    slab = lax.axis_index("mlp")
    count, model = tokens.shape
    length = count * parts
    share = count // slabs
    rows = min(256, count)
    spots, places = stored_order(parts, rank)
    into_local = jnp.take(invert(owner_table), spots, mode="clip")
    from_local = jnp.take(places, owner_table, mode="clip")
    rank_ref = rank.reshape(1).astype(jnp.int32)

    blocks = w_gates.shape[1]
    gate_part = w_gates.shape[2]
    lead = 2 * blocks
    rnn_part = w_rnn.shape[1]
    small = jnp.concatenate(
        [w_gates.reshape(lead, gate_part), w_rnn, w_gains.reshape(lead, -1)], axis=1
    ).astype(bf16)
    if parts == 8:
        small_four = gather_start(small[None])
        small_rest = hop(small_four, CORE)
        small_all = jnp.concatenate(
            [small_four] + [small_rest[p : p + 1] for p in (0, 2, 1, 3)], axis=0
        )
    else:
        small_all = lax.all_gather(small, "tok", axis=0, tiled=False)
    turn = lambda array: jnp.swapaxes(array, 1, 2)
    rec_own = turn(w_in_rec).astype(bf16)[None]
    join = lambda *arrays: jnp.concatenate(arrays, axis=0)
    out_own = lax.all_gather(w_out_rec.astype(bf16), "mlp", axis=0, tiled=False)[None]
    if parts == 8:
        rec_two = join(rec_own, hop(rec_own, FAR))
        rec_near = hop(rec_two, NEAR)
        rec_core = hop(rec_two, CORE)
    gains_all = small_all[:, :, gate_part + rnn_part :].reshape(parts, 2, model // parts)
    gains_f = (
        gains_all
        .transpose(1, 0, 2)
        .reshape(2, model)
        .astype(f32)
    )
    ordered = jnp.take(small_all[:, :, : gate_part + rnn_part], from_local, axis=0, mode="clip")
    gate_mats = ordered[:, :, :gate_part].transpose(1, 0, 2).reshape(2, blocks, BW, BW)
    w_a = block_diagonal(gate_mats[0])
    w_i = block_diagonal(gate_mats[1])
    rnn_f = ordered[:, :, gate_part:].transpose(1, 0, 2).reshape(lead, -1).astype(f32)
    lam = rnn_f[CONV + 1]
    vec = rnn_f.at[CONV + 1].set(-8.0 * jax.nn.softplus(lam))

    tok_s = permute_columns(tokens, into_local)
    cot_s = permute_columns(cotangent, into_local)
    forward_pairs = [(i, i + 1) for i in range(parts - 1)]
    rim = lax.ppermute(tokens[count - HALO :], "tok", forward_pairs)
    halo = permute_columns(rim, into_local)
    rim_ids = lax.ppermute(segment_ids[count - HALO :], "tok", forward_pairs)
    ids = jnp.concatenate(
        [
            jnp.where(rank == 0, -1, rim_ids).astype(f32),
            segment_ids.astype(f32),
            jnp.full((HALO,), -1.0, f32),
        ]
    )
    mask = masks(ids[:, None], count)
    if parts == 8:
        rec_near = after(rec_near, tok_s, halo, mask, w_a, w_i, vec)
        rec_w = (rec_two, rec_near, rec_core, hop(rec_near, CORE))
        up_own = w_in_mlp.astype(bf16)[None]
        out_far = hop(after(out_own, rec_near), FAR)
        up_far = hop(after(up_own, rec_near), FAR)
    else:
        rec_w = (lax.all_gather(rec_own[0], "tok", axis=2, tiled=True)[None],) * 4
        out_w = (lax.all_gather(out_own[0], "tok", axis=2, tiled=True)[None],) * 4

    xn_one, y_pre, u_low, u_halo, conv_low, pre_decay, pre_input, decay, h_loc, p_loc, ends = front(
        tok_s, halo, gains_f[0:1], rec_w, w_a, w_i, vec, mask, rows
    )
    ends_all = lax.all_gather(ends[0:2], "tok", axis=0, tiled=False)
    state, state_prev, mixed = finish_state(rank_ref, ends_all, h_loc, p_loc, y_pre, rows)
    own = lambda array: lax.dynamic_slice_in_dim(array, slab * share, share, 0)
    slab_ref = slab.reshape(1).astype(jnp.int32)
    own_tok = own(tok_s)
    mixed_all = lax.all_gather(mixed, "mlp", axis=0, tiled=False)
    down_own = w_out_mlp.astype(bf16)[None]
    if parts == 8:
        out_two = join(out_own, after(out_far, ends))
        up_two = join(up_own, after(up_far, ends))
        out_near = hop(out_two, NEAR)
        up_near = hop(up_two, NEAR)
        down_far = hop(after(down_own, ends), FAR)
        out_core = hop(after(out_two, mixed), CORE)
        out_w = (out_two, out_near, out_core, hop(after(out_near, mixed), CORE))
        down_two = join(down_own, after(down_far, mixed))
        down_near = hop(down_two, NEAR)
        down_core = hop(down_two, CORE)
        up_core = hop(after(up_two, mixed), CORE)
        up_w = (up_two, up_near, up_core, hop(after(up_near, mixed), CORE))
        down_last = hop(down_near, CORE)
        down = jnp.concatenate(
            [
                down_two[0], down_two[1], down_near[0], down_near[1],
                down_core[0], down_last[0], down_core[1], down_last[1],
            ],
            axis=1,
        )
    else:
        down = lax.all_gather(down_own[0], "tok", axis=1, tiled=True)
        up_own = w_in_mlp.astype(bf16)
        up_w = (lax.all_gather(up_own, "tok", axis=1, tiled=True)[None],) * 4
    cot_s = permute_columns(after(cotangent, mixed), into_local)
    d_hidden = nt(cot_s, down)
    xn_two, second = lift(slab_ref, mixed_all, tok_s, gains_f[1:2], out_w)
    hidden, d_gate, d_up, d_branch = mlp(xn_two, d_hidden, up_w, min(512, count))
    d_xn_two = scatter_slabs(d_branch)
    low = lambda array: array.astype(bf16)
    sum_gate = grad_rows(xn_two, d_gate)
    sum_up = grad_rows(xn_two, d_up)
    sum_down = grad_rows(cot_s, hidden)
    branch_two = nn(hidden, down).astype(bf16)
    d_xn_two = after(
        d_xn_two, sum_gate.first(), sum_up.first(), sum_down.first(), branch_two
    )
    sum_gate.second()
    sum_up.second()
    sum_down.second()
    g_in_mlp = jnp.stack([low(sum_gate.third()), low(sum_up.third())])
    g_out_mlp = low(sum_down.third())

    lead_one = lambda *arrays: [array[None] for array in arrays]
    split = lambda height: max(
        n for n in range(2 * TILE, height + 1, 2 * TILE) if height % n == 0 and n <= 512
    )
    in_mlp_new = soap(w_in_mlp, m_in_mlp, v_in_mlp, g_in_mlp, q_in_mlp, TILE)

    d_second, d_second_low, g_gain_two = settle(
        second, d_xn_two, gains_f[1:2], own(cot_s), from_local, False
    )
    d_rec = gather_slabs(d_second_low)
    branch_two = after(branch_two, in_mlp_new[0])
    d_rec = after(d_rec, in_mlp_new[0])
    branch_sum = scatter_slabs(branch_two)
    result_own = second + branch_sum.astype(f32)
    result_low = permute_columns(result_own.astype(bf16), from_local)
    d_ypre, g_loc, q_loc, ends_back = back_scan(slab_ref, d_rec, out_w, y_pre, state, decay, rows)
    ends_back_all = lax.all_gather(ends_back[0:2], "tok", axis=0, tiled=False)
    d_pa, d_pi, d_u, d_u_tail, spill, sums = gates_back(
        rank_ref, ends_back_all, g_loc, q_loc, pre_decay, pre_input, conv_low, state_prev,
        u_low, u_halo, mask, w_a, w_i, vec, rows,
    )
    from_next = lax.ppermute(spill, "tok", [(i + 1, i) for i in range(parts - 1)])
    d_pair, d_u = pair_back(d_ypre, d_u, d_u_tail, from_next, rec_w, model, rows)
    d_xn_one = scatter_slabs(after(d_pair, branch_sum))
    out_mlp_new = soap(
        *lead_one(w_out_mlp, m_out_mlp, v_out_mlp, after(g_out_mlp, d_pair), q_out_mlp),
        split(w_out_mlp.shape[0]), turned=True,
    )
    d_rec, mixed, xn_one, d_ypre, d_u, d_pa, d_pi, conv_low = lax.optimization_barrier(
        (d_rec, mixed, xn_one, d_ypre, d_u, d_pa, d_pi, conv_low, d_pair)
    )[:8]
    sum_out = grad_columns(mixed, d_rec)
    sum_y = grad_columns(d_ypre, xn_one)
    sum_u = grad_columns(d_u, xn_one)
    d_xn_one = after(
        d_xn_one, sum_out.first(), sum_y.first(), sum_u.first(), out_mlp_new[0]
    )
    _, d_input_low, g_gain_one = settle(
        own_tok, d_xn_one, gains_f[0:1], d_second, from_local, True
    )
    d_input = gather_slabs(d_input_low)
    sum_out.second()
    sum_y.second()
    sum_u.second()
    g_out_rec = low(sum_out.third())
    g_in_rec = jnp.stack([low(sum_y.third()), low(sum_u.third())])
    result = gather_slabs(after(result_low, d_input_low))

    g_gates = jnp.stack(
        [
            diagonal_blocks(tn(conv_low, d_pa), blocks),
            diagonal_blocks(tn(conv_low, d_pi), blocks),
        ]
    )
    g_rnn = sums.at[CONV + 1].multiply(-8.0 * jax.nn.sigmoid(lam))
    g_small = jnp.concatenate(
        [g_gates.reshape(lead, parts, gate_part), g_rnn.reshape(lead, parts, rnn_part)], axis=2
    ).transpose(1, 0, 2)
    g_small = jnp.take(g_small, into_local, axis=0, mode="clip")
    sum_small = sums_of(g_small)[0]
    sum_gates = sum_small[:, :gate_part].reshape(w_gates.shape)
    sum_rnn = sum_small[:, gate_part:]
    g_gains = jnp.stack([g_gain_one, g_gain_two]).reshape(2, parts, -1).transpose(1, 0, 2)
    sum_gains = lax.psum(sums_of(g_gains)[0], "mlp")

    out_rec_new = soap(
        *lead_one(w_out_rec, m_out_rec, v_out_rec, g_out_rec, q_out_rec), w_out_rec.shape[0]
    )
    in_rec_new = soap(
        turn(w_in_rec), turn(m_in_rec), turn(v_in_rec), g_in_rec, q_in_rec, w_in_rec.shape[2],
        swapped=True,
    )
    out_mlp_new = [array[0] for array in out_mlp_new]
    out_rec_new = [array[0] for array in out_rec_new]
    in_rec_new = [turn(array) for array in in_rec_new]
    gates_m, gates_v, gates_n = moments_step(m_gates, v_gates, sum_gates)
    gates_w = w_gates - learn_rate * (gates_n + decay_rate * w_gates)
    rnn_m, rnn_v, _ = moments_step(m_rnn, v_rnn, sum_rnn)
    gains_m, gains_v, _ = moments_step(m_gains, v_gains, sum_gains)
    d_input = after(
        d_input, in_rec_new[0], out_rec_new[0], gates_w, rnn_m
    ).astype(f32)
    return (
        result, d_input,
        in_rec_new[0], in_rec_new[1], in_rec_new[2],
        out_rec_new[0], out_rec_new[1], out_rec_new[2],
        in_mlp_new[0], in_mlp_new[1], in_mlp_new[2],
        out_mlp_new[0], out_mlp_new[1], out_mlp_new[2],
        gates_m, gates_v, gates_w, rnn_m, rnn_v, gains_m, gains_v,
    )


def solution(mesh):
    in_specs = (
        P("tok", None),
        P("tok"),
        P(),
        P("tok", None),
        P(None, "tok", "mlp"),
        P(None, "tok", "mlp"),
        P(None, "tok", "mlp"),
        P(None, "tok", "mlp", None, None, None),
        P("mlp", "tok"),
        P("mlp", "tok"),
        P("mlp", "tok"),
        P("mlp", "tok", None, None, None),
        P(None, "tok", "mlp"),
        P(None, "tok", "mlp"),
        P(None, "tok", "mlp"),
        P(None, "tok", "mlp", None, None, None),
        P("mlp", "tok"),
        P("mlp", "tok"),
        P("mlp", "tok"),
        P("mlp", "tok", None, None, None),
        P(None, "mlp", "tok"),
        P(None, "mlp", "tok"),
        P(None, "mlp", "tok"),
        P(None, ("mlp", "tok")),
        P(None, ("mlp", "tok")),
        P(None, ("mlp", "tok")),
        P(None, "tok"),
        P(None, "tok"),
        P(None, "tok"),
    )
    out_specs = (
        P("tok", None),
        P("tok", None),
        P(None, "tok", "mlp"),
        P(None, "tok", "mlp"),
        P(None, "tok", "mlp"),
        P("mlp", "tok"),
        P("mlp", "tok"),
        P("mlp", "tok"),
        P(None, "tok", "mlp"),
        P(None, "tok", "mlp"),
        P(None, "tok", "mlp"),
        P("mlp", "tok"),
        P("mlp", "tok"),
        P("mlp", "tok"),
        P(None, "mlp", "tok"),
        P(None, "mlp", "tok"),
        P(None, "mlp", "tok"),
        P(None, ("mlp", "tok")),
        P(None, ("mlp", "tok")),
        P(None, "tok"),
        P(None, "tok"),
    )
    return jax.shard_map(
        on_device, mesh=mesh, in_specs=in_specs, out_specs=out_specs, check_vma=False
    )
```

```python
import functools

import jax
import jax.numpy as jnp
from jax import lax
from jax.experimental import pallas as pl
from jax.experimental.pallas import tpu as pltpu
from jax.sharding import PartitionSpec as P

BW = 176
CONV = 4
TILE = 64
STEP = 7
HALO = 16
LANES = 128

norm_eps = 1e-06
learn_rate = 0.02
beta_first = 0.9
beta_second = 0.999
adam_eps = 1e-08
decay_rate = 0.1

f32 = jnp.float32
bf16 = jnp.bfloat16


def params(limit=56):
    return pltpu.CompilerParams(
        dimension_semantics=("arbitrary",), vmem_limit_bytes=limit * 1024 * 1024
    )


def cost(micros):
    return pl.CostEstimate(
        flops=int(micros * 1.1e9), bytes_accessed=int(micros * 3.3e6), transcendentals=0
    )


def whole(shape):
    return pl.BlockSpec(shape, lambda *_: (0,) * len(shape), pipeline_mode=pl.Buffered(1))


def nn(left, right):
    return lax.dot_general(left, right, (((1,), (0,)), ((), ())), preferred_element_type=f32)


def nt(left, right):
    return lax.dot_general(left, right, (((1,), (1,)), ((), ())), preferred_element_type=f32)


def tn(left, right):
    return lax.dot_general(left, right, (((0,), (0,)), ((), ())), preferred_element_type=f32)


def gelu_both(value):
    square = value * value
    bent = jnp.tanh(0.7978845608028654 * (value + 0.044715 * value * square))
    half = 0.5 * (1.0 + bent)
    slope = half + (0.5 * 0.7978845608028654) * value * (1.0 - bent * bent) * (
        1.0 + (3.0 * 0.044715) * square
    )
    return value * half, slope


def gelu_tanh(value):
    return (
        0.5
        * value
        * (1.0 + jnp.tanh(0.7978845608028654 * (value + 0.044715 * value * value * value)))
    )


def one_less_square(log_value, value):
    twice = 2.0 * log_value
    series = 1.0 + twice * (1.0 / 6.0)
    for order in range(5, 1, -1):
        series = 1.0 + twice * series * (1.0 / order)
    return jnp.where(twice > -0.0625, -twice * series, 1.0 - value * value)


def gate_terms(pre_decay, pre_input, slope, live):
    rate = 0.5 + 0.5 * jnp.tanh(0.5 * pre_decay)
    gate = 0.5 + 0.5 * jnp.tanh(0.5 * pre_input)
    log_decay = slope * rate
    raw = jnp.exp(log_decay)
    root = jnp.sqrt(one_less_square(log_decay, raw))
    mult = (1.0 - live) + live * root
    return rate, gate, raw, root, mult


def put_tiles(buffer, value):
    width = value.shape[1]
    span = value.shape[0] // 8
    for tile in range(pl.cdiv(width, LANES)):
        size = min(LANES, width - tile * LANES)
        for chunk in range(8):
            at = chunk * (span + 1)
            buffer[tile, at : at + span, :size] = value[
                chunk * span : (chunk + 1) * span, tile * LANES : tile * LANES + size
            ]


def scan_tiles(first, second, carry_state, carry_prod, out_state, out_prod, width, backward):
    tiles, rows, _ = first.shape
    span = rows // 8 - 1

    def body(step, held):
        row = (span - 1 - step) if backward else step
        at = pl.ds(row, 8, stride=span + 1)
        states, prods = [], []
        for tile in range(tiles):
            state, prod = held[0][tile], held[1][tile]
            decay = first[tile, at, :]
            drive = second[tile, at, :]
            if backward:
                total = drive + state
                second[tile, at, :] = total
                first[tile, at, :] = prod
                states.append(decay * total)
                prods.append(decay * prod)
            else:
                states.append(decay * state + drive)
                prods.append(decay * prod)
                second[tile, at, :] = states[-1]
                first[tile, at, :] = prods[-1]
        return tuple(states), tuple(prods)

    states, prods = lax.fori_loop(
        0,
        span,
        body,
        (
            (jnp.zeros((8, LANES), f32),) * tiles,
            (jnp.ones((8, LANES), f32),) * tiles,
        ),
        unroll=4,
    )
    for tile in range(tiles):
        size = min(LANES, width - tile * LANES)
        cols = slice(tile * LANES, tile * LANES + size)
        wide = slice(tile * LANES, (tile + 1) * LANES)
        state, prod = states[tile], prods[tile]
        state_in = carry_state[0:1, wide]
        prod_in = carry_prod[0:1, wide]
        for chunk in range(7, -1, -1) if backward else range(8):
            at = slice(chunk * span, (chunk + 1) * span)
            held = slice(chunk * (span + 1), chunk * (span + 1) + span)
            local = first[tile, held, :]
            out_state[at, cols] = (second[tile, held, :] + local * state_in)[:, :size]
            out_prod[at, cols] = (local * prod_in)[:, :size]
            state_in = state[chunk : chunk + 1] + prod[chunk : chunk + 1] * state_in
            prod_in = prod[chunk : chunk + 1] * prod_in
        carry_state[0:1, wide] = state_in
        carry_prod[0:1, wide] = prod_in


SPOTS = ((0, 1), (2, 3), (4, 6), (5, 7))


def piece_copies(arrays, which, held, sem, along):
    copies = []
    for array, spots in zip(arrays, SPOTS):
        size = array.shape[1 + along]
        if size == held.shape[along]:
            spots = (0,)
        for piece, spot in enumerate(spots):
            at = pl.ds(spot * size, size)
            for slot, kind in which:
                place = held.at[slot, at, :] if along == 1 else held.at[slot, :, at]
                copies.append(pltpu.make_async_copy(array.at[piece, kind], place, sem))
        if size == held.shape[along]:
            break
    return copies


def load_pieces(arrays, which, held, sem, along):
    copies = []
    for array, spots in zip(arrays, SPOTS):
        size = array.shape[1 + along]
        if size == held.shape[along]:
            spots = (0,)
        for piece, spot in enumerate(spots):
            at = pl.ds(spot * size, size)
            for slot, kind in enumerate(which):
                place = held.at[slot, at, :] if along == 1 else held.at[slot, :, at]
                copies.append(pltpu.make_async_copy(array.at[piece, kind], place, sem))
        if size == held.shape[along]:
            break
    for copy in copies:
        copy.start()
    for copy in copies:
        copy.wait()


def any_specs():
    return [pl.BlockSpec(memory_space=pl.ANY)] * len(SPOTS)


def rms_low(value, gain):
    return (
        value * lax.rsqrt(jnp.mean(value * value, axis=-1, keepdims=True) + norm_eps) * gain
    ).astype(bf16)


def front_kernel(
    tok, halo, gain, w_0, w_1, w_2, w_3, w_a, w_i, vec, mask,
    xn_o, y_o, u_o, uh_o, xc_o, pa_o, pi_o, a_o, h_o, p_o, end_o,
    ubuf, abuf, bbuf, car_s, car_p, w_in, sem,
):
    step = pl.program_id(0)
    rows = tok.shape[0]
    width = y_o.shape[1]

    @pl.when(step == 0)
    def _():
        load_pieces((w_0, w_1, w_2, w_3), (0, 1), w_in, sem, 2)
        low = nt(rms_low(halo[...].astype(f32), gain[...]), w_in[1]).astype(bf16)
        uh_o[...] = low
        ubuf[0:HALO, :] = low.astype(f32)
        car_s[...] = jnp.zeros_like(car_s)
        car_p[...] = jnp.ones_like(car_p)

    xn = rms_low(tok[...].astype(f32), gain[...])
    xn_o[...] = xn
    y_o[...] = nt(xn, w_in[0])
    u_low = nt(xn, w_in[1]).astype(bf16)
    u_o[...] = u_low
    u_now = u_low.astype(f32)
    ubuf[HALO : HALO + rows, :] = u_now
    conv = vec[CONV : CONV + 1] + vec[0:1] * u_now
    for back in range(1, CONV):
        conv = conv + vec[back : back + 1] * mask[:, back : back + 1] * ubuf[
            HALO - back : HALO - back + rows, :
        ]
    ubuf[0:HALO, :] = u_now[rows - HALO :, :]
    conv_low = conv.astype(bf16)
    xc_o[...] = conv_low
    pre_decay = nn(conv_low, w_a[...]) + vec[CONV + 2 : CONV + 3]
    pre_input = nn(conv_low, w_i[...]) + vec[CONV + 3 : CONV + 4]
    pa_o[...] = pre_decay
    pi_o[...] = pre_input
    live = mask[:, 0:1]
    _, gate, raw, _, mult = gate_terms(pre_decay, pre_input, vec[CONV + 1 : CONV + 2], live)
    decay = raw * live
    a_o[...] = decay
    put_tiles(abuf, decay)
    put_tiles(bbuf, gate * conv_low.astype(f32) * mult)
    scan_tiles(abuf, bbuf, car_s, car_p, h_o, p_o, width, False)
    end_o[0:1, :] = car_s[0:1, :width]
    end_o[1:2, :] = car_p[0:1, :width]


def front(tok, halo, gain, weights, w_a, w_i, vec, mask, rows):
    count, model = tok.shape
    width = weights[0].shape[2]
    tiles = pl.cdiv(width, LANES)
    row = lambda size: pl.BlockSpec((rows, size), lambda i: (i, 0))
    like = lambda size, kind: jax.ShapeDtypeStruct((count, size), kind)
    return pl.pallas_call(
        front_kernel,
        grid=(count // rows,),
        in_specs=[
            row(model), whole(halo.shape), whole(gain.shape), *any_specs(),
            whole(w_a.shape), whole(w_i.shape), whole(vec.shape), row(mask.shape[1]),
        ],
        out_specs=[
            row(model), row(width), row(width), whole((HALO, width)), row(width), row(width),
            row(width), row(width), row(width), row(width), whole((8, width)),
        ],
        out_shape=[
            like(model, bf16), like(width, f32), like(width, bf16),
            jax.ShapeDtypeStruct((HALO, width), bf16), like(width, bf16), like(width, f32),
            like(width, f32), like(width, f32), like(width, f32), like(width, f32),
            jax.ShapeDtypeStruct((8, width), f32),
        ],
        scratch_shapes=[
            pltpu.VMEM((HALO + rows, width), f32),
            pltpu.VMEM((tiles, rows + 8, LANES), f32),
            pltpu.VMEM((tiles, rows + 8, LANES), f32),
            pltpu.VMEM((8, tiles * LANES), f32),
            pltpu.VMEM((8, tiles * LANES), f32),
            pltpu.VMEM((2, width, model), bf16),
            pltpu.SemaphoreType.DMA,
        ],
        compiler_params=params(),
        cost_estimate=cost(26),
        name="front",
    )(tok, halo, gain, *weights, w_a, w_i, vec, mask)


def state_kernel(
    rank, ends, h_l, p_l, y, h_o, hp_o, o_o, packed_o, hin, hbuf
):
    step = pl.program_id(0)
    rows = h_l.shape[0]

    @pl.when(step == 0)
    def _():
        def fold(at, held):
            return jnp.where(at < rank[0], ends[at, 0:1, :] + ends[at, 1:2, :] * held, held)

        start = lax.fori_loop(0, ends.shape[0], fold, jnp.zeros((1, h_l.shape[1]), f32))
        hin[0:1, :] = start
        hbuf[7:8, :] = start

    state = h_l[...] + p_l[...] * hin[0:1, :]
    h_o[...] = state
    hbuf[8 : 8 + rows, :] = state
    hp_o[...] = hbuf[7 : 7 + rows, :]
    hbuf[7:8, :] = state[rows - 1 :, :]
    mixed = (state * gelu_tanh(y[...])).astype(bf16)
    o_o[...] = mixed
    odd = step % 2
    full = mixed.shape[1] // LANES
    for tile in range(full):
        packed_o[2 * tile + odd] = mixed[:, tile * LANES : (tile + 1) * LANES]
    rest = mixed[:, full * LANES :]
    side = LANES // 2

    @pl.when(odd == 0)
    def _():
        packed_o[2 * full, :, :side] = rest

    @pl.when(odd == 1)
    def _():
        packed_o[2 * full, :, side:] = rest


def finish_state(rank, ends, h_l, p_l, y, rows):
    count, width = h_l.shape
    assert width % LANES == LANES // 2 and count // rows % 2 == 0
    row = lambda size: pl.BlockSpec((rows, size), lambda i: (i, 0))
    like = lambda size, kind: jax.ShapeDtypeStruct((count, size), kind)
    return pl.pallas_call(
        state_kernel,
        grid=(count // rows,),
        in_specs=[
            pl.BlockSpec(memory_space=pltpu.SMEM), whole(ends.shape), row(width), row(width),
            row(width),
        ],
        out_specs=[
            row(width), row(width), row(width),
            pl.BlockSpec((2 * width // LANES, rows, LANES), lambda i: (0, i // 2, 0)),
        ],
        out_shape=[
            like(width, f32), like(width, f32), like(width, bf16),
            jax.ShapeDtypeStruct((2 * width // LANES, count // 2, LANES), bf16),
        ],
        scratch_shapes=[
            pltpu.VMEM((8, width), f32),
            pltpu.VMEM((8 + rows, width), f32),
        ],
        compiler_params=params(),
        cost_estimate=cost(8),
        name="finish_state",
    )(rank, ends, h_l, p_l, y)


def middle_kernel(
    slab, mixed, tok, gain, dhid, w_0, w_1, w_2, w_3, u_0, u_1, u_2, u_3, *rest
):
    xn_o, hm_o, dg_o, du_o, part_o, own_o, low, w_o, w_up, o_sems, up_sem = rest[-11:]
    step = pl.program_id(0)
    kinds = w_o.shape[0]
    out_copies = lambda kind: piece_copies(
        (w_0, w_1, w_2, w_3), ((kind, kind),), w_o, o_sems.at[kind], 2
    )
    up_copies = lambda: piece_copies(
        (u_0, u_1, u_2, u_3), ((0, 0), (1, 1)), w_up, up_sem, 1
    )

    @pl.when(step == 0)
    def _():
        for kind in range(kinds):
            for copy in out_copies(kind):
                copy.start()
        for copy in up_copies():
            copy.start()

    odd = step % 2
    full = low.shape[2] // LANES
    for kind in range(kinds):
        for tile in range(full):
            low[kind, :, tile * LANES : (tile + 1) * LANES] = mixed[kind, 2 * tile + odd]
        both = mixed[kind, 2 * full].astype(f32)
        side = LANES // 2
        low[kind, :, full * LANES :] = jnp.where(
            odd == 0, both[:, :side], both[:, side:]
        ).astype(bf16)

    total = None
    for kind in range(kinds):

        @pl.when(step == 0)
        def _():
            for copy in out_copies(kind):
                copy.wait()

        more = nn(low[kind], w_o[kind])
        total = more if kind == 0 else total + more
    rows, model = xn_o.shape
    second = tok[...].astype(f32) + total
    xn = rms_low(second, gain[...])
    xn_o[...] = xn

    @pl.when(step == slab[0])
    def _():
        own_o[...] = second

    @pl.when(step == 0)
    def _():
        for copy in up_copies():
            copy.wait()

    w_g, w_u = w_up.at[0], w_up.at[1]
    hidden = dhid.shape[1]
    piece = hidden // 3
    for at in range(0, hidden, piece):
        cols = slice(at, at + piece)
        z_gate = nn(xn_o[...], w_g[:, cols])
        z_up = nn(xn_o[...], w_u[:, cols])
        d_hid = dhid[:, cols]
        act, slope = gelu_both(z_gate)
        hm_o[:, cols] = (act * z_up).astype(bf16)
        dg_o[:, cols] = (d_hid * z_up * slope).astype(bf16)
        du_o[:, cols] = (d_hid * act).astype(bf16)
    piece = model // 4
    for at in range(0, model, piece):
        cols = slice(at, at + piece)
        part_o[:, cols] = (nt(dg_o[...], w_g[cols, :]) + nt(du_o[...], w_u[cols, :])).astype(bf16)


def middle(slab, mixed, tok, gain, dhid, out_w, up_w):
    slabs = mixed.shape[0]
    width = out_w[0].shape[2]
    count, hidden = dhid.shape
    model = gain.shape[1]
    rows = count // slabs
    row = lambda size: pl.BlockSpec((rows, size), lambda i: (i, 0))
    like = lambda size: jax.ShapeDtypeStruct((count, size), bf16)
    return pl.pallas_call(
        middle_kernel,
        grid=(slabs,),
        in_specs=[
            pl.BlockSpec(memory_space=pltpu.SMEM),
            pl.BlockSpec((slabs, mixed.shape[1], rows, LANES), lambda i: (0, 0, i // 2, 0)),
            row(model), whole(gain.shape), row(hidden), *any_specs(), *any_specs(),
        ],
        out_specs=[
            row(model), row(hidden), row(hidden), row(hidden), row(model), whole((rows, model)),
        ],
        out_shape=[
            like(model), like(hidden), like(hidden), like(hidden), like(model),
            jax.ShapeDtypeStruct((rows, model), f32),
        ],
        scratch_shapes=[
            pltpu.VMEM((slabs, rows, width), bf16),
            pltpu.VMEM((slabs, width, model), bf16),
            pltpu.VMEM((2, model, hidden), bf16),
            pltpu.SemaphoreType.DMA((slabs,)),
            pltpu.SemaphoreType.DMA,
        ],
        compiler_params=params(61),
        cost_estimate=cost(52),
        name="middle",
    )(slab, mixed, tok, gain, dhid, *out_w, *up_w)


def back_kernel(
    slab, d_rec, w_0, w_1, w_2, w_3, y, h, a, dy_o, g_o, p_o, end_o, abuf, bbuf, car_s, car_p, w_o, sem
):
    step = pl.program_id(0)
    width = y.shape[1]

    @pl.when(step == 0)
    def _():
        load_pieces((w_0, w_1, w_2, w_3), (slab[0],), w_o, sem, 2)
        car_s[...] = jnp.zeros_like(car_s)
        car_p[...] = jnp.ones_like(car_p)

    d_mixed = nt(d_rec[...], w_o[0])
    act, slope = gelu_both(y[...])
    dy_o[...] = (d_mixed * h[...] * slope).astype(bf16)
    put_tiles(abuf, a[...])
    put_tiles(bbuf, d_mixed * act)
    scan_tiles(abuf, bbuf, car_s, car_p, g_o, p_o, width, True)
    end_o[0:1, :] = car_s[0:1, :width]
    end_o[1:2, :] = car_p[0:1, :width]


def back_scan(slab, d_rec, weights, y, h, a, rows):
    count, model = d_rec.shape
    width = y.shape[1]
    tiles = pl.cdiv(width, LANES)
    steps = count // rows
    row = lambda size: pl.BlockSpec((rows, size), lambda i: (steps - 1 - i, 0))
    like = lambda size, kind: jax.ShapeDtypeStruct((count, size), kind)
    return pl.pallas_call(
        back_kernel,
        grid=(steps,),
        in_specs=[
            pl.BlockSpec(memory_space=pltpu.SMEM), row(model), *any_specs(), row(width), row(width),
            row(width),
        ],
        out_specs=[row(width), row(width), row(width), whole((8, width))],
        out_shape=[
            like(width, bf16), like(width, f32), like(width, f32),
            jax.ShapeDtypeStruct((8, width), f32),
        ],
        scratch_shapes=[
            pltpu.VMEM((tiles, rows + 8, LANES), f32),
            pltpu.VMEM((tiles, rows + 8, LANES), f32),
            pltpu.VMEM((8, tiles * LANES), f32),
            pltpu.VMEM((8, tiles * LANES), f32),
            pltpu.VMEM((1, width, model), bf16),
            pltpu.SemaphoreType.DMA,
        ],
        compiler_params=params(),
        cost_estimate=cost(12),
        name="back_scan",
    )(slab, d_rec, *weights, y, h, a)


def gates_kernel(
    rank, ends, g_l, p_l, pa, pi, xc, hp, u, u_prev, u_halo, mask, w_a, w_i, vec,
    dpa_o, dpi_o, du_o, tail_o, spill_o, sum_o,
    qin, dbuf, ubuf,
):
    step = pl.program_id(0)
    steps = pl.num_programs(0)
    rows, width = g_l.shape

    @pl.when(step == 0)
    def _():
        count = ends.shape[0]

        def fold(back, held):
            at = count - 1 - back
            return jnp.where(at > rank[0], ends[at, 0:1, :] + ends[at, 1:2, :] * held, held)

        qin[0:1, :] = lax.fori_loop(0, count, fold, jnp.zeros((1, width), f32))
        sum_o[...] = jnp.zeros_like(sum_o)
        dbuf[rows : rows + 8, :] = jnp.zeros((8, width), f32)

    grad = g_l[...] + p_l[...] * qin[0:1, :]
    live = mask[:, 0:1]
    slope = vec[CONV + 1 : CONV + 2]
    rate, gate, raw, root, mult = gate_terms(pa[...], pi[...], slope, live)
    conv = xc[...].astype(f32)
    d_mult = grad * gate * conv
    d_log = live * (grad * hp[...] * raw - d_mult * (raw * raw) / root)
    d_log_rate = d_log * rate
    d_conv = grad * gate * mult
    d_pa = (d_log_rate * slope * (1.0 - rate)).astype(bf16)
    d_pi = (grad * mult * conv * gate * (1.0 - gate)).astype(bf16)
    dpa_o[...] = d_pa
    dpi_o[...] = d_pi
    d_conv = d_conv + nt(d_pa, w_a[...]) + nt(d_pi, w_i[...])
    total = lambda value: jnp.sum(value, axis=0, keepdims=True)
    u_now = u[...].astype(f32)
    before = jnp.where(step == steps - 1, u_halo[...], u_prev[...]).astype(f32)
    ubuf[0:HALO, :] = before
    ubuf[HALO : HALO + rows, :] = u_now
    dbuf[0:rows, :] = d_conv
    sum_o[0:1, :] += total(d_conv * u_now)
    d_u = vec[0:1] * d_conv
    for back in range(1, CONV):
        sum_o[back : back + 1, :] += total(
            d_conv * mask[:, back : back + 1] * ubuf[HALO - back : HALO - back + rows, :]
        )
        d_u = d_u + vec[back : back + 1] * mask[:, CONV - 1 + back : CONV + back] * dbuf[
            back : back + rows, :
        ]
    sum_o[CONV : CONV + 1, :] += total(d_conv)
    sum_o[CONV + 1 : CONV + 2, :] += total(d_log_rate)
    sum_o[CONV + 2 : CONV + 3, :] += total(d_pa.astype(f32))
    sum_o[CONV + 3 : CONV + 4, :] += total(d_pi.astype(f32))
    du_o[...] = d_u.astype(bf16)

    @pl.when(step == 0)
    def _():
        tail_o[...] = d_u[rows - HALO :, :]

    head = d_conv[0:8, :]
    dbuf[rows : rows + 8, :] = head

    @pl.when(step == steps - 1)
    def _():
        spill_o[...] = jnp.zeros_like(spill_o)
        for ahead in range(CONV - 1, 0, -1):
            row = 0.0
            for back in range(ahead, CONV):
                at = back - ahead
                row = row + vec[back : back + 1] * mask[at : at + 1, back : back + 1] * d_conv[
                    at : at + 1, :
                ]
            spill_o[HALO - ahead : HALO - ahead + 1, :] = row


def gates_back(rank, ends, g_l, p_l, pa, pi, xc, hp, u, u_halo, mask, w_a, w_i, vec, rows):
    count, width = g_l.shape
    steps = count // rows
    at = lambda i: steps - 1 - i
    row = lambda size: pl.BlockSpec((rows, size), lambda i: (at(i), 0))
    like = lambda size, kind: jax.ShapeDtypeStruct((count, size), kind)
    per = rows // HALO
    return pl.pallas_call(
        gates_kernel,
        grid=(steps,),
        in_specs=[
            pl.BlockSpec(memory_space=pltpu.SMEM), whole(ends.shape), row(width), row(width),
            row(width), row(width), row(width), row(width), row(width),
            pl.BlockSpec((HALO, width), lambda i: (jnp.maximum(at(i) * per - 1, 0), 0)),
            whole(u_halo.shape), row(mask.shape[1]), whole(w_a.shape), whole(w_i.shape),
            whole(vec.shape),
        ],
        out_specs=[
            row(width), row(width), row(width), whole((HALO, width)), whole((HALO, width)),
            whole((8, width)),
        ],
        out_shape=[
            like(width, bf16), like(width, bf16), like(width, bf16),
            jax.ShapeDtypeStruct((HALO, width), f32), jax.ShapeDtypeStruct((HALO, width), f32),
            jax.ShapeDtypeStruct((8, width), f32),
        ],
        scratch_shapes=[
            pltpu.VMEM((8, width), f32),
            pltpu.VMEM((rows + 8, width), f32),
            pltpu.VMEM((HALO + rows, width), f32),
        ],
        compiler_params=params(),
        cost_estimate=cost(19),
        name="gates_back",
    )(rank, ends, g_l, p_l, pa, pi, xc, hp, u, u, u_halo, mask, w_a, w_i, vec)


def pair_kernel(left, right, tail, more, w_0, w_1, w_2, w_3, out, right_o, held, sem):
    step = pl.program_id(0)
    rows = left.shape[0]

    @pl.when(step == 0)
    def _():
        load_pieces((w_0, w_1, w_2, w_3), (0, 1), held, sem, 2)

    right_o[...] = right[...]

    @pl.when(step == pl.num_programs(0) - 1)
    def _():
        right_o[rows - HALO :, :] = (tail[...] + more[...]).astype(bf16)

    out[...] = (nn(left[...], held[0]) + nn(right_o[...], held[1])).astype(bf16)


def pair_back(left, right, tail, more, weights, model, rows):
    count, width = left.shape
    row = lambda size: pl.BlockSpec((rows, size), lambda i: (i, 0))
    return pl.pallas_call(
        pair_kernel,
        grid=(count // rows,),
        in_specs=[
            row(width), row(width), whole(tail.shape), whole(more.shape), *any_specs(),
        ],
        out_specs=[row(model), row(width)],
        out_shape=[
            jax.ShapeDtypeStruct((count, model), bf16),
            jax.ShapeDtypeStruct((count, width), bf16),
        ],
        scratch_shapes=[pltpu.VMEM((2, width, model), bf16), pltpu.SemaphoreType.DMA],
        compiler_params=params(),
        cost_estimate=cost(12),
        name="pair_back",
    )(left, right, tail, more, *weights)


def mask_kernel(ids, out):
    rows = out.shape[0]
    now = ids[HALO : HALO + rows, :]
    same = lambda by: (now == ids[HALO + by : HALO + by + rows, :]).astype(f32)
    out[...] = jnp.zeros_like(out)
    out[:, 0:1] = same(-1)
    for back in range(1, CONV):
        out[:, back : back + 1] = same(-back)
        out[:, CONV - 1 + back : CONV + back] = same(back)


def masks(ids, count):
    return pl.pallas_call(
        mask_kernel,
        out_shape=jax.ShapeDtypeStruct((count, 8), f32),
        compiler_params=pltpu.CompilerParams(vmem_limit_bytes=16 * 1024 * 1024),
        cost_estimate=cost(2),
        name="masks",
    )(ids)


def moments_step(first, second, grad):
    new_first = beta_first * first + (1.0 - beta_first) * grad
    new_second = beta_second * second + (1.0 - beta_second) * grad * grad
    normal = (
        new_first
        * (1.0 / (1.0 - beta_first**STEP))
        / (jnp.sqrt(new_second * (1.0 / (1.0 - beta_second**STEP))) + adam_eps)
    )
    return new_first, new_second, normal


def soap_tiles(turned, tile_rows, tile_cols, w, m, v, bases, nm, nv, nw):
    side = lax.broadcasted_iota(jnp.int32, (TILE, 2 * TILE), 1) < TILE
    square = (lax.broadcasted_iota(jnp.int32, (2 * TILE, 2 * TILE), 0) < TILE) == (
        lax.broadcasted_iota(jnp.int32, (2 * TILE, 2 * TILE), 1) < TILE
    )
    for i in range(tile_rows):
        for j in range(0, tile_cols, 2):
            rows = slice(i * TILE, (i + 1) * TILE)
            cols = slice(j * TILE, (j + 2) * TILE)
            left_a, right_a = bases(i, j)
            left_b, right_b = bases(i, j + 1)
            lefts = [left_a.astype(bf16), left_b.astype(bf16)]
            both = jnp.concatenate([right_a, right_b], axis=0)
            right = jnp.where(square, jnp.concatenate([both, both], axis=1), 0.0).astype(bf16)
            choose = lambda parts: jnp.where(side, parts[0], parts[1])
            inner = choose([turned(rows, cols, left) for left in lefts]).astype(bf16)
            grad = nn(inner, right)
            new_first, new_second, normal = moments_step(m[rows, cols], v[rows, cols], grad)
            nm[rows, cols] = new_first
            nv[rows, cols] = new_second
            low = normal.astype(bf16)
            outer = choose([nn(left, low) for left in lefts]).astype(bf16)
            master = w[rows, cols]
            nw[rows, cols] = master - learn_rate * (nt(outer, right) + decay_rate * master)


def soap_kernel(turned, swapped, w, m, v, g, q, nm, nv, nw):
    def plain(rows, cols, left):
        return tn(left, g[0, rows, cols])

    def across(rows, cols, left):
        return lax.dot_general(
            left, g[0, cols, rows], (((0,), (1,)), ((), ())), preferred_element_type=f32
        )

    if swapped:
        bases = lambda i, j: (q[0, j, i, 1], q[0, j, i, 0])
    else:
        bases = lambda i, j: (q[0, i, j, 0], q[0, i, j, 1])
    soap_tiles(
        across if turned else plain, w.shape[1] // TILE, w.shape[2] // TILE,
        w.at[0], m.at[0], v.at[0], bases, nm.at[0], nv.at[0], nw.at[0],
    )


def soap(w, m, v, g, q, rows, turned=False, swapped=False):
    group, height, width = w.shape
    if width < 2 * TILE:
        q = jnp.concatenate([q, q], axis=1 if swapped else 2)
        padded = [jnp.concatenate([array, array], axis=2) for array in (w, m, v)]
        g = jnp.concatenate([g, g], axis=1 if turned else 2)
        results = soap(*padded, g, q, rows, turned, swapped)
        return [array[:, :, :width] for array in results]
    row = pl.BlockSpec((1, rows, width), lambda n, i: (n, i, 0))
    out = jax.ShapeDtypeStruct(w.shape, f32)
    if swapped:
        q_block = (1, width // TILE, rows // TILE, 2, TILE, TILE)
        q_at = lambda n, i: (n, 0, i, 0, 0, 0)
    else:
        q_block = (1, rows // TILE, width // TILE, 2, TILE, TILE)
        q_at = lambda n, i: (n, i, 0, 0, 0, 0)
    return pl.pallas_call(
        functools.partial(soap_kernel, turned, swapped),
        grid=(group, height // rows),
        in_specs=[row] * 3
        + [
            pl.BlockSpec((1, width, rows), lambda n, i: (n, 0, i)) if turned else row,
            pl.BlockSpec(q_block, q_at),
        ],
        out_specs=[row] * 3,
        out_shape=[out] * 3,
        compiler_params=pltpu.CompilerParams(
            dimension_semantics=("arbitrary", "arbitrary"), vmem_limit_bytes=56 * 1024 * 1024
        ),
        cost_estimate=cost(group * height * width / 24000),
        name="soap",
    )(w, m, v, g, q)


def reorder(array, dim, order):
    shape = array.shape
    parts = order.shape[0]
    reshaped = array.reshape(shape[:dim] + (parts, shape[dim] // parts) + shape[dim + 1 :])
    return jnp.take(reshaped, order, axis=dim, mode="clip").reshape(shape)


def gather_slabs(array):
    return lax.all_gather(array, "mlp", axis=0, tiled=True)


def scatter_slabs(array):
    return lax.psum_scatter(array, "mlp", scatter_dimension=0, tiled=True)


def hop(array, pairs):
    count = lax.axis_size("tok")
    return lax.ppermute(array, "tok", [(i, i ^ pairs[i % 2]) for i in range(count)])


CORE, NEAR, FAR = (1, 1), (2, 4), (4, 2)


def stored_order(parts, rank):
    indices = jnp.arange(parts, dtype=jnp.int32)
    if parts != 8:
        return indices, indices
    near, far = indices // 2 % 2, indices % 2
    spots = rank ^ (
        indices // 4 + jnp.where(rank % 2 == 0, near * 2 + far * 4, near * 4 + far * 2)
    )
    return spots, invert(spots)


def invert(order):
    indices = jnp.arange(order.shape[0], dtype=jnp.int32)
    return jnp.sum(jnp.where(order[None, :] == indices[:, None], indices[None, :], 0), axis=1)


def gather_start(own):
    two = jnp.concatenate([own, hop(own, FAR)], axis=0)
    return jnp.concatenate([two, hop(two, NEAR)], axis=0)


class Sums:
    def __init__(self, keep, send, dim):
        self.keep, self.send, self.dim = keep, send, dim
        self.whole = lax.axis_size("tok") != 8

    def cut(self, array, blocks, at):
        size = array.shape[self.dim] // blocks
        return lax.slice_in_dim(array, at * size, (at + 1) * size, axis=self.dim).astype(f32)

    def mixed(self, at, there):
        return self.cut(self.keep, 4, at) + self.cut(self.got, 4, there)

    def first(self, *before):
        if self.whole:
            return self.send
        self.got = hop(self.send, CORE)
        self.near_send = after(
            jnp.concatenate([self.mixed(2, 1), self.mixed(3, 3)], axis=self.dim).astype(
                self.send.dtype
            ),
            *before,
        )
        return self.near_send

    def second(self, *before):
        if self.whole:
            return self.send
        self.near = hop(self.near_send, NEAR)
        self.far_send = after(
            (self.mixed(1, 2) + self.cut(self.near, 2, 1)).astype(self.send.dtype), *before
        )
        return self.far_send

    def third(self):
        if self.whole:
            both = jnp.concatenate([self.keep.astype(self.send.dtype), self.send], axis=self.dim)
            return lax.psum_scatter(both, "tok", scatter_dimension=self.dim, tiled=True)
        far = hop(self.far_send, FAR)
        return self.mixed(0, 0) + self.cut(self.near, 2, 0) + far.astype(f32)


def sums_of(array):
    half = array.shape[0] // 2
    sums = Sums(array[:half], array[half:], 0)
    sums.first()
    sums.second()
    return sums.third()


def halves(array):
    half = array.shape[1] // 2
    return array[:, :half], array[:, half:]


def grad_rows(left, right):
    keep, send = halves(left)
    return Sums(tn(keep, right), tn(send, right).astype(bf16), 0)


def grad_columns(left, right):
    keep, send = halves(right)
    return Sums(tn(left, keep), tn(left, send).astype(bf16), 1)


def permute_kernel(order, array, out):
    parts = order.shape[0]
    size = array.shape[1] // parts
    for part in range(parts):
        at = pl.multiple_of(order[part] * size, LANES)
        out[:, part * size : (part + 1) * size] = array[:, pl.ds(at, size)]


def permute_columns(array, order):
    parts = order.shape[0]
    count, width = array.shape
    if width // parts % LANES:
        return reorder(array, 1, order)
    rows = min(256, count)
    row = pl.BlockSpec((rows, width), lambda i: (i, 0))
    return pl.pallas_call(
        permute_kernel,
        grid=(count // rows,),
        in_specs=[pl.BlockSpec(memory_space=pltpu.SMEM), row],
        out_specs=row,
        out_shape=jax.ShapeDtypeStruct(array.shape, array.dtype),
        compiler_params=params(),
        cost_estimate=cost(count * width / 420000),
        name="permute_columns",
    )(order, array)


def settle_kernel(move, order, value, upstream, gain, base, total_o, low_o, sum_o, hold):
    @pl.when(pl.program_id(0) == 0)
    def _():
        sum_o[...] = jnp.zeros_like(sum_o)

    held = value[...].astype(f32)
    grad = upstream[...].astype(f32)
    scale = lax.rsqrt(jnp.mean(held * held, axis=-1, keepdims=True) + norm_eps)
    weighted = grad * gain[...]
    inner = jnp.mean(held * weighted, axis=-1, keepdims=True)
    total = base[...].astype(f32) + (scale * weighted - held * (scale * scale * scale * inner))
    sum_o[0:1, :] += jnp.sum(grad * held * scale, axis=0, keepdims=True)
    total_o[...] = total
    low = total.astype(bf16)
    if not move:
        low_o[...] = low
        return
    hold[...] = low
    parts = order.shape[0]
    size = low.shape[1] // parts
    for part in range(parts):
        at = pl.multiple_of(order[part] * size, LANES)
        low_o[:, part * size : (part + 1) * size] = hold[:, pl.ds(at, size)]


def settle(value, upstream, gain, base, order, move):
    count, model = value.shape
    inside = move and (model // order.shape[0]) % LANES == 0
    rows = min(128, count)
    row = pl.BlockSpec((rows, model), lambda i: (i, 0))
    total, low, sums = pl.pallas_call(
        functools.partial(settle_kernel, inside),
        grid=(count // rows,),
        in_specs=[pl.BlockSpec(memory_space=pltpu.SMEM), row, row, whole(gain.shape), row],
        out_specs=[row, row, whole((8, model))],
        out_shape=[
            jax.ShapeDtypeStruct((count, model), f32),
            jax.ShapeDtypeStruct((count, model), bf16),
            jax.ShapeDtypeStruct((8, model), f32),
        ],
        scratch_shapes=[pltpu.VMEM((rows, model), bf16)],
        compiler_params=params(),
        cost_estimate=cost(4),
        name="settle",
    )(order, value, upstream, gain, base)
    if move and not inside:
        low = reorder(low, 1, order)
    return total, low, sums[0]


def after(array, *others):
    return lax.optimization_barrier((array,) + others)[0]


def block_diagonal(blocks):
    count, width, _ = blocks.shape
    return jnp.concatenate(
        [
            jnp.pad(blocks[n], ((0, 0), (n * width, (count - 1 - n) * width)))
            for n in range(count)
        ],
        axis=0,
    )


def diagonal_blocks(array, count):
    width = array.shape[0] // count
    return jnp.stack(
        [array[n * width : (n + 1) * width, n * width : (n + 1) * width] for n in range(count)]
    )


def on_device(
    tokens, segment_ids, owner_table, cotangent,
    w_in_rec, m_in_rec, v_in_rec, q_in_rec,
    w_out_rec, m_out_rec, v_out_rec, q_out_rec,
    w_in_mlp, m_in_mlp, v_in_mlp, q_in_mlp,
    w_out_mlp, m_out_mlp, v_out_mlp, q_out_mlp,
    w_gates, m_gates, v_gates, w_rnn, m_rnn, v_rnn, w_gains, m_gains, v_gains,
):
    parts = lax.axis_size("tok")
    rank = lax.axis_index("tok")
    slabs = lax.axis_size("mlp")
    slab = lax.axis_index("mlp")
    count, model = tokens.shape
    length = count * parts
    share = count // slabs
    rows = min(256, count)
    spots, places = stored_order(parts, rank)
    into_local = jnp.take(invert(owner_table), spots, mode="clip")
    from_local = jnp.take(places, owner_table, mode="clip")
    rank_ref = rank.reshape(1).astype(jnp.int32)

    blocks = w_gates.shape[1]
    gate_part = w_gates.shape[2]
    lead = 2 * blocks
    rnn_part = w_rnn.shape[1]
    small = jnp.concatenate(
        [w_gates.reshape(lead, gate_part), w_rnn, w_gains.reshape(lead, -1)], axis=1
    ).astype(bf16)
    if parts == 8:
        small_four = gather_start(small[None])
        small_rest = hop(small_four, CORE)
        small_all = jnp.concatenate(
            [small_four] + [small_rest[p : p + 1] for p in (0, 2, 1, 3)], axis=0
        )
    else:
        small_all = lax.all_gather(small, "tok", axis=0, tiled=False)
    turn = lambda array: jnp.swapaxes(array, 1, 2)
    rec_own = turn(w_in_rec).astype(bf16)[None]
    join = lambda *arrays: jnp.concatenate(arrays, axis=0)
    out_own = lax.all_gather(w_out_rec.astype(bf16), "mlp", axis=0, tiled=False)[None]
    if parts == 8:
        rec_two = join(rec_own, hop(rec_own, FAR))
        rec_near = hop(rec_two, NEAR)
        rec_core = hop(rec_two, CORE)
    gains_all = small_all[:, :, gate_part + rnn_part :].reshape(parts, 2, model // parts)
    gains_f = (
        gains_all
        .transpose(1, 0, 2)
        .reshape(2, model)
        .astype(f32)
    )
    ordered = jnp.take(small_all[:, :, : gate_part + rnn_part], from_local, axis=0, mode="clip")
    gate_mats = ordered[:, :, :gate_part].transpose(1, 0, 2).reshape(2, blocks, BW, BW)
    w_a = block_diagonal(gate_mats[0])
    w_i = block_diagonal(gate_mats[1])
    rnn_f = ordered[:, :, gate_part:].transpose(1, 0, 2).reshape(lead, -1).astype(f32)
    lam = rnn_f[CONV + 1]
    vec = rnn_f.at[CONV + 1].set(-8.0 * jax.nn.softplus(lam))

    tok_s = permute_columns(tokens, into_local)
    cot_s = permute_columns(cotangent, into_local)
    forward_pairs = [(i, i + 1) for i in range(parts - 1)]
    rim = lax.ppermute(tokens[count - HALO :], "tok", forward_pairs)
    halo = permute_columns(rim, into_local)
    rim_ids = lax.ppermute(segment_ids[count - HALO :], "tok", forward_pairs)
    ids = jnp.concatenate(
        [
            jnp.where(rank == 0, -1, rim_ids).astype(f32),
            segment_ids.astype(f32),
            jnp.full((HALO,), -1.0, f32),
        ]
    )
    mask = masks(ids[:, None], count)
    if parts == 8:
        rec_near = after(rec_near, tok_s, halo, mask, w_a, w_i, vec)
        rec_w = (rec_two, rec_near, rec_core, hop(rec_near, CORE))
        up_own = w_in_mlp.astype(bf16)[None]
        out_far = hop(after(out_own, rec_near), FAR)
        up_far = hop(after(up_own, rec_near), FAR)
    else:
        rec_w = (lax.all_gather(rec_own[0], "tok", axis=2, tiled=True)[None],) * 4
        out_w = (lax.all_gather(out_own[0], "tok", axis=2, tiled=True)[None],) * 4

    xn_one, y_pre, u_low, u_halo, conv_low, pre_decay, pre_input, decay, h_loc, p_loc, ends = front(
        tok_s, halo, gains_f[0:1], rec_w, w_a, w_i, vec, mask, rows
    )
    ends_all = lax.all_gather(ends[0:2], "tok", axis=0, tiled=False)
    state, state_prev, mixed, packed = finish_state(rank_ref, ends_all, h_loc, p_loc, y_pre, rows)
    own = lambda array: lax.dynamic_slice_in_dim(array, slab * share, share, 0)
    slab_ref = slab.reshape(1).astype(jnp.int32)
    own_tok = own(tok_s)
    mixed_all = lax.all_gather(packed, "mlp", axis=0, tiled=False)
    down_own = w_out_mlp.astype(bf16)[None]
    if parts == 8:
        out_two = join(out_own, after(out_far, ends))
        up_two = join(up_own, after(up_far, ends))
        out_near = hop(out_two, NEAR)
        up_near = hop(up_two, NEAR)
        down_far = hop(after(down_own, ends), FAR)
        out_core = hop(after(out_two, mixed), CORE)
        down_two = join(down_own, after(down_far, mixed))
        down_near = hop(down_two, NEAR)
        down_core = hop(down_two, CORE)
        up_core = hop(after(up_two, mixed), CORE)
        down_last = hop(down_near, CORE)
        down = jnp.concatenate(
            [
                down_two[0], down_two[1], down_near[0], down_near[1],
                down_core[0], down_last[0], down_core[1], down_last[1],
            ],
            axis=1,
        )
    else:
        down = lax.all_gather(down_own[0], "tok", axis=1, tiled=True)
        up_own = w_in_mlp.astype(bf16)
        up_w = (lax.all_gather(up_own, "tok", axis=1, tiled=True)[None],) * 4
    cot_s = permute_columns(after(cotangent, mixed), into_local)
    d_hidden = nt(cot_s, down)
    if parts == 8:
        out_near, up_near = after(out_near, d_hidden), after(up_near, d_hidden)
        out_w = (out_two, out_near, out_core, hop(out_near, CORE))
        up_w = (up_two, up_near, up_core, hop(up_near, CORE))
    xn_two, hidden, d_gate, d_up, d_branch, second = middle(
        slab_ref, mixed_all, tok_s, gains_f[1:2], d_hidden, out_w, up_w
    )
    d_xn_two = scatter_slabs(d_branch)
    low = lambda array: array.astype(bf16)
    sum_gate = grad_rows(xn_two, d_gate)
    sum_up = grad_rows(xn_two, d_up)
    sum_down = grad_rows(cot_s, hidden)
    branch_two = nn(hidden, down).astype(bf16)
    d_xn_two = after(
        d_xn_two, sum_gate.first(), sum_up.first(), sum_down.first()
    )
    sum_gate.second()
    sum_up.second()
    sum_down.second()
    g_in_mlp = jnp.stack([low(sum_gate.third()), low(sum_up.third())])
    g_out_mlp = low(sum_down.third())

    lead_one = lambda *arrays: [array[None] for array in arrays]
    split = lambda height: max(
        n for n in range(2 * TILE, height + 1, 2 * TILE) if height % n == 0 and n <= 512
    )
    in_mlp_new = soap(w_in_mlp, m_in_mlp, v_in_mlp, g_in_mlp, q_in_mlp, TILE)

    d_second, d_second_low, g_gain_two = settle(
        second, d_xn_two, gains_f[1:2], own(cot_s), from_local, False
    )
    d_rec = gather_slabs(d_second_low)
    branch_two = after(branch_two, in_mlp_new[0])
    d_rec = after(d_rec, in_mlp_new[0])
    branch_sum = scatter_slabs(branch_two)
    result_own = second + branch_sum.astype(f32)
    result_low = permute_columns(result_own.astype(bf16), from_local)
    d_ypre, g_loc, q_loc, ends_back = back_scan(slab_ref, d_rec, out_w, y_pre, state, decay, rows)
    ends_back_all = lax.all_gather(ends_back[0:2], "tok", axis=0, tiled=False)
    d_pa, d_pi, d_u, d_u_tail, spill, sums = gates_back(
        rank_ref, ends_back_all, g_loc, q_loc, pre_decay, pre_input, conv_low, state_prev,
        u_low, u_halo, mask, w_a, w_i, vec, rows,
    )
    from_next = lax.ppermute(spill, "tok", [(i + 1, i) for i in range(parts - 1)])
    d_pair, d_u = pair_back(d_ypre, d_u, d_u_tail, from_next, rec_w, model, rows)
    d_xn_one = scatter_slabs(after(d_pair, branch_sum))
    out_mlp_new = soap(
        *lead_one(w_out_mlp, m_out_mlp, v_out_mlp, after(g_out_mlp, d_pair), q_out_mlp),
        split(w_out_mlp.shape[0]), turned=True,
    )
    d_rec, mixed, xn_one, d_ypre, d_u, d_pa, d_pi, conv_low = lax.optimization_barrier(
        (d_rec, mixed, xn_one, d_ypre, d_u, d_pa, d_pi, conv_low, d_pair)
    )[:8]
    sum_out = grad_columns(mixed, d_rec)
    sum_y = grad_columns(d_ypre, xn_one)
    sum_u = grad_columns(d_u, xn_one)
    d_xn_one = after(
        d_xn_one, sum_out.first(), sum_y.first(), sum_u.first(), out_mlp_new[0]
    )
    _, d_input_low, g_gain_one = settle(
        own_tok, d_xn_one, gains_f[0:1], d_second, from_local, True
    )
    d_input = gather_slabs(d_input_low)
    sum_out.second()
    sum_y.second()
    sum_u.second()
    g_out_rec = low(sum_out.third())
    g_in_rec = jnp.stack([low(sum_y.third()), low(sum_u.third())])
    result = gather_slabs(after(result_low, d_input_low))

    g_gates = jnp.stack(
        [
            diagonal_blocks(tn(conv_low, d_pa), blocks),
            diagonal_blocks(tn(conv_low, d_pi), blocks),
        ]
    )
    g_rnn = sums.at[CONV + 1].multiply(-8.0 * jax.nn.sigmoid(lam))
    g_small = jnp.concatenate(
        [g_gates.reshape(lead, parts, gate_part), g_rnn.reshape(lead, parts, rnn_part)], axis=2
    ).transpose(1, 0, 2)
    g_small = jnp.take(g_small, into_local, axis=0, mode="clip")
    sum_small = sums_of(g_small)[0]
    sum_gates = sum_small[:, :gate_part].reshape(w_gates.shape)
    sum_rnn = sum_small[:, gate_part:]
    g_gains = jnp.stack([g_gain_one, g_gain_two]).reshape(2, parts, -1).transpose(1, 0, 2)
    sum_gains = lax.psum(sums_of(g_gains)[0], "mlp")

    out_rec_new = soap(
        *lead_one(w_out_rec, m_out_rec, v_out_rec, g_out_rec, q_out_rec), w_out_rec.shape[0]
    )
    in_rec_new = soap(
        turn(w_in_rec), turn(m_in_rec), turn(v_in_rec), g_in_rec, q_in_rec, w_in_rec.shape[2],
        swapped=True,
    )
    out_mlp_new = [array[0] for array in out_mlp_new]
    out_rec_new = [array[0] for array in out_rec_new]
    in_rec_new = [turn(array) for array in in_rec_new]
    gates_m, gates_v, gates_n = moments_step(m_gates, v_gates, sum_gates)
    gates_w = w_gates - learn_rate * (gates_n + decay_rate * w_gates)
    rnn_m, rnn_v, _ = moments_step(m_rnn, v_rnn, sum_rnn)
    gains_m, gains_v, _ = moments_step(m_gains, v_gains, sum_gains)
    d_input = after(
        d_input, in_rec_new[0], out_rec_new[0], gates_w, rnn_m
    ).astype(f32)
    return (
        result, d_input,
        in_rec_new[0], in_rec_new[1], in_rec_new[2],
        out_rec_new[0], out_rec_new[1], out_rec_new[2],
        in_mlp_new[0], in_mlp_new[1], in_mlp_new[2],
        out_mlp_new[0], out_mlp_new[1], out_mlp_new[2],
        gates_m, gates_v, gates_w, rnn_m, rnn_v, gains_m, gains_v,
    )


def solution(mesh):
    in_specs = (
        P("tok", None),
        P("tok"),
        P(),
        P("tok", None),
        P(None, "tok", "mlp"),
        P(None, "tok", "mlp"),
        P(None, "tok", "mlp"),
        P(None, "tok", "mlp", None, None, None),
        P("mlp", "tok"),
        P("mlp", "tok"),
        P("mlp", "tok"),
        P("mlp", "tok", None, None, None),
        P(None, "tok", "mlp"),
        P(None, "tok", "mlp"),
        P(None, "tok", "mlp"),
        P(None, "tok", "mlp", None, None, None),
        P("mlp", "tok"),
        P("mlp", "tok"),
        P("mlp", "tok"),
        P("mlp", "tok", None, None, None),
        P(None, "mlp", "tok"),
        P(None, "mlp", "tok"),
        P(None, "mlp", "tok"),
        P(None, ("mlp", "tok")),
        P(None, ("mlp", "tok")),
        P(None, ("mlp", "tok")),
        P(None, "tok"),
        P(None, "tok"),
        P(None, "tok"),
    )
    out_specs = (
        P("tok", None),
        P("tok", None),
        P(None, "tok", "mlp"),
        P(None, "tok", "mlp"),
        P(None, "tok", "mlp"),
        P("mlp", "tok"),
        P("mlp", "tok"),
        P("mlp", "tok"),
        P(None, "tok", "mlp"),
        P(None, "tok", "mlp"),
        P(None, "tok", "mlp"),
        P("mlp", "tok"),
        P("mlp", "tok"),
        P("mlp", "tok"),
        P(None, "mlp", "tok"),
        P(None, "mlp", "tok"),
        P(None, "mlp", "tok"),
        P(None, ("mlp", "tok")),
        P(None, ("mlp", "tok")),
        P(None, "tok"),
        P(None, "tok"),
    )
    return jax.shard_map(
        on_device, mesh=mesh, in_specs=in_specs, out_specs=out_specs, check_vma=False
    )
```

```python
import functools

import jax
import jax.numpy as jnp
from jax import lax
from jax.experimental import pallas as pl
from jax.experimental.pallas import tpu as pltpu
from jax.sharding import PartitionSpec as P

BW = 176
CONV = 4
TILE = 64
STEP = 7
HALO = 16
LANES = 128

norm_eps = 1e-06
learn_rate = 0.02
beta_first = 0.9
beta_second = 0.999
adam_eps = 1e-08
decay_rate = 0.1

f32 = jnp.float32
bf16 = jnp.bfloat16


def params(limit=56):
    return pltpu.CompilerParams(
        dimension_semantics=("arbitrary",), vmem_limit_bytes=limit * 1024 * 1024
    )


def cost(micros):
    return pl.CostEstimate(
        flops=int(micros * 1.1e9), bytes_accessed=int(micros * 3.3e6), transcendentals=0
    )


def whole(shape):
    return pl.BlockSpec(shape, lambda *_: (0,) * len(shape), pipeline_mode=pl.Buffered(1))


def nn(left, right):
    return lax.dot_general(left, right, (((1,), (0,)), ((), ())), preferred_element_type=f32)


def nt(left, right):
    return lax.dot_general(left, right, (((1,), (1,)), ((), ())), preferred_element_type=f32)


def tn(left, right):
    return lax.dot_general(left, right, (((0,), (0,)), ((), ())), preferred_element_type=f32)


def gelu_both(value):
    square = value * value
    bent = jnp.tanh(0.7978845608028654 * (value + 0.044715 * value * square))
    half = 0.5 * (1.0 + bent)
    slope = half + (0.5 * 0.7978845608028654) * value * (1.0 - bent * bent) * (
        1.0 + (3.0 * 0.044715) * square
    )
    return value * half, slope


def gelu_tanh(value):
    return (
        0.5
        * value
        * (1.0 + jnp.tanh(0.7978845608028654 * (value + 0.044715 * value * value * value)))
    )


def one_less_square(log_value, value):
    twice = 2.0 * log_value
    series = 1.0 + twice * (1.0 / 6.0)
    for order in range(5, 1, -1):
        series = 1.0 + twice * series * (1.0 / order)
    return jnp.where(twice > -0.0625, -twice * series, 1.0 - value * value)


def gate_terms(pre_decay, pre_input, slope, live):
    rate = 0.5 + 0.5 * jnp.tanh(0.5 * pre_decay)
    gate = 0.5 + 0.5 * jnp.tanh(0.5 * pre_input)
    log_decay = slope * rate
    raw = jnp.exp(log_decay)
    root = jnp.sqrt(one_less_square(log_decay, raw))
    mult = (1.0 - live) + live * root
    return rate, gate, raw, root, mult


def put_tiles(buffer, value):
    width = value.shape[1]
    span = value.shape[0] // 8
    for tile in range(pl.cdiv(width, LANES)):
        size = min(LANES, width - tile * LANES)
        for chunk in range(8):
            at = chunk * (span + 1)
            buffer[tile, at : at + span, :size] = value[
                chunk * span : (chunk + 1) * span, tile * LANES : tile * LANES + size
            ]


def scan_tiles(first, second, carry_state, carry_prod, out_state, out_prod, width, backward):
    tiles, rows, _ = first.shape
    span = rows // 8 - 1

    def body(step, held):
        row = (span - 1 - step) if backward else step
        at = pl.ds(row, 8, stride=span + 1)
        states, prods = [], []
        for tile in range(tiles):
            state, prod = held[0][tile], held[1][tile]
            decay = first[tile, at, :]
            drive = second[tile, at, :]
            if backward:
                total = drive + state
                second[tile, at, :] = total
                first[tile, at, :] = prod
                states.append(decay * total)
                prods.append(decay * prod)
            else:
                states.append(decay * state + drive)
                prods.append(decay * prod)
                second[tile, at, :] = states[-1]
                first[tile, at, :] = prods[-1]
        return tuple(states), tuple(prods)

    states, prods = lax.fori_loop(
        0,
        span,
        body,
        (
            (jnp.zeros((8, LANES), f32),) * tiles,
            (jnp.ones((8, LANES), f32),) * tiles,
        ),
        unroll=4,
    )
    for tile in range(tiles):
        size = min(LANES, width - tile * LANES)
        cols = slice(tile * LANES, tile * LANES + size)
        wide = slice(tile * LANES, (tile + 1) * LANES)
        state, prod = states[tile], prods[tile]
        state_in = carry_state[0:1, wide]
        prod_in = carry_prod[0:1, wide]
        for chunk in range(7, -1, -1) if backward else range(8):
            at = slice(chunk * span, (chunk + 1) * span)
            held = slice(chunk * (span + 1), chunk * (span + 1) + span)
            local = first[tile, held, :]
            out_state[at, cols] = (second[tile, held, :] + local * state_in)[:, :size]
            out_prod[at, cols] = (local * prod_in)[:, :size]
            state_in = state[chunk : chunk + 1] + prod[chunk : chunk + 1] * state_in
            prod_in = prod[chunk : chunk + 1] * prod_in
        carry_state[0:1, wide] = state_in
        carry_prod[0:1, wide] = prod_in


SPOTS = ((0, 1), (2, 3), (4, 6), (5, 7))


def piece_copies(arrays, which, held, sem, along):
    copies = []
    for array, spots in zip(arrays, SPOTS):
        size = array.shape[1 + along]
        if size == held.shape[along]:
            spots = (0,)
        for piece, spot in enumerate(spots):
            at = pl.ds(spot * size, size)
            for slot, kind in which:
                place = held.at[slot, at, :] if along == 1 else held.at[slot, :, at]
                copies.append(pltpu.make_async_copy(array.at[piece, kind], place, sem))
        if size == held.shape[along]:
            break
    return copies


def load_pieces(arrays, which, held, sem, along):
    copies = []
    for array, spots in zip(arrays, SPOTS):
        size = array.shape[1 + along]
        if size == held.shape[along]:
            spots = (0,)
        for piece, spot in enumerate(spots):
            at = pl.ds(spot * size, size)
            for slot, kind in enumerate(which):
                place = held.at[slot, at, :] if along == 1 else held.at[slot, :, at]
                copies.append(pltpu.make_async_copy(array.at[piece, kind], place, sem))
        if size == held.shape[along]:
            break
    for copy in copies:
        copy.start()
    for copy in copies:
        copy.wait()


def any_specs():
    return [pl.BlockSpec(memory_space=pl.ANY)] * len(SPOTS)


def rms_low(value, gain):
    return (
        value * lax.rsqrt(jnp.mean(value * value, axis=-1, keepdims=True) + norm_eps) * gain
    ).astype(bf16)


def front_kernel(
    tok, halo, gain, w_0, w_1, w_2, w_3, w_a, w_i, vec, mask,
    xn_o, y_o, u_o, uh_o, xc_o, pa_o, pi_o, a_o, h_o, p_o, end_o,
    ubuf, abuf, bbuf, car_s, car_p, w_in, sem,
):
    step = pl.program_id(0)
    rows = tok.shape[0]
    width = y_o.shape[1]

    @pl.when(step == 0)
    def _():
        load_pieces((w_0, w_1, w_2, w_3), (0, 1), w_in, sem, 2)
        low = nt(rms_low(halo[...].astype(f32), gain[...]), w_in[1]).astype(bf16)
        uh_o[...] = low
        ubuf[0:HALO, :] = low.astype(f32)
        car_s[...] = jnp.zeros_like(car_s)
        car_p[...] = jnp.ones_like(car_p)

    xn = rms_low(tok[...].astype(f32), gain[...])
    xn_o[...] = xn
    y_o[...] = nt(xn, w_in[0])
    u_low = nt(xn, w_in[1]).astype(bf16)
    u_o[...] = u_low
    u_now = u_low.astype(f32)
    ubuf[HALO : HALO + rows, :] = u_now
    conv = vec[CONV : CONV + 1] + vec[0:1] * u_now
    for back in range(1, CONV):
        conv = conv + vec[back : back + 1] * mask[:, back : back + 1] * ubuf[
            HALO - back : HALO - back + rows, :
        ]
    ubuf[0:HALO, :] = u_now[rows - HALO :, :]
    conv_low = conv.astype(bf16)
    xc_o[...] = conv_low
    pre_decay = nn(conv_low, w_a[...]) + vec[CONV + 2 : CONV + 3]
    pre_input = nn(conv_low, w_i[...]) + vec[CONV + 3 : CONV + 4]
    pa_o[...] = pre_decay
    pi_o[...] = pre_input
    live = mask[:, 0:1]
    _, gate, raw, _, mult = gate_terms(pre_decay, pre_input, vec[CONV + 1 : CONV + 2], live)
    decay = raw * live
    a_o[...] = decay
    put_tiles(abuf, decay)
    put_tiles(bbuf, gate * conv_low.astype(f32) * mult)
    scan_tiles(abuf, bbuf, car_s, car_p, h_o, p_o, width, False)
    end_o[0:1, :] = car_s[0:1, :width]
    end_o[1:2, :] = car_p[0:1, :width]


def front(tok, halo, gain, weights, w_a, w_i, vec, mask, rows):
    count, model = tok.shape
    width = weights[0].shape[2]
    tiles = pl.cdiv(width, LANES)
    row = lambda size: pl.BlockSpec((rows, size), lambda i: (i, 0))
    like = lambda size, kind: jax.ShapeDtypeStruct((count, size), kind)
    return pl.pallas_call(
        front_kernel,
        grid=(count // rows,),
        in_specs=[
            row(model), whole(halo.shape), whole(gain.shape), *any_specs(),
            whole(w_a.shape), whole(w_i.shape), whole(vec.shape), row(mask.shape[1]),
        ],
        out_specs=[
            row(model), row(width), row(width), whole((HALO, width)), row(width), row(width),
            row(width), row(width), row(width), row(width), whole((8, width)),
        ],
        out_shape=[
            like(model, bf16), like(width, f32), like(width, bf16),
            jax.ShapeDtypeStruct((HALO, width), bf16), like(width, bf16), like(width, f32),
            like(width, f32), like(width, f32), like(width, f32), like(width, f32),
            jax.ShapeDtypeStruct((8, width), f32),
        ],
        scratch_shapes=[
            pltpu.VMEM((HALO + rows, width), f32),
            pltpu.VMEM((tiles, rows + 8, LANES), f32),
            pltpu.VMEM((tiles, rows + 8, LANES), f32),
            pltpu.VMEM((8, tiles * LANES), f32),
            pltpu.VMEM((8, tiles * LANES), f32),
            pltpu.VMEM((2, width, model), bf16),
            pltpu.SemaphoreType.DMA,
        ],
        compiler_params=params(),
        cost_estimate=cost(26),
        name="front",
    )(tok, halo, gain, *weights, w_a, w_i, vec, mask)


def state_kernel(
    rank, ends, h_l, p_l, y, h_o, hp_o, o_o, hin, hbuf
):
    step = pl.program_id(0)
    rows = h_l.shape[0]

    @pl.when(step == 0)
    def _():
        def fold(at, held):
            return jnp.where(at < rank[0], ends[at, 0:1, :] + ends[at, 1:2, :] * held, held)

        start = lax.fori_loop(0, ends.shape[0], fold, jnp.zeros((1, h_l.shape[1]), f32))
        hin[0:1, :] = start
        hbuf[7:8, :] = start

    state = h_l[...] + p_l[...] * hin[0:1, :]
    h_o[...] = state
    hbuf[8 : 8 + rows, :] = state
    hp_o[...] = hbuf[7 : 7 + rows, :]
    hbuf[7:8, :] = state[rows - 1 :, :]
    o_o[...] = (state * gelu_tanh(y[...])).astype(bf16)


def finish_state(rank, ends, h_l, p_l, y, rows):
    count, width = h_l.shape
    row = lambda size: pl.BlockSpec((rows, size), lambda i: (i, 0))
    like = lambda size, kind: jax.ShapeDtypeStruct((count, size), kind)
    return pl.pallas_call(
        state_kernel,
        grid=(count // rows,),
        in_specs=[
            pl.BlockSpec(memory_space=pltpu.SMEM), whole(ends.shape), row(width), row(width),
            row(width),
        ],
        out_specs=[row(width), row(width), row(width)],
        out_shape=[like(width, f32), like(width, f32), like(width, bf16)],
        scratch_shapes=[
            pltpu.VMEM((8, width), f32),
            pltpu.VMEM((8 + rows, width), f32),
        ],
        compiler_params=params(),
        cost_estimate=cost(8),
        name="finish_state",
    )(rank, ends, h_l, p_l, y)


def middle_kernel(
    slab, mixed, tok, gain, dhid, w_0, w_1, w_2, w_3, u_0, u_1, u_2, u_3, *rest
):
    xn_o, hm_o, dg_o, du_o, part_o, own_o, w_o, w_up, o_sems, up_sem = rest[-10:]
    step = pl.program_id(0)
    kinds = w_o.shape[0]
    out_copies = lambda kind: piece_copies(
        (w_0, w_1, w_2, w_3), ((kind, kind),), w_o, o_sems.at[kind], 2
    )
    up_copies = lambda: piece_copies(
        (u_0, u_1, u_2, u_3), ((0, 0), (1, 1)), w_up, up_sem, 1
    )

    @pl.when(step == 0)
    def _():
        for kind in range(kinds):
            for copy in out_copies(kind):
                copy.start()
        for copy in up_copies():
            copy.start()

    total = None
    for kind in range(kinds):

        @pl.when(step == 0)
        def _():
            for copy in out_copies(kind):
                copy.wait()

        more = nn(mixed[kind], w_o[kind])
        total = more if kind == 0 else total + more
    rows, model = xn_o.shape
    second = tok[...].astype(f32) + total
    xn = rms_low(second, gain[...])
    xn_o[...] = xn

    @pl.when(step == slab[0])
    def _():
        own_o[...] = second

    @pl.when(step == 0)
    def _():
        for copy in up_copies():
            copy.wait()

    w_g, w_u = w_up.at[0], w_up.at[1]
    hidden = dhid.shape[1]
    piece = hidden // 3
    for at in range(0, hidden, piece):
        cols = slice(at, at + piece)
        z_gate = nn(xn_o[...], w_g[:, cols])
        z_up = nn(xn_o[...], w_u[:, cols])
        d_hid = dhid[:, cols]
        act, slope = gelu_both(z_gate)
        hm_o[:, cols] = (act * z_up).astype(bf16)
        dg_o[:, cols] = (d_hid * z_up * slope).astype(bf16)
        du_o[:, cols] = (d_hid * act).astype(bf16)
    piece = model // 4
    for at in range(0, model, piece):
        cols = slice(at, at + piece)
        part_o[:, cols] = (nt(dg_o[...], w_g[cols, :]) + nt(du_o[...], w_u[cols, :])).astype(bf16)


def middle(slab, mixed, tok, gain, dhid, out_w, up_w):
    slabs, count, width = mixed.shape
    hidden = dhid.shape[1]
    model = gain.shape[1]
    rows = count // slabs
    row = lambda size: pl.BlockSpec((rows, size), lambda i: (i, 0))
    like = lambda size: jax.ShapeDtypeStruct((count, size), bf16)
    return pl.pallas_call(
        middle_kernel,
        grid=(slabs,),
        in_specs=[
            pl.BlockSpec(memory_space=pltpu.SMEM),
            pl.BlockSpec((slabs, rows, width), lambda i: (0, i, 0)),
            row(model), whole(gain.shape), row(hidden), *any_specs(), *any_specs(),
        ],
        out_specs=[
            row(model), row(hidden), row(hidden), row(hidden), row(model), whole((rows, model)),
        ],
        out_shape=[
            like(model), like(hidden), like(hidden), like(hidden), like(model),
            jax.ShapeDtypeStruct((rows, model), f32),
        ],
        scratch_shapes=[
            pltpu.VMEM((slabs, width, model), bf16),
            pltpu.VMEM((2, model, hidden), bf16),
            pltpu.SemaphoreType.DMA((slabs,)),
            pltpu.SemaphoreType.DMA,
        ],
        compiler_params=params(61),
        cost_estimate=cost(52),
        name="middle",
    )(slab, mixed, tok, gain, dhid, *out_w, *up_w)


def back_kernel(
    slab, d_rec, w_0, w_1, w_2, w_3, y, h, a, dy_o, g_o, p_o, end_o, abuf, bbuf, car_s, car_p, w_o, sem
):
    step = pl.program_id(0)
    width = y.shape[1]

    @pl.when(step == 0)
    def _():
        load_pieces((w_0, w_1, w_2, w_3), (slab[0],), w_o, sem, 2)
        car_s[...] = jnp.zeros_like(car_s)
        car_p[...] = jnp.ones_like(car_p)

    d_mixed = nt(d_rec[...], w_o[0])
    act, slope = gelu_both(y[...])
    dy_o[...] = (d_mixed * h[...] * slope).astype(bf16)
    put_tiles(abuf, a[...])
    put_tiles(bbuf, d_mixed * act)
    scan_tiles(abuf, bbuf, car_s, car_p, g_o, p_o, width, True)
    end_o[0:1, :] = car_s[0:1, :width]
    end_o[1:2, :] = car_p[0:1, :width]


def back_scan(slab, d_rec, weights, y, h, a, rows):
    count, model = d_rec.shape
    width = y.shape[1]
    tiles = pl.cdiv(width, LANES)
    steps = count // rows
    row = lambda size: pl.BlockSpec((rows, size), lambda i: (steps - 1 - i, 0))
    like = lambda size, kind: jax.ShapeDtypeStruct((count, size), kind)
    return pl.pallas_call(
        back_kernel,
        grid=(steps,),
        in_specs=[
            pl.BlockSpec(memory_space=pltpu.SMEM), row(model), *any_specs(), row(width), row(width),
            row(width),
        ],
        out_specs=[row(width), row(width), row(width), whole((8, width))],
        out_shape=[
            like(width, bf16), like(width, f32), like(width, f32),
            jax.ShapeDtypeStruct((8, width), f32),
        ],
        scratch_shapes=[
            pltpu.VMEM((tiles, rows + 8, LANES), f32),
            pltpu.VMEM((tiles, rows + 8, LANES), f32),
            pltpu.VMEM((8, tiles * LANES), f32),
            pltpu.VMEM((8, tiles * LANES), f32),
            pltpu.VMEM((1, width, model), bf16),
            pltpu.SemaphoreType.DMA,
        ],
        compiler_params=params(),
        cost_estimate=cost(12),
        name="back_scan",
    )(slab, d_rec, *weights, y, h, a)


def gates_kernel(
    rank, ends, g_l, p_l, pa, pi, xc, hp, u, u_prev, u_halo, mask, w_a, w_i, vec,
    dpa_o, dpi_o, du_o, tail_o, spill_o, sum_o,
    qin, dbuf, ubuf,
):
    step = pl.program_id(0)
    steps = pl.num_programs(0)
    rows, width = g_l.shape

    @pl.when(step == 0)
    def _():
        count = ends.shape[0]

        def fold(back, held):
            at = count - 1 - back
            return jnp.where(at > rank[0], ends[at, 0:1, :] + ends[at, 1:2, :] * held, held)

        qin[0:1, :] = lax.fori_loop(0, count, fold, jnp.zeros((1, width), f32))
        sum_o[...] = jnp.zeros_like(sum_o)
        dbuf[rows : rows + 8, :] = jnp.zeros((8, width), f32)

    grad = g_l[...] + p_l[...] * qin[0:1, :]
    live = mask[:, 0:1]
    slope = vec[CONV + 1 : CONV + 2]
    rate, gate, raw, root, mult = gate_terms(pa[...], pi[...], slope, live)
    conv = xc[...].astype(f32)
    d_mult = grad * gate * conv
    d_log = live * (grad * hp[...] * raw - d_mult * (raw * raw) / root)
    d_log_rate = d_log * rate
    d_conv = grad * gate * mult
    d_pa = (d_log_rate * slope * (1.0 - rate)).astype(bf16)
    d_pi = (grad * mult * conv * gate * (1.0 - gate)).astype(bf16)
    dpa_o[...] = d_pa
    dpi_o[...] = d_pi
    d_conv = d_conv + nt(d_pa, w_a[...]) + nt(d_pi, w_i[...])
    total = lambda value: jnp.sum(value, axis=0, keepdims=True)
    u_now = u[...].astype(f32)
    before = jnp.where(step == steps - 1, u_halo[...], u_prev[...]).astype(f32)
    ubuf[0:HALO, :] = before
    ubuf[HALO : HALO + rows, :] = u_now
    dbuf[0:rows, :] = d_conv
    sum_o[0:1, :] += total(d_conv * u_now)
    d_u = vec[0:1] * d_conv
    for back in range(1, CONV):
        sum_o[back : back + 1, :] += total(
            d_conv * mask[:, back : back + 1] * ubuf[HALO - back : HALO - back + rows, :]
        )
        d_u = d_u + vec[back : back + 1] * mask[:, CONV - 1 + back : CONV + back] * dbuf[
            back : back + rows, :
        ]
    sum_o[CONV : CONV + 1, :] += total(d_conv)
    sum_o[CONV + 1 : CONV + 2, :] += total(d_log_rate)
    sum_o[CONV + 2 : CONV + 3, :] += total(d_pa.astype(f32))
    sum_o[CONV + 3 : CONV + 4, :] += total(d_pi.astype(f32))
    du_o[...] = d_u.astype(bf16)

    @pl.when(step == 0)
    def _():
        tail_o[...] = d_u[rows - HALO :, :]

    head = d_conv[0:8, :]
    dbuf[rows : rows + 8, :] = head

    @pl.when(step == steps - 1)
    def _():
        spill_o[...] = jnp.zeros_like(spill_o)
        for ahead in range(CONV - 1, 0, -1):
            row = 0.0
            for back in range(ahead, CONV):
                at = back - ahead
                row = row + vec[back : back + 1] * mask[at : at + 1, back : back + 1] * d_conv[
                    at : at + 1, :
                ]
            spill_o[HALO - ahead : HALO - ahead + 1, :] = row


def gates_back(rank, ends, g_l, p_l, pa, pi, xc, hp, u, u_halo, mask, w_a, w_i, vec, rows):
    count, width = g_l.shape
    steps = count // rows
    at = lambda i: steps - 1 - i
    row = lambda size: pl.BlockSpec((rows, size), lambda i: (at(i), 0))
    like = lambda size, kind: jax.ShapeDtypeStruct((count, size), kind)
    per = rows // HALO
    return pl.pallas_call(
        gates_kernel,
        grid=(steps,),
        in_specs=[
            pl.BlockSpec(memory_space=pltpu.SMEM), whole(ends.shape), row(width), row(width),
            row(width), row(width), row(width), row(width), row(width),
            pl.BlockSpec((HALO, width), lambda i: (jnp.maximum(at(i) * per - 1, 0), 0)),
            whole(u_halo.shape), row(mask.shape[1]), whole(w_a.shape), whole(w_i.shape),
            whole(vec.shape),
        ],
        out_specs=[
            row(width), row(width), row(width), whole((HALO, width)), whole((HALO, width)),
            whole((8, width)),
        ],
        out_shape=[
            like(width, bf16), like(width, bf16), like(width, bf16),
            jax.ShapeDtypeStruct((HALO, width), f32), jax.ShapeDtypeStruct((HALO, width), f32),
            jax.ShapeDtypeStruct((8, width), f32),
        ],
        scratch_shapes=[
            pltpu.VMEM((8, width), f32),
            pltpu.VMEM((rows + 8, width), f32),
            pltpu.VMEM((HALO + rows, width), f32),
        ],
        compiler_params=params(),
        cost_estimate=cost(19),
        name="gates_back",
    )(rank, ends, g_l, p_l, pa, pi, xc, hp, u, u, u_halo, mask, w_a, w_i, vec)


def pair_kernel(left, right, tail, more, w_0, w_1, w_2, w_3, out, right_o, held, sem):
    step = pl.program_id(0)
    rows = left.shape[0]

    @pl.when(step == 0)
    def _():
        load_pieces((w_0, w_1, w_2, w_3), (0, 1), held, sem, 2)

    right_o[...] = right[...]

    @pl.when(step == pl.num_programs(0) - 1)
    def _():
        right_o[rows - HALO :, :] = (tail[...] + more[...]).astype(bf16)

    out[...] = (nn(left[...], held[0]) + nn(right_o[...], held[1])).astype(bf16)


def pair_back(left, right, tail, more, weights, model, rows):
    count, width = left.shape
    row = lambda size: pl.BlockSpec((rows, size), lambda i: (i, 0))
    return pl.pallas_call(
        pair_kernel,
        grid=(count // rows,),
        in_specs=[
            row(width), row(width), whole(tail.shape), whole(more.shape), *any_specs(),
        ],
        out_specs=[row(model), row(width)],
        out_shape=[
            jax.ShapeDtypeStruct((count, model), bf16),
            jax.ShapeDtypeStruct((count, width), bf16),
        ],
        scratch_shapes=[pltpu.VMEM((2, width, model), bf16), pltpu.SemaphoreType.DMA],
        compiler_params=params(),
        cost_estimate=cost(12),
        name="pair_back",
    )(left, right, tail, more, *weights)


def mask_kernel(ids, out):
    rows = out.shape[0]
    now = ids[HALO : HALO + rows, :]
    same = lambda by: (now == ids[HALO + by : HALO + by + rows, :]).astype(f32)
    out[...] = jnp.zeros_like(out)
    out[:, 0:1] = same(-1)
    for back in range(1, CONV):
        out[:, back : back + 1] = same(-back)
        out[:, CONV - 1 + back : CONV + back] = same(back)


def masks(ids, count):
    return pl.pallas_call(
        mask_kernel,
        out_shape=jax.ShapeDtypeStruct((count, 8), f32),
        compiler_params=pltpu.CompilerParams(vmem_limit_bytes=16 * 1024 * 1024),
        cost_estimate=cost(2),
        name="masks",
    )(ids)


def moments_step(first, second, grad):
    new_first = beta_first * first + (1.0 - beta_first) * grad
    new_second = beta_second * second + (1.0 - beta_second) * grad * grad
    normal = (
        new_first
        * (1.0 / (1.0 - beta_first**STEP))
        / (jnp.sqrt(new_second * (1.0 / (1.0 - beta_second**STEP))) + adam_eps)
    )
    return new_first, new_second, normal


def soap_tiles(turned, tile_rows, tile_cols, w, m, v, bases, nm, nv, nw):
    side = lax.broadcasted_iota(jnp.int32, (TILE, 2 * TILE), 1) < TILE
    square = (lax.broadcasted_iota(jnp.int32, (2 * TILE, 2 * TILE), 0) < TILE) == (
        lax.broadcasted_iota(jnp.int32, (2 * TILE, 2 * TILE), 1) < TILE
    )
    for i in range(tile_rows):
        for j in range(0, tile_cols, 2):
            rows = slice(i * TILE, (i + 1) * TILE)
            cols = slice(j * TILE, (j + 2) * TILE)
            left_a, right_a = bases(i, j)
            left_b, right_b = bases(i, j + 1)
            lefts = [left_a.astype(bf16), left_b.astype(bf16)]
            both = jnp.concatenate([right_a, right_b], axis=0)
            right = jnp.where(square, jnp.concatenate([both, both], axis=1), 0.0).astype(bf16)
            choose = lambda parts: jnp.where(side, parts[0], parts[1])
            inner = choose([turned(rows, cols, left) for left in lefts]).astype(bf16)
            grad = nn(inner, right)
            new_first, new_second, normal = moments_step(m[rows, cols], v[rows, cols], grad)
            nm[rows, cols] = new_first
            nv[rows, cols] = new_second
            low = normal.astype(bf16)
            outer = choose([nn(left, low) for left in lefts]).astype(bf16)
            master = w[rows, cols]
            nw[rows, cols] = master - learn_rate * (nt(outer, right) + decay_rate * master)


def soap_kernel(turned, swapped, w, m, v, g, q, nm, nv, nw):
    def plain(rows, cols, left):
        return tn(left, g[0, rows, cols])

    def across(rows, cols, left):
        return lax.dot_general(
            left, g[0, cols, rows], (((0,), (1,)), ((), ())), preferred_element_type=f32
        )

    if swapped:
        bases = lambda i, j: (q[0, j, i, 1], q[0, j, i, 0])
    else:
        bases = lambda i, j: (q[0, i, j, 0], q[0, i, j, 1])
    soap_tiles(
        across if turned else plain, w.shape[1] // TILE, w.shape[2] // TILE,
        w.at[0], m.at[0], v.at[0], bases, nm.at[0], nv.at[0], nw.at[0],
    )


def soap(w, m, v, g, q, rows, turned=False, swapped=False):
    group, height, width = w.shape
    if width < 2 * TILE:
        q = jnp.concatenate([q, q], axis=1 if swapped else 2)
        padded = [jnp.concatenate([array, array], axis=2) for array in (w, m, v)]
        g = jnp.concatenate([g, g], axis=1 if turned else 2)
        results = soap(*padded, g, q, rows, turned, swapped)
        return [array[:, :, :width] for array in results]
    row = pl.BlockSpec((1, rows, width), lambda n, i: (n, i, 0))
    out = jax.ShapeDtypeStruct(w.shape, f32)
    if swapped:
        q_block = (1, width // TILE, rows // TILE, 2, TILE, TILE)
        q_at = lambda n, i: (n, 0, i, 0, 0, 0)
    else:
        q_block = (1, rows // TILE, width // TILE, 2, TILE, TILE)
        q_at = lambda n, i: (n, i, 0, 0, 0, 0)
    return pl.pallas_call(
        functools.partial(soap_kernel, turned, swapped),
        grid=(group, height // rows),
        in_specs=[row] * 3
        + [
            pl.BlockSpec((1, width, rows), lambda n, i: (n, 0, i)) if turned else row,
            pl.BlockSpec(q_block, q_at),
        ],
        out_specs=[row] * 3,
        out_shape=[out] * 3,
        compiler_params=pltpu.CompilerParams(
            dimension_semantics=("arbitrary", "arbitrary"), vmem_limit_bytes=56 * 1024 * 1024
        ),
        cost_estimate=cost(group * height * width / 24000),
        name="soap",
    )(w, m, v, g, q)


def reorder(array, dim, order):
    shape = array.shape
    parts = order.shape[0]
    reshaped = array.reshape(shape[:dim] + (parts, shape[dim] // parts) + shape[dim + 1 :])
    return jnp.take(reshaped, order, axis=dim, mode="clip").reshape(shape)


def gather_slabs(array):
    return lax.all_gather(array, "mlp", axis=0, tiled=True)


def scatter_slabs(array):
    return lax.psum_scatter(array, "mlp", scatter_dimension=0, tiled=True)


def hop(array, pairs):
    count = lax.axis_size("tok")
    return lax.ppermute(array, "tok", [(i, i ^ pairs[i % 2]) for i in range(count)])


CORE, NEAR, FAR = (1, 1), (2, 4), (4, 2)


def stored_order(parts, rank):
    indices = jnp.arange(parts, dtype=jnp.int32)
    if parts != 8:
        return indices, indices
    near, far = indices // 2 % 2, indices % 2
    spots = rank ^ (
        indices // 4 + jnp.where(rank % 2 == 0, near * 2 + far * 4, near * 4 + far * 2)
    )
    return spots, invert(spots)


def invert(order):
    indices = jnp.arange(order.shape[0], dtype=jnp.int32)
    return jnp.sum(jnp.where(order[None, :] == indices[:, None], indices[None, :], 0), axis=1)


def gather_start(own):
    two = jnp.concatenate([own, hop(own, FAR)], axis=0)
    return jnp.concatenate([two, hop(two, NEAR)], axis=0)


class Sums:
    def __init__(self, keep, send, dim):
        self.keep, self.send, self.dim = keep, send, dim
        self.whole = lax.axis_size("tok") != 8

    def cut(self, array, blocks, at):
        size = array.shape[self.dim] // blocks
        return lax.slice_in_dim(array, at * size, (at + 1) * size, axis=self.dim).astype(f32)

    def mixed(self, at, there):
        return self.cut(self.keep, 4, at) + self.cut(self.got, 4, there)

    def first(self, *before):
        if self.whole:
            return self.send
        self.got = hop(self.send, CORE)
        self.near_send = after(
            jnp.concatenate([self.mixed(2, 1), self.mixed(3, 3)], axis=self.dim).astype(
                self.send.dtype
            ),
            *before,
        )
        return self.near_send

    def second(self, *before):
        if self.whole:
            return self.send
        self.near = hop(self.near_send, NEAR)
        self.far_send = after(
            (self.mixed(1, 2) + self.cut(self.near, 2, 1)).astype(self.send.dtype), *before
        )
        return self.far_send

    def third(self):
        if self.whole:
            both = jnp.concatenate([self.keep.astype(self.send.dtype), self.send], axis=self.dim)
            return lax.psum_scatter(both, "tok", scatter_dimension=self.dim, tiled=True)
        far = hop(self.far_send, FAR)
        return self.mixed(0, 0) + self.cut(self.near, 2, 0) + far.astype(f32)


def sums_of(array):
    half = array.shape[0] // 2
    sums = Sums(array[:half], array[half:], 0)
    sums.first()
    sums.second()
    return sums.third()


def halves(array):
    half = array.shape[1] // 2
    return array[:, :half], array[:, half:]


def grad_rows(left, right):
    keep, send = halves(left)
    return Sums(tn(keep, right), tn(send, right).astype(bf16), 0)


def grad_columns(left, right):
    keep, send = halves(right)
    return Sums(tn(left, keep), tn(left, send).astype(bf16), 1)


def permute_kernel(order, array, out):
    parts = order.shape[0]
    size = array.shape[1] // parts
    for part in range(parts):
        at = pl.multiple_of(order[part] * size, LANES)
        out[:, part * size : (part + 1) * size] = array[:, pl.ds(at, size)]


def permute_columns(array, order):
    parts = order.shape[0]
    count, width = array.shape
    if width // parts % LANES:
        return reorder(array, 1, order)
    rows = min(256, count)
    row = pl.BlockSpec((rows, width), lambda i: (i, 0))
    return pl.pallas_call(
        permute_kernel,
        grid=(count // rows,),
        in_specs=[pl.BlockSpec(memory_space=pltpu.SMEM), row],
        out_specs=row,
        out_shape=jax.ShapeDtypeStruct(array.shape, array.dtype),
        compiler_params=params(),
        cost_estimate=cost(count * width / 420000),
        name="permute_columns",
    )(order, array)


def settle_kernel(move, order, value, upstream, gain, base, total_o, low_o, sum_o, hold):
    @pl.when(pl.program_id(0) == 0)
    def _():
        sum_o[...] = jnp.zeros_like(sum_o)

    held = value[...].astype(f32)
    grad = upstream[...].astype(f32)
    scale = lax.rsqrt(jnp.mean(held * held, axis=-1, keepdims=True) + norm_eps)
    weighted = grad * gain[...]
    inner = jnp.mean(held * weighted, axis=-1, keepdims=True)
    total = base[...].astype(f32) + (scale * weighted - held * (scale * scale * scale * inner))
    sum_o[0:1, :] += jnp.sum(grad * held * scale, axis=0, keepdims=True)
    total_o[...] = total
    low = total.astype(bf16)
    if not move:
        low_o[...] = low
        return
    hold[...] = low
    parts = order.shape[0]
    size = low.shape[1] // parts
    for part in range(parts):
        at = pl.multiple_of(order[part] * size, LANES)
        low_o[:, part * size : (part + 1) * size] = hold[:, pl.ds(at, size)]


def settle(value, upstream, gain, base, order, move):
    count, model = value.shape
    inside = move and (model // order.shape[0]) % LANES == 0
    rows = min(128, count)
    row = pl.BlockSpec((rows, model), lambda i: (i, 0))
    total, low, sums = pl.pallas_call(
        functools.partial(settle_kernel, inside),
        grid=(count // rows,),
        in_specs=[pl.BlockSpec(memory_space=pltpu.SMEM), row, row, whole(gain.shape), row],
        out_specs=[row, row, whole((8, model))],
        out_shape=[
            jax.ShapeDtypeStruct((count, model), f32),
            jax.ShapeDtypeStruct((count, model), bf16),
            jax.ShapeDtypeStruct((8, model), f32),
        ],
        scratch_shapes=[pltpu.VMEM((rows, model), bf16)],
        compiler_params=params(),
        cost_estimate=cost(4),
        name="settle",
    )(order, value, upstream, gain, base)
    if move and not inside:
        low = reorder(low, 1, order)
    return total, low, sums[0]


def after(array, *others):
    return lax.optimization_barrier((array,) + others)[0]


def block_diagonal(blocks):
    count, width, _ = blocks.shape
    return jnp.concatenate(
        [
            jnp.pad(blocks[n], ((0, 0), (n * width, (count - 1 - n) * width)))
            for n in range(count)
        ],
        axis=0,
    )


def diagonal_blocks(array, count):
    width = array.shape[0] // count
    return jnp.stack(
        [array[n * width : (n + 1) * width, n * width : (n + 1) * width] for n in range(count)]
    )


def on_device(
    tokens, segment_ids, owner_table, cotangent,
    w_in_rec, m_in_rec, v_in_rec, q_in_rec,
    w_out_rec, m_out_rec, v_out_rec, q_out_rec,
    w_in_mlp, m_in_mlp, v_in_mlp, q_in_mlp,
    w_out_mlp, m_out_mlp, v_out_mlp, q_out_mlp,
    w_gates, m_gates, v_gates, w_rnn, m_rnn, v_rnn, w_gains, m_gains, v_gains,
):
    parts = lax.axis_size("tok")
    rank = lax.axis_index("tok")
    slabs = lax.axis_size("mlp")
    slab = lax.axis_index("mlp")
    count, model = tokens.shape
    length = count * parts
    share = count // slabs
    rows = min(256, count)
    spots, places = stored_order(parts, rank)
    into_local = jnp.take(invert(owner_table), spots, mode="clip")
    from_local = jnp.take(places, owner_table, mode="clip")
    rank_ref = rank.reshape(1).astype(jnp.int32)

    blocks = w_gates.shape[1]
    gate_part = w_gates.shape[2]
    lead = 2 * blocks
    rnn_part = w_rnn.shape[1]
    small = jnp.concatenate(
        [w_gates.reshape(lead, gate_part), w_rnn, w_gains.reshape(lead, -1)], axis=1
    ).astype(bf16)
    if parts == 8:
        small_four = gather_start(small[None])
        small_rest = hop(small_four, CORE)
        small_all = jnp.concatenate(
            [small_four] + [small_rest[p : p + 1] for p in (0, 2, 1, 3)], axis=0
        )
    else:
        small_all = lax.all_gather(small, "tok", axis=0, tiled=False)
    turn = lambda array: jnp.swapaxes(array, 1, 2)
    rec_own = turn(w_in_rec).astype(bf16)[None]
    join = lambda *arrays: jnp.concatenate(arrays, axis=0)
    out_own = lax.all_gather(w_out_rec.astype(bf16), "mlp", axis=0, tiled=False)[None]
    if parts == 8:
        rec_two = join(rec_own, hop(rec_own, FAR))
        rec_near = hop(rec_two, NEAR)
        rec_core = hop(rec_two, CORE)
    gains_all = small_all[:, :, gate_part + rnn_part :].reshape(parts, 2, model // parts)
    gains_f = (
        gains_all
        .transpose(1, 0, 2)
        .reshape(2, model)
        .astype(f32)
    )
    ordered = jnp.take(small_all[:, :, : gate_part + rnn_part], from_local, axis=0, mode="clip")
    gate_mats = ordered[:, :, :gate_part].transpose(1, 0, 2).reshape(2, blocks, BW, BW)
    w_a = block_diagonal(gate_mats[0])
    w_i = block_diagonal(gate_mats[1])
    rnn_f = ordered[:, :, gate_part:].transpose(1, 0, 2).reshape(lead, -1).astype(f32)
    lam = rnn_f[CONV + 1]
    vec = rnn_f.at[CONV + 1].set(-8.0 * jax.nn.softplus(lam))

    tok_s = permute_columns(tokens, into_local)
    cot_s = permute_columns(cotangent, into_local)
    forward_pairs = [(i, i + 1) for i in range(parts - 1)]
    rim = lax.ppermute(tokens[count - HALO :], "tok", forward_pairs)
    halo = permute_columns(rim, into_local)
    rim_ids = lax.ppermute(segment_ids[count - HALO :], "tok", forward_pairs)
    ids = jnp.concatenate(
        [
            jnp.where(rank == 0, -1, rim_ids).astype(f32),
            segment_ids.astype(f32),
            jnp.full((HALO,), -1.0, f32),
        ]
    )
    mask = masks(ids[:, None], count)
    if parts == 8:
        rec_near = after(rec_near, tok_s, halo, mask, w_a, w_i, vec)
        rec_w = (rec_two, rec_near, rec_core, hop(rec_near, CORE))
        up_own = w_in_mlp.astype(bf16)[None]
        out_far = hop(after(out_own, rec_near), FAR)
        up_far = hop(after(up_own, rec_near), FAR)
    else:
        rec_w = (lax.all_gather(rec_own[0], "tok", axis=2, tiled=True)[None],) * 4
        out_w = (lax.all_gather(out_own[0], "tok", axis=2, tiled=True)[None],) * 4

    xn_one, y_pre, u_low, u_halo, conv_low, pre_decay, pre_input, decay, h_loc, p_loc, ends = front(
        tok_s, halo, gains_f[0:1], rec_w, w_a, w_i, vec, mask, rows
    )
    ends_all = lax.all_gather(ends[0:2], "tok", axis=0, tiled=False)
    state, state_prev, mixed = finish_state(rank_ref, ends_all, h_loc, p_loc, y_pre, rows)
    own = lambda array: lax.dynamic_slice_in_dim(array, slab * share, share, 0)
    slab_ref = slab.reshape(1).astype(jnp.int32)
    own_tok = own(tok_s)
    mixed_all = lax.all_gather(mixed, "mlp", axis=0, tiled=False)
    down_own = w_out_mlp.astype(bf16)[None]
    if parts == 8:
        out_two = join(out_own, after(out_far, ends))
        up_two = join(up_own, after(up_far, ends))
        out_near = hop(out_two, NEAR)
        up_near = hop(up_two, NEAR)
        down_far = hop(after(down_own, ends), FAR)
        out_core = hop(after(out_two, mixed), CORE)
        out_w = (out_two, out_near, out_core, hop(after(out_near, mixed), CORE))
        down_two = join(down_own, after(down_far, mixed))
        down_near = hop(down_two, NEAR)
        down_core = hop(down_two, CORE)
        up_core = hop(after(up_two, mixed), CORE)
        up_w = (up_two, up_near, up_core, hop(after(up_near, mixed), CORE))
        down_last = hop(down_near, CORE)
        down = jnp.concatenate(
            [
                down_two[0], down_two[1], down_near[0], down_near[1],
                down_core[0], down_last[0], down_core[1], down_last[1],
            ],
            axis=1,
        )
    else:
        down = lax.all_gather(down_own[0], "tok", axis=1, tiled=True)
        up_own = w_in_mlp.astype(bf16)
        up_w = (lax.all_gather(up_own, "tok", axis=1, tiled=True)[None],) * 4
    cot_s = permute_columns(after(cotangent, mixed), into_local)
    d_hidden = nt(cot_s, down)
    xn_two, hidden, d_gate, d_up, d_branch, second = middle(
        slab_ref, mixed_all, tok_s, gains_f[1:2], d_hidden, out_w, up_w
    )
    d_xn_two = scatter_slabs(d_branch)
    low = lambda array: array.astype(bf16)
    sum_gate = grad_rows(xn_two, d_gate)
    sum_up = grad_rows(xn_two, d_up)
    sum_down = grad_rows(cot_s, hidden)
    branch_two = nn(hidden, down).astype(bf16)
    d_xn_two = after(
        d_xn_two, sum_gate.first(), sum_up.first(), sum_down.first()
    )
    sum_gate.second()
    sum_up.second()
    sum_down.second()
    g_in_mlp = jnp.stack([low(sum_gate.third()), low(sum_up.third())])
    g_out_mlp = low(sum_down.third())

    lead_one = lambda *arrays: [array[None] for array in arrays]
    split = lambda height: max(
        n for n in range(2 * TILE, height + 1, 2 * TILE) if height % n == 0 and n <= 512
    )
    in_mlp_new = soap(w_in_mlp, m_in_mlp, v_in_mlp, g_in_mlp, q_in_mlp, TILE)

    d_second, d_second_low, g_gain_two = settle(
        second, d_xn_two, gains_f[1:2], own(cot_s), from_local, False
    )
    d_rec = gather_slabs(d_second_low)
    branch_two = after(branch_two, in_mlp_new[0])
    d_rec = after(d_rec, in_mlp_new[0])
    branch_sum = scatter_slabs(branch_two)
    result_own = second + branch_sum.astype(f32)
    result_low = permute_columns(result_own.astype(bf16), from_local)
    d_ypre, g_loc, q_loc, ends_back = back_scan(slab_ref, d_rec, out_w, y_pre, state, decay, rows)
    ends_back_all = lax.all_gather(ends_back[0:2], "tok", axis=0, tiled=False)
    d_pa, d_pi, d_u, d_u_tail, spill, sums = gates_back(
        rank_ref, ends_back_all, g_loc, q_loc, pre_decay, pre_input, conv_low, state_prev,
        u_low, u_halo, mask, w_a, w_i, vec, rows,
    )
    from_next = lax.ppermute(spill, "tok", [(i + 1, i) for i in range(parts - 1)])
    d_pair, d_u = pair_back(d_ypre, d_u, d_u_tail, from_next, rec_w, model, rows)
    d_xn_one = scatter_slabs(after(d_pair, branch_sum))
    out_mlp_new = soap(
        *lead_one(w_out_mlp, m_out_mlp, v_out_mlp, after(g_out_mlp, d_pair), q_out_mlp),
        split(w_out_mlp.shape[0]), turned=True,
    )
    d_rec, mixed, xn_one, d_ypre, d_u, d_pa, d_pi, conv_low = lax.optimization_barrier(
        (d_rec, mixed, xn_one, d_ypre, d_u, d_pa, d_pi, conv_low, d_pair)
    )[:8]
    sum_out = grad_columns(mixed, d_rec)
    sum_y = grad_columns(d_ypre, xn_one)
    sum_u = grad_columns(d_u, xn_one)
    d_xn_one = after(
        d_xn_one, sum_out.first(), sum_y.first(), sum_u.first(), out_mlp_new[0]
    )
    _, d_input_low, g_gain_one = settle(
        own_tok, d_xn_one, gains_f[0:1], d_second, from_local, True
    )
    d_input = gather_slabs(d_input_low)
    sum_out.second()
    sum_y.second()
    sum_u.second()
    g_out_rec = low(sum_out.third())
    g_in_rec = jnp.stack([low(sum_y.third()), low(sum_u.third())])
    result = gather_slabs(after(result_low, d_input_low))

    g_gates = jnp.stack(
        [
            diagonal_blocks(tn(conv_low, d_pa), blocks),
            diagonal_blocks(tn(conv_low, d_pi), blocks),
        ]
    )
    g_rnn = sums.at[CONV + 1].multiply(-8.0 * jax.nn.sigmoid(lam))
    g_small = jnp.concatenate(
        [g_gates.reshape(lead, parts, gate_part), g_rnn.reshape(lead, parts, rnn_part)], axis=2
    ).transpose(1, 0, 2)
    g_small = jnp.take(g_small, into_local, axis=0, mode="clip")
    sum_small = sums_of(g_small)[0]
    sum_gates = sum_small[:, :gate_part].reshape(w_gates.shape)
    sum_rnn = sum_small[:, gate_part:]
    g_gains = jnp.stack([g_gain_one, g_gain_two]).reshape(2, parts, -1).transpose(1, 0, 2)
    sum_gains = lax.psum(sums_of(g_gains)[0], "mlp")

    out_rec_new = soap(
        *lead_one(w_out_rec, m_out_rec, v_out_rec, g_out_rec, q_out_rec), w_out_rec.shape[0]
    )
    in_rec_new = soap(
        turn(w_in_rec), turn(m_in_rec), turn(v_in_rec), g_in_rec, q_in_rec, w_in_rec.shape[2],
        swapped=True,
    )
    out_mlp_new = [array[0] for array in out_mlp_new]
    out_rec_new = [array[0] for array in out_rec_new]
    in_rec_new = [turn(array) for array in in_rec_new]
    gates_m, gates_v, gates_n = moments_step(m_gates, v_gates, sum_gates)
    gates_w = w_gates - learn_rate * (gates_n + decay_rate * w_gates)
    rnn_m, rnn_v, _ = moments_step(m_rnn, v_rnn, sum_rnn)
    gains_m, gains_v, _ = moments_step(m_gains, v_gains, sum_gains)
    d_input = after(
        d_input, in_rec_new[0], out_rec_new[0], gates_w, rnn_m
    ).astype(f32)
    return (
        result, d_input,
        in_rec_new[0], in_rec_new[1], in_rec_new[2],
        out_rec_new[0], out_rec_new[1], out_rec_new[2],
        in_mlp_new[0], in_mlp_new[1], in_mlp_new[2],
        out_mlp_new[0], out_mlp_new[1], out_mlp_new[2],
        gates_m, gates_v, gates_w, rnn_m, rnn_v, gains_m, gains_v,
    )


def solution(mesh):
    in_specs = (
        P("tok", None),
        P("tok"),
        P(),
        P("tok", None),
        P(None, "tok", "mlp"),
        P(None, "tok", "mlp"),
        P(None, "tok", "mlp"),
        P(None, "tok", "mlp", None, None, None),
        P("mlp", "tok"),
        P("mlp", "tok"),
        P("mlp", "tok"),
        P("mlp", "tok", None, None, None),
        P(None, "tok", "mlp"),
        P(None, "tok", "mlp"),
        P(None, "tok", "mlp"),
        P(None, "tok", "mlp", None, None, None),
        P("mlp", "tok"),
        P("mlp", "tok"),
        P("mlp", "tok"),
        P("mlp", "tok", None, None, None),
        P(None, "mlp", "tok"),
        P(None, "mlp", "tok"),
        P(None, "mlp", "tok"),
        P(None, ("mlp", "tok")),
        P(None, ("mlp", "tok")),
        P(None, ("mlp", "tok")),
        P(None, "tok"),
        P(None, "tok"),
        P(None, "tok"),
    )
    out_specs = (
        P("tok", None),
        P("tok", None),
        P(None, "tok", "mlp"),
        P(None, "tok", "mlp"),
        P(None, "tok", "mlp"),
        P("mlp", "tok"),
        P("mlp", "tok"),
        P("mlp", "tok"),
        P(None, "tok", "mlp"),
        P(None, "tok", "mlp"),
        P(None, "tok", "mlp"),
        P("mlp", "tok"),
        P("mlp", "tok"),
        P("mlp", "tok"),
        P(None, "mlp", "tok"),
        P(None, "mlp", "tok"),
        P(None, "mlp", "tok"),
        P(None, ("mlp", "tok")),
        P(None, ("mlp", "tok")),
        P(None, "tok"),
        P(None, "tok"),
    )
    return jax.shard_map(
        on_device, mesh=mesh, in_specs=in_specs, out_specs=out_specs, check_vma=False
    )
```
